128 devices in a mesh: gz: 4 (over z_hi, core), xy: 32 (over y, z_lo, x).
Axes of the slice: x: 4, y: 4, z: 4 (z_hi: 2, z_lo: 2; z = z_hi * 2 + z_lo), core: 2. Of those that a mesh axis runs over, the one named last changes fastest.
Arguments:
- raw_volume: float32 [12, 32, 256, 256], P(None, 'gz', 'xy'), may hold values from -256 to 256
- face_slot: int32 [32, 256, 256], P('gz', 'xy'), may hold values from -1024 to 1023
- touched: int32 [4, 32, 16], P('gz', 'xy'), may hold values from 0 to 31, as said below
- block_owner: int32 [4, 32], P('gz'), may hold values from 0 to 31, as said below
Outputs:
- edge_features: float32 [4, 32, 144, 64], P('gz', 'xy')
The draws below stay inside these ranges and needn't reach their ends.
Inputs may be any that keep to these rules, and one draw needn't show every extreme that they name: `face_slot`: a negative value marks a voxel on no contact face. `touched`: the 16 blocks of one device have 16 different owners; in each slab one owner is named by every device of the slab. `block_owner`: each tile owns exactly 1 block of its slab.
All inputs are finite; a program needn't handle non-finite values.
Results may differ from the reference program's by a relative error of at most 0.0003.
Values sent between devices are 32-bit elements; how exact they have to be, the bound alone decides.
A program may use at most 192 MiB of HBM per device.

```python
import jax
import jax.numpy as jnp
from jax import lax

C = 12
CZ = 8
CY = 8
CX = 256
RADIUS = 8
EB = 64
BLK_DEV = 1
TOUCH = 16
NBS = 32
NZ = 32
NY = 256
N_GZ = 4
N_XY = 32


def slab_layout(key):
    slab_keys = jax.random.split(key, N_GZ)

    def one_slab(slab_key):
        owner_key, hottest_key, source_key = jax.random.split(slab_key, 3)
        owners = jax.random.permutation(owner_key, jnp.tile(jnp.arange(N_XY, dtype=jnp.int32), BLK_DEV))
        listing = jnp.argsort(owners, stable=True).astype(jnp.int32).reshape(N_XY, BLK_DEV)
        hottest = jax.random.randint(hottest_key, (), 0, N_XY).astype(jnp.int32)

        def one_source(tile_key):
            order_key, shuffle_key, choose_key = jax.random.split(tile_key, 3)
            others = (hottest + 1 + jax.random.permutation(order_key, N_XY - 1).astype(jnp.int32)) % N_XY
            chosen = jnp.concatenate([hottest[None], others[:TOUCH - 1]]).astype(jnp.int32)
            chosen = jax.random.permutation(shuffle_key, chosen)
            picked_slot = jax.random.randint(choose_key, (TOUCH,), 0, BLK_DEV).astype(jnp.int32)
            return listing[chosen, picked_slot]
        touched_rows = jax.vmap(one_source)(jax.random.split(source_key, N_XY))
        return (owners, touched_rows)
    return jax.vmap(one_slab)(slab_keys)


def draw_touched(key, part):
    owners, touched_rows = slab_layout(key)
    return touched_rows.astype(jnp.int32)


def draw_block_owner(key, part):
    owners, touched_rows = slab_layout(key)
    return owners.astype(jnp.int32)


def with_ends(values, rng, least, top_value):
    longest = values.shape.index(max(values.shape))
    spots = []
    for shift in (0, 1):
        where = [jax.random.randint(jax.random.fold_in(rng, axis), (), 0, length) for axis, length in enumerate(values.shape)]
        where[longest] = (where[longest] + shift) % values.shape[longest]
        spots.append(tuple(where))
    return values.at[spots[0]].set(least).at[spots[1]].set(top_value)


def levels(rng, dims, cuts, low, high):
    def one(position, blocks):
        steps = jax.random.uniform(jax.random.fold_in(jax.random.fold_in(rng, 6), position), (blocks,), jnp.float32, low / len(cuts), high / len(cuts))
        return jnp.repeat(jnp.exp(steps), dims[position] // blocks).reshape((-1,) + (1,) * (len(dims) - position - 1))

    loudness = one(*cuts[0])
    for cut in cuts[1:]:
        loudness = loudness * one(*cut)
    return loudness


def noise(own_key, extent, scale, limit, shards=(), held_as=jnp.bfloat16):
    values = scale * jax.random.normal(own_key, extent, jnp.float32)
    if shards:
        values = values * levels(own_key, extent, shards, -0.22, 0.18)
    return jnp.clip(values, -limit, limit).astype(held_as)


def setup_inputs(seed: int = 0) -> dict:
    splits = jax.random.split(jax.random.key(seed), 5)
    return {
        "raw_volume": noise(splits[0], (C, NZ, NY, CX), 32.0, 256.0, ((1, 4), (2, 32)), jnp.float32),
        "face_slot": with_ends(jax.random.randint(splits[1], (NZ, NY, CX), -TOUCH * EB, TOUCH * EB), jax.random.fold_in(splits[1], 1), -TOUCH * EB, (TOUCH * EB) - 1).astype(jnp.int32),
        "touched": draw_touched(jax.random.fold_in(splits[4], 71), 0),
        "block_owner": draw_block_owner(jax.random.fold_in(splits[4], 71), 0),
    }


far_value = 1e+30

def kernel_taps(radius):
    sigma = radius / 3.0
    offsets = jnp.arange(2 * radius + 1).astype(jnp.float32) - radius
    gauss = jnp.exp(-offsets * offsets / (2.0 * sigma * sigma))
    gauss = gauss / jnp.sum(gauss)
    slope = -(offsets / sigma) * gauss
    curve = (offsets * offsets / (sigma * sigma) - 1.0) * gauss
    return (gauss, slope, curve)

def filter_along(field, kernel, axis, length, radius):
    total = kernel[0] * lax.slice_in_dim(field, 0, length, axis=axis)
    for offset in range(1, 2 * radius + 1):
        total = total + kernel[offset] * lax.slice_in_dim(field, offset, offset + length, axis=axis)
    return total

def line_matrix(kernel, breadth, radius):
    row_index = jnp.arange(breadth)[:, None]
    col_index = jnp.arange(breadth)[None, :]
    distance = row_index - col_index
    picked = kernel[jnp.clip(distance + radius, 0, 2 * radius)]
    return jnp.where(jnp.abs(distance) <= radius, picked, 0.0)

def voxel_features(z_smooth, z_slope, height, breadth, radius):
    gauss, slope, curve = kernel_taps(radius)
    plain = filter_along(z_smooth, gauss, 2, height, radius)
    sloped = filter_along(z_smooth, slope, 2, height, radius)
    curved = filter_along(z_smooth, curve, 2, height, radius)
    lifted = filter_along(z_slope, gauss, 2, height, radius)
    tables = jnp.concatenate([line_matrix(gauss, breadth, radius), line_matrix(slope, breadth, radius), line_matrix(curve, breadth, radius)], axis=1)

    def apply_x(field, columns):
        flat = field.reshape(-1, breadth)
        result = jnp.dot(flat, tables[:, :columns * breadth], precision=lax.Precision.HIGHEST)
        return result.reshape(flat.shape[0], columns, breadth)
    triple = apply_x(plain, 3)
    double = apply_x(sloped, 2)
    hess_yy = apply_x(curved, 1)[:, 0]
    grad_z = apply_x(lifted, 1)[:, 0]
    smooth, grad_x, hess_xx = (triple[:, 0], triple[:, 1], triple[:, 2])
    grad_y, hess_xy = (double[:, 0], double[:, 1])
    magnitude = jnp.sqrt(grad_z * grad_z + grad_y * grad_y + grad_x * grad_x)
    half_trace = (hess_yy + hess_xx) * 0.5
    spread = (hess_yy - hess_xx) * 0.5
    deviation = jnp.sqrt(spread * spread + hess_xy * hess_xy)
    stacked = jnp.stack([smooth, magnitude, half_trace + deviation, half_trace - deviation])
    channels = z_smooth.shape[0]
    return stacked.reshape(4 * channels, -1)

def pool_faces(feature_rows, targets, slot_count):
    feature_count = feature_rows.shape[0]
    sums = jnp.zeros((feature_count, slot_count), jnp.float32).at[:, targets].add(feature_rows, mode='drop')
    maxima = jnp.full((feature_count, slot_count), -far_value, jnp.float32).at[:, targets].max(feature_rows, mode='drop')
    minima = jnp.full((feature_count, slot_count), far_value, jnp.float32).at[:, targets].min(feature_rows, mode='drop')
    counts = jnp.zeros((slot_count,), jnp.float32).at[targets].add(jnp.ones(targets.shape, jnp.float32), mode='drop')
    return (sums, maxima, minima, counts)

def finalize(sums, maxima, minima, counts):
    present = counts[..., None, :] > 0.0
    average = sums / jnp.maximum(counts, 1.0)[..., None, :]
    largest = jnp.where(present, maxima, 0.0)
    smallest = jnp.where(present, minima, 0.0)
    stacked = jnp.concatenate([average, largest, smallest], axis=-2)
    stacked = jnp.swapaxes(stacked, -3, -2)
    return stacked.reshape(stacked.shape[:-2] + (stacked.shape[-2] * stacked.shape[-1],))

def reference(raw_volume, face_slot, touched, block_owner):
    radius = RADIUS
    gauss, slope, curve = kernel_taps(radius)
    padded = jnp.pad(raw_volume, ((0, 0), (radius, radius), (radius, radius), (0, 0)))
    feature_count = 4 * C
    total_slots = N_GZ * NBS * EB
    zero = jnp.zeros((), jnp.int32)
    initial = (jnp.zeros((feature_count, total_slots), jnp.float32), jnp.full((feature_count, total_slots), -far_value, jnp.float32), jnp.full((feature_count, total_slots), far_value, jnp.float32), jnp.zeros((total_slots,), jnp.float32))

    def accumulate(index_flat, carry):
        index_flat = jnp.asarray(index_flat).astype(jnp.int32)
        slab_index = (index_flat // N_XY).astype(jnp.int32)
        tile_index = (index_flat % N_XY).astype(jnp.int32)
        window = lax.dynamic_slice(padded, (zero, slab_index * CZ, tile_index * CY, zero), (C, CZ + 2 * radius, CY + 2 * radius, CX))
        z_smooth = filter_along(window, gauss, 1, CZ, radius)
        z_slope = filter_along(window, slope, 1, CZ, radius)
        feature_rows = voxel_features(z_smooth, z_slope, CY, CX, radius)
        face_slots = lax.dynamic_slice(face_slot, (slab_index * CZ, tile_index * CY, zero), (CZ, CY, CX)).reshape(-1)
        my_blocks = lax.dynamic_slice(touched, (slab_index, tile_index, zero), (1, 1, TOUCH)).reshape(TOUCH)
        clamped = jnp.clip(face_slots, 0, TOUCH * EB - 1)
        global_slot = slab_index * (NBS * EB) + my_blocks[clamped // EB] * EB + clamped % EB
        global_slot = jnp.where(face_slots < 0, total_slots, global_slot).astype(jnp.int32)
        sums, maxima, minima, counts = pool_faces(feature_rows, global_slot, total_slots)
        return (carry[0] + sums, jnp.maximum(carry[1], maxima), jnp.minimum(carry[2], minima), carry[3] + counts)
    sums, maxima, minima, counts = lax.fori_loop(0, N_GZ * N_XY, accumulate, initial)
    order = jnp.argsort(block_owner, axis=1, stable=True).astype(jnp.int32)
    slab_rows = jnp.arange(N_GZ).astype(jnp.int32)[:, None]

    def arrange(values):
        blocked = values.reshape(feature_count, N_GZ, NBS, EB).transpose(1, 2, 0, 3)
        return blocked[slab_rows, order].reshape(N_GZ, N_XY, BLK_DEV, feature_count, EB)
    counted = counts.reshape(N_GZ, NBS, EB)[slab_rows, order].reshape(N_GZ, N_XY, BLK_DEV, EB)
    return finalize(arrange(sums), arrange(maxima), arrange(minima), counted)
```

```python
import functools

import jax
import jax.numpy as jnp
import ml_dtypes
import numpy as np
from jax import lax
from jax.experimental import pallas as pl
from jax.experimental.pallas import tpu as pltpu
from jax.sharding import PartitionSpec as P

RADIUS = 8
C = 12
Z = 8
Y = 8
X = 256
EB = 64
TOUCH = 16
BLOCKS = 32
TILES = 32
SLABS = 4
ZY = Z * Y
HALF = X // 2
FEATURES = 4 * C
PARTS = 4
PART = C // PARTS
ACCS = 8
ROWS = 2 * (TOUCH * EB) + 16
SENT = EB + EB // 4
FAR = -1e30
MESH = pl.DeviceIdType.MESH


def taps():
    sigma = np.float32(RADIUS / 3.0)
    offsets = np.arange(-RADIUS, RADIUS + 1).astype(np.float32)
    gauss = np.exp(-offsets * offsets / (2.0 * sigma * sigma)).astype(np.float32)
    gauss = gauss / gauss.sum()
    slope = -(offsets / sigma) * gauss
    curve = (offsets * offsets / (sigma * sigma) - 1.0) * gauss
    return [tap.astype(np.float64) for tap in (gauss, slope, curve)]


def two_terms(table):
    table = table.astype(np.float32)
    high = table.astype(ml_dtypes.bfloat16)
    low = (table - high.astype(np.float32)).astype(ml_dtypes.bfloat16)
    return high, low


def band(tap, size, start, stop):
    offset = np.arange(start, stop)[None, :] - np.arange(size)[:, None]
    return np.where(np.abs(offset) <= RADIUS, tap[np.clip(offset + RADIUS, 0, 2 * RADIUS)], 0.0)


def tables():
    gauss, slope, curve = taps()
    rows = []
    for kz, ky in ((gauss, gauss), (gauss, slope), (gauss, curve), (slope, gauss)):
        bz = band(kz, Z, -Z, 2 * Z).reshape(Z, 3, Z)
        by = band(ky, Y, -Y, 2 * Y).reshape(Y, 3, Y)
        rows.append(np.einsum("pdz,qey->pqdezy", bz, by).reshape(ZY, 9 * ZY))
    high, low = two_terms(np.concatenate(rows, axis=0))
    across = np.concatenate([high, low], axis=0)
    along = [two_terms(band(tap, X, 0, X).T) for tap in (gauss, slope, curve)]
    return across, np.concatenate([t[0] for t in along], 1), np.concatenate([t[1] for t in along], 1)


def split(values):
    high = values.astype(jnp.bfloat16)
    return high, (values - high.astype(jnp.float32)).astype(jnp.bfloat16)


def slot(dz, dt):
    return (dz + 1) * 3 + (dt + 1)


def filter_kernel(raw, across, along_hi, along_lo, out, win, send, recv):
    g, t = lax.axis_index("gz"), lax.axis_index("xy")
    mate = g + 1 - 2 * lax.rem(g, 2)
    inner = (g == 1) | (g == 2)
    other = 3 - g
    has_left, has_right = t > 0, t < TILES - 1

    barrier = pltpu.get_barrier_semaphore()

    def greet(dg, dt):
        pl.semaphore_signal(barrier, inc=1, device_id=(dg, dt), device_id_type=MESH)

    pl.when(has_left)(lambda: greet(g, t - 1))
    pl.when(has_right)(lambda: greet(g, t + 1))
    greet(mate, t)
    pl.when(inner)(lambda: greet(other, t))
    greeted = 1 + has_left.astype(jnp.int32) + has_right.astype(jnp.int32) + inner.astype(jnp.int32)
    pl.semaphore_wait(barrier, greeted)

    def part(ref, q):
        return ref.at[pl.ds(q * PART, PART)]

    def copy(kind, q, source, target, dg, dt):
        return pltpu.make_async_remote_copy(
            src_ref=part(source, q),
            dst_ref=part(win.at[target], q),
            send_sem=send.at[kind, q],
            recv_sem=recv.at[kind, q],
            device_id=(dg, dt),
            device_id_type=MESH,
        )

    def copies(q):
        up = other - g

        def made(*args):
            return lambda: copy(*args)

        return (
            (made(0, q, raw, slot(0, -1), g, t + 1), has_right, has_left),
            (made(1, q, raw, slot(0, 1), g, t - 1), has_left, has_right),
            (made(2, q, raw, slot(g - mate, 0), mate, t), True, True),
            (made(3, q, raw, slot(g - other, 0), other, t), inner, inner),
            (made(4, q, win.at[slot(0, -1)], slot(g - mate, -1), mate, t), has_left, has_left),
            (made(5, q, win.at[slot(0, 1)], slot(g - mate, 1), mate, t), has_right, has_right),
            (made(6, q, win.at[slot(up, 0)], slot(up, -1), g, t + 1), inner & has_right, inner & has_left),
            (made(7, q, win.at[slot(up, 0)], slot(up, 1), g, t - 1), inner & has_left, inner & has_right),
        )

    def start(q, kinds):
        for made, sent, _ in [copies(q)[k] for k in kinds]:
            pl.when(sent)(lambda made=made: made().start())

    def arrived(q, kinds):
        for made, _, received in [copies(q)[k] for k in kinds]:
            pl.when(received)(lambda made=made: made().wait_recv())

    def first(q, carry):
        start(q, range(4))
        return carry

    lax.fori_loop(0, PARTS, first, 0)

    def clear(index):
        def one(c, carry):
            win[index, c] = jnp.zeros((ZY, X), jnp.float32)
            return carry

        lax.fori_loop(0, C, one, 0)

    for d in (-1, 0, 1):
        pl.when(t == 0)(lambda d=d: clear(slot(d, -1)))
        pl.when(t == TILES - 1)(lambda d=d: clear(slot(d, 1)))
        pl.when(g == 0)(lambda d=d: clear(slot(-1, d)))
        pl.when(g == SLABS - 1)(lambda d=d: clear(slot(1, d)))

    def forward(q, carry):
        arrived(q, (0, 1, 3))
        start(q, (4, 5, 6, 7))
        return carry

    lax.fori_loop(0, PARTS, forward, 0)

    def dot(a, b):
        return jnp.dot(a, b, preferred_element_type=jnp.float32)

    def channel(c, carry):
        field = jnp.concatenate([raw[c] if s == 4 else win[s, c] for s in range(9)], axis=0)
        high, low = split(field)
        both = dot(across[...], high)
        mixed = both[: 4 * ZY] + both[4 * ZY :] + dot(across[: 4 * ZY], low)
        high, low = split(mixed)

        def along(rows, k):
            columns = slice(k * X, (k + 1) * X)
            return (
                dot(high[:rows], along_hi[:, columns])
                + dot(low[:rows], along_hi[:, columns])
                + dot(high[:rows], along_lo[:, columns])
            )

        by_gauss, by_slope, by_curve = along(4 * ZY, 0), along(2 * ZY, 1), along(ZY, 2)
        smooth, grad_y, hess_yy, grad_z = (by_gauss[k * ZY : (k + 1) * ZY] for k in range(4))
        grad_x, hess_xy = by_slope[:ZY], by_slope[ZY:]
        half_trace = (hess_yy + by_curve) * 0.5
        spread = (hess_yy - by_curve) * 0.5
        deviation = jnp.sqrt(spread * spread + hess_xy * hess_xy)
        magnitude = jnp.sqrt(grad_z * grad_z + grad_y * grad_y + grad_x * grad_x)
        for k, value in enumerate((smooth, magnitude, half_trace + deviation, half_trace - deviation)):
            rows = pl.ds(pl.multiple_of((k * C + c) * ZY, ZY), ZY)
            out[0, rows, :] = value[:, :HALF]
            out[1, rows, :] = value[:, HALF:]
        return carry

    def work(q, carry):
        arrived(q, (2, 4, 5, 6, 7))
        return lax.fori_loop(q * PART, (q + 1) * PART, channel, carry)

    lax.fori_loop(0, PARTS, work, 0)

    def finish(q, carry):
        for made, sent, _ in copies(q):
            pl.when(sent)(lambda made=made: made().wait_send())
        return carry

    lax.fori_loop(0, PARTS, finish, 0)


def filtered(raw):
    across, along_hi, along_lo = tables()
    vmem = pl.BlockSpec(memory_space=pltpu.VMEM)
    return pl.pallas_call(
        filter_kernel,
        out_shape=jax.ShapeDtypeStruct((2, FEATURES * ZY, HALF), jnp.float32),
        in_specs=[vmem] * 4,
        out_specs=vmem,
        scratch_shapes=[
            pltpu.VMEM((9, C, ZY, X), jnp.float32),
            pltpu.SemaphoreType.DMA((8, PARTS)),
            pltpu.SemaphoreType.DMA((8, PARTS)),
        ],
        compiler_params=pltpu.CompilerParams(
            collective_id=0, has_side_effects=True, vmem_limit_bytes=40 * 2**20
        ),
    )(raw, jnp.asarray(across), jnp.asarray(along_hi), jnp.asarray(along_lo))


def pool_kernel(features, index, touched, owner, out, row_a, row_b, merged, *accs):
    def summed(rows):
        sub = lax.broadcasted_iota(jnp.int32, (rows, HALF), 0)
        lane = lax.broadcasted_iota(jnp.int32, (rows, HALF), 1)
        return (lax.rem(sub, 2) == 1) | (lane >= 2 * FEATURES)

    pair, tile = summed(2), summed(16)
    start = jnp.where(tile, 0.0, FAR)

    def reset(i, carry):
        for acc in accs:
            acc[pl.ds(i * 16, 16), :] = start
        return carry

    lax.fori_loop(0, ROWS // 16, reset, 0)
    ones = jnp.ones((1, HALF), jnp.float32)

    def turn(half, zy, row):
        values = features[half, pl.ds(zy, FEATURES, stride=ZY), :]
        row[...] = jnp.concatenate([values, -values, values[:31], ones], axis=0).T

    def collect(half, zy, row):
        targets = index.at[zy * 2 + half]
        for v in range(HALF):
            acc = accs[v % ACCS]
            at = pl.ds(targets[v], 2)
            value = jnp.broadcast_to(row[v : v + 1, :], (2, HALF))
            old = acc[at, :]
            acc[at, :] = jnp.where(pair, old + value, jnp.maximum(old, value))

    turn(0, 0, row_a)

    def body(zy, carry):
        turn(1, zy, row_b)
        collect(0, zy, row_a)
        turn(0, jnp.minimum(zy + 1, ZY - 1), row_a)
        collect(1, zy, row_b)
        return carry

    lax.fori_loop(0, ZY, body, 0)

    lane = lax.broadcasted_iota(jnp.int32, (EB, HALF), 1)
    empty = jnp.where(lane >= 2 * FEATURES, 0.0, FAR)

    def fill(b, carry):
        out[b, :EB, :] = empty
        out[b, EB:, :] = jnp.zeros((SENT - EB, HALF), jnp.float32)
        return carry

    lax.fori_loop(0, BLOCKS, fill, 0)
    lane = lax.broadcasted_iota(jnp.int32, (EB // 4, HALF), 1)

    def place(i, carry):
        for k in range(2 * EB // 16):
            rows = pl.ds(pl.multiple_of(i * 2 * EB + k * 16, 16), 16)
            total = accs[0][rows, :]
            for acc in accs[1:]:
                more = acc[rows, :]
                total = jnp.where(tile, total + more, jnp.maximum(total, more))
            merged[pl.ds(k * 16, 16), :] = total
        to = owner[touched[i]]
        out[to, :EB, :] = merged[pl.ds(0, EB, stride=2), :]
        sums = merged[pl.ds(1, EB, stride=2), :]
        packed = jnp.zeros((EB // 4, HALF), jnp.float32)
        for j in range(4):
            group = pltpu.roll(sums[j * 16 : (j + 1) * 16], (32 * j - 16) % HALF, 1)
            packed = jnp.where((lane >= 32 * j) & (lane < 32 * j + 32), group, packed)
        out[to, EB:, :] = packed
        return carry

    lax.fori_loop(0, TOUCH, place, 0)


def pooled(features, index, touched, owner):
    vmem, smem = pl.BlockSpec(memory_space=pltpu.VMEM), pl.BlockSpec(memory_space=pltpu.SMEM)
    return pl.pallas_call(
        pool_kernel,
        out_shape=jax.ShapeDtypeStruct((BLOCKS, SENT, HALF), jnp.float32),
        in_specs=[vmem, smem, smem, smem],
        out_specs=vmem,
        scratch_shapes=[pltpu.VMEM((HALF, HALF), jnp.float32)] * 3
        + [pltpu.VMEM((ROWS, HALF), jnp.float32)] * ACCS,
        compiler_params=pltpu.CompilerParams(vmem_limit_bytes=40 * 2**20),
    )(features, index, touched, owner)


def merge_kernel(mine, out, got, send, recv):
    g, t = lax.axis_index("gz"), lax.axis_index("xy")
    barrier = pltpu.get_barrier_semaphore()

    def peer(k):
        return lax.rem(t + k, TILES)

    def greet(k, carry):
        pl.semaphore_signal(barrier, inc=1, device_id=(g, peer(k)), device_id_type=MESH)
        return carry

    lax.fori_loop(1, TILES, greet, 0)
    pl.semaphore_wait(barrier, TILES - 1)

    def copy(k):
        return pltpu.make_async_remote_copy(
            src_ref=mine.at[peer(k)],
            dst_ref=got.at[k],
            send_sem=send.at[k],
            recv_sem=recv.at[k],
            device_id=(g, peer(k)),
            device_id_type=MESH,
        )

    def start(k, carry):
        copy(k).start()
        return carry

    lax.fori_loop(1, TILES, start, 0)
    lane = lax.broadcasted_iota(jnp.int32, (SENT, HALF), 1)
    row = lax.broadcasted_iota(jnp.int32, (SENT, HALF), 0)
    summed = (lane >= 2 * FEATURES) | (row >= EB)

    def join(k, total):
        copy(k).wait_recv()
        more = got[k]
        return jnp.where(summed, total + more, jnp.maximum(total, more))

    total = lax.fori_loop(1, TILES, join, mine[t])
    extremes = total[:EB]
    packed = total[EB:]
    rest = jnp.concatenate([pltpu.roll(packed, (HALF - 32 * j) % HALF, 1) for j in range(4)], axis=0)
    both = jnp.concatenate([extremes, rest], axis=0).T
    left, right = both[:, :EB], both[:, EB:]
    count = left[HALF - 1 :]
    present = count > 0.0
    share = 1.0 / jnp.maximum(count, 1.0)
    out[:31, :] = left[2 * FEATURES : HALF - 1] * share
    out[31:FEATURES, :] = right[15:32] * share
    out[FEATURES : 2 * FEATURES, :] = jnp.where(present, left[:FEATURES], 0.0)
    out[2 * FEATURES :, :] = jnp.where(present, -left[FEATURES : 2 * FEATURES], 0.0)

    def finish(k, carry):
        copy(k).wait_send()
        return carry

    lax.fori_loop(1, TILES, finish, 0)


def merged_stats(stats):
    vmem = pl.BlockSpec(memory_space=pltpu.VMEM)
    return pl.pallas_call(
        merge_kernel,
        out_shape=jax.ShapeDtypeStruct((3 * FEATURES, EB), jnp.float32),
        in_specs=[vmem],
        out_specs=vmem,
        scratch_shapes=[
            pltpu.VMEM((TILES, SENT, HALF), jnp.float32),
            pltpu.SemaphoreType.DMA((TILES,)),
            pltpu.SemaphoreType.DMA((TILES,)),
        ],
        compiler_params=pltpu.CompilerParams(
            collective_id=1, has_side_effects=True, vmem_limit_bytes=20 * 2**20
        ),
    )(stats)


def per_device(raw_volume, face_slot, touched, block_owner):
    raw = raw_volume.reshape(C, ZY, X)
    slots = face_slot.reshape(2 * ZY, HALF)
    index = jnp.where(slots < 0, TOUCH * EB, slots) * 2
    features = filtered(raw)
    stats = pooled(features, index, touched.reshape(-1), block_owner.reshape(-1))
    return merged_stats(stats)[None, None]


def solution(mesh):
    placed = (P(None, "gz", "xy", None), P("gz", "xy", None), P("gz", "xy", None), P("gz", None))
    return jax.shard_map(
        per_device, mesh=mesh, in_specs=placed, out_specs=P("gz", "xy", None, None), check_vma=False
    )
```

```python
import functools

import jax
import jax.numpy as jnp
import ml_dtypes
import numpy as np
from jax import lax
from jax.experimental import pallas as pl
from jax.experimental.pallas import tpu as pltpu
from jax.sharding import PartitionSpec as P

RADIUS = 8
C = 12
Z = 8
Y = 8
X = 256
EB = 64
TOUCH = 16
BLOCKS = 32
TILES = 32
SLABS = 4
ZY = Z * Y
HALF = X // 2
FEATURES = 4 * C
PARTS = 4
PART = C // PARTS
ACCS = 8
ROW = 4
ROWS = 2 * (TOUCH * EB) + 16
SENT = EB + EB // 4
FAR = -1e30
MESH = pl.DeviceIdType.MESH


def taps():
    sigma = np.float32(RADIUS / 3.0)
    offsets = np.arange(-RADIUS, RADIUS + 1).astype(np.float32)
    gauss = np.exp(-offsets * offsets / (2.0 * sigma * sigma)).astype(np.float32)
    gauss = gauss / gauss.sum()
    slope = -(offsets / sigma) * gauss
    curve = (offsets * offsets / (sigma * sigma) - 1.0) * gauss
    return [tap.astype(np.float64) for tap in (gauss, slope, curve)]


def two_terms(table):
    table = table.astype(np.float32)
    high = table.astype(ml_dtypes.bfloat16)
    low = (table - high.astype(np.float32)).astype(ml_dtypes.bfloat16)
    return high, low


def band(tap, size, start, stop):
    offset = np.arange(start, stop)[None, :] - np.arange(size)[:, None]
    return np.where(np.abs(offset) <= RADIUS, tap[np.clip(offset + RADIUS, 0, 2 * RADIUS)], 0.0)


def tables():
    gauss, slope, curve = taps()
    rows = []
    for kz, ky in ((gauss, gauss), (gauss, slope), (gauss, curve), (slope, gauss)):
        bz = band(kz, Z, -Z, 2 * Z).reshape(Z, 3, Z)
        by = band(ky, Y, -Y, 2 * Y).reshape(Y, 3, Y)
        rows.append(np.einsum("pdz,qey->pqdezy", bz, by).reshape(ZY, 9 * ZY))
    high, low = two_terms(np.concatenate(rows, axis=0))
    across = np.concatenate([high, low], axis=0)
    along = [two_terms(band(tap, X, 0, X).T) for tap in (gauss, slope, curve)]
    return across, np.concatenate([t[0] for t in along], 1), np.concatenate([t[1] for t in along], 1)


def split(values):
    high = values.astype(jnp.bfloat16)
    return high, (values - high.astype(jnp.float32)).astype(jnp.bfloat16)


def slot(dz, dt):
    return (dz + 1) * 3 + (dt + 1)


def filter_kernel(
    raw, faces, across_in, along_hi_in, along_lo_in, out, index,
    win, features, across, along_hi, along_lo, mixed_hi, mixed_lo, send, recv, local, stored,
):
    g, t = lax.axis_index("gz"), lax.axis_index("xy")
    mate = g + 1 - 2 * lax.rem(g, 2)
    inner = (g == 1) | (g == 2)
    other = 3 - g
    has_left, has_right = t > 0, t < TILES - 1
    first_x, last_x = lax.rem(t, ROW) == 0, lax.rem(t, ROW) == ROW - 1
    cross_left, cross_right = inner & first_x & has_left, inner & last_x & has_right

    loads = [
        pltpu.make_async_copy(raw, win.at[slot(0, 0)], local.at[0]),
        pltpu.make_async_copy(across_in, across, local.at[1]),
        pltpu.make_async_copy(along_hi_in, along_hi, local.at[2]),
        pltpu.make_async_copy(along_lo_in, along_lo, local.at[3]),
    ]
    for load in loads:
        load.start()

    barrier = pltpu.get_barrier_semaphore()
    greeted = 0
    for condition, dg, dt in (
        (has_left, g, t - 1),
        (has_right, g, t + 1),
        (inner, other, t),
        (cross_left, other, t - 1),
        (cross_right, other, t + 1),
    ):
        @pl.when(condition)
        def _():
            pl.semaphore_signal(barrier, inc=1, device_id=(dg, dt), device_id_type=MESH)

        greeted += condition.astype(jnp.int32)
    pl.semaphore_signal(barrier, inc=1, device_id=(mate, t), device_id_type=MESH)
    pl.semaphore_wait(barrier, greeted + 1)

    def part(ref, q):
        return ref.at[pl.ds(q * PART, PART)]

    def copy(kind, q, source, target, dg, dt):
        return pltpu.make_async_remote_copy(
            src_ref=part(source, q),
            dst_ref=part(win.at[target], q),
            send_sem=send.at[kind, q],
            recv_sem=recv.at[kind, q],
            device_id=(dg, dt),
            device_id_type=MESH,
        )

    def copies(q):
        up = other - g

        def made(*args):
            return lambda: copy(*args)

        return (
            (made(0, q, raw, slot(0, -1), g, t + 1), has_right, has_left),
            (made(1, q, raw, slot(0, 1), g, t - 1), has_left, has_right),
            (made(2, q, raw, slot(g - mate, 0), mate, t), True, True),
            (made(3, q, raw, slot(g - other, 0), other, t), inner, inner),
            (made(4, q, win.at[slot(0, -1)], slot(g - mate, -1), mate, t), has_left, has_left),
            (made(5, q, win.at[slot(0, 1)], slot(g - mate, 1), mate, t), has_right, has_right),
            (made(6, q, win.at[slot(up, 0)], slot(up, -1), g, t + 1), inner & ~last_x, inner & ~first_x),
            (made(7, q, win.at[slot(up, 0)], slot(up, 1), g, t - 1), inner & ~first_x, inner & ~last_x),
            (made(8, q, raw, slot(g - other, -1), other, t + 1), cross_right, cross_left),
            (made(9, q, raw, slot(g - other, 1), other, t - 1), cross_left, cross_right),
        )

    def start(q, kinds):
        for made, sent, _ in [copies(q)[k] for k in kinds]:
            pl.when(sent)(lambda made=made: made().start())

    def arrived(q, kinds):
        for made, _, received in [copies(q)[k] for k in kinds]:
            pl.when(received)(lambda made=made: made().wait_recv())

    def first(q, carry):
        start(q, (3, 0, 1, 8, 9, 2))
        return carry

    lax.fori_loop(0, PARTS, first, 0)

    def clear(index):
        def one(c, carry):
            win[index, c] = jnp.zeros((ZY, X), jnp.float32)
            return carry

        lax.fori_loop(0, C, one, 0)

    for d in (-1, 0, 1):
        pl.when(t == 0)(lambda d=d: clear(slot(d, -1)))
        pl.when(t == TILES - 1)(lambda d=d: clear(slot(d, 1)))
        pl.when(g == 0)(lambda d=d: clear(slot(-1, d)))
        pl.when(g == SLABS - 1)(lambda d=d: clear(slot(1, d)))
    for half in range(2):
        found = faces[:, half * HALF : (half + 1) * HALF]
        index[half] = jnp.where(found < 0, TOUCH * EB, found) * 2
    for load in loads:
        load.wait()

    def forward(q, carry):
        arrived(q, (0, 1))
        start(q, (4, 5))
        arrived(q, (3,))
        start(q, (6, 7))
        return carry

    lax.fori_loop(0, PARTS, forward, 0)

    def dot(a, b):
        return jnp.dot(a, b, preferred_element_type=jnp.float32)

    rows = PART * ZY

    def store(q, half, k):
        at = pl.ds(pl.multiple_of(k * C * ZY + q * rows, 8), rows)
        return pltpu.make_async_copy(features.at[half, at], out.at[half, at], stored.at[q, half * 4 + k])

    def work(q, carry):
        arrived(q, (2, 4, 5, 6, 7, 8, 9))
        for j in range(PART):
            c = q * PART + j
            high, low = split(jnp.concatenate([win[s, c] for s in range(9)], axis=0))
            both = dot(across[...], high)
            high, low = split(both[: 4 * ZY] + both[4 * ZY :] + dot(across[: 4 * ZY], low))
            for k in range(4):
                mixed_hi[k, j * ZY : (j + 1) * ZY, :] = high[k * ZY : (k + 1) * ZY]
                mixed_lo[k, j * ZY : (j + 1) * ZY, :] = low[k * ZY : (k + 1) * ZY]
        high, low = mixed_hi[...].reshape(4 * rows, X), mixed_lo[...].reshape(4 * rows, X)

        def along(n, k):
            columns = slice(k * X, (k + 1) * X)
            return (
                dot(high[:n], along_hi[:, columns])
                + dot(low[:n], along_hi[:, columns])
                + dot(high[:n], along_lo[:, columns])
            )

        by_gauss, by_slope, by_curve = along(4 * rows, 0), along(2 * rows, 1), along(rows, 2)
        smooth, grad_y, hess_yy, grad_z = (by_gauss[k * rows : (k + 1) * rows] for k in range(4))
        grad_x, hess_xy = by_slope[:rows], by_slope[rows:]
        half_trace = (hess_yy + by_curve) * 0.5
        spread = (hess_yy - by_curve) * 0.5
        deviation = jnp.sqrt(spread * spread + hess_xy * hess_xy)
        magnitude = jnp.sqrt(grad_z * grad_z + grad_y * grad_y + grad_x * grad_x)
        for k, value in enumerate((smooth, magnitude, half_trace + deviation, half_trace - deviation)):
            at = pl.ds(pl.multiple_of(k * C * ZY + q * rows, 8), rows)
            features[0, at, :] = value[:, :HALF]
            features[1, at, :] = value[:, HALF:]
            store(q, 0, k).start()
            store(q, 1, k).start()
        return carry

    lax.fori_loop(0, PARTS, work, 0)

    def finish(q, carry):
        for made, sent, _ in copies(q):
            pl.when(sent)(lambda made=made: made().wait_send())
        for k in range(4):
            store(q, 0, k).wait()
            store(q, 1, k).wait()
        return carry

    lax.fori_loop(0, PARTS, finish, 0)


def filtered(raw, faces):
    across, along_hi, along_lo = tables()
    vmem, hbm = pl.BlockSpec(memory_space=pltpu.VMEM), pl.BlockSpec(memory_space=pl.ANY)
    return pl.pallas_call(
        filter_kernel,
        out_shape=(
            jax.ShapeDtypeStruct((2, FEATURES * ZY, HALF), jnp.float32),
            jax.ShapeDtypeStruct((2, ZY, HALF), jnp.int32),
        ),
        in_specs=[hbm, vmem, hbm, hbm, hbm],
        out_specs=(hbm, vmem),
        scratch_shapes=[
            pltpu.VMEM((9, C, ZY, X), jnp.float32),
            pltpu.VMEM((2, FEATURES * ZY, HALF), jnp.float32),
            pltpu.VMEM(across.shape, jnp.bfloat16),
            pltpu.VMEM(along_hi.shape, jnp.bfloat16),
            pltpu.VMEM(along_lo.shape, jnp.bfloat16),
            pltpu.VMEM((4, PART * ZY, X), jnp.bfloat16),
            pltpu.VMEM((4, PART * ZY, X), jnp.bfloat16),
            pltpu.SemaphoreType.DMA((10, PARTS)),
            pltpu.SemaphoreType.DMA((10, PARTS)),
            pltpu.SemaphoreType.DMA((4,)),
            pltpu.SemaphoreType.DMA((PARTS, 8)),
        ],
        compiler_params=pltpu.CompilerParams(
            collective_id=0, has_side_effects=True, vmem_limit_bytes=40 * 2**20
        ),
    )(raw, faces, jnp.asarray(across), jnp.asarray(along_hi), jnp.asarray(along_lo))


def pool_kernel(features, index, touched, owner, out, row_a, row_b, merged, *accs):
    def summed(rows):
        sub = lax.broadcasted_iota(jnp.int32, (rows, HALF), 0)
        lane = lax.broadcasted_iota(jnp.int32, (rows, HALF), 1)
        return (lax.rem(sub, 2) == 1) | (lane >= 2 * FEATURES)

    pair, tile = summed(2), summed(16)
    start = jnp.where(tile, 0.0, FAR)

    def reset(i, carry):
        for acc in accs:
            acc[pl.ds(i * 16, 16), :] = start
        return carry

    lax.fori_loop(0, ROWS // 16, reset, 0)
    ones = jnp.ones((1, HALF), jnp.float32)

    def turn(half, zy, row):
        values = features[half, pl.ds(zy, FEATURES, stride=ZY), :]
        row[...] = jnp.concatenate([values, -values, values[:31], ones], axis=0).T

    def collect(half, zy, row):
        targets = index.at[half * ZY + zy]
        for v in range(HALF):
            acc = accs[v % ACCS]
            at = pl.ds(targets[v], 2)
            value = jnp.broadcast_to(row[v : v + 1, :], (2, HALF))
            old = acc[at, :]
            acc[at, :] = jnp.where(pair, old + value, jnp.maximum(old, value))

    turn(0, 0, row_a)

    def body(zy, carry):
        turn(1, zy, row_b)
        collect(0, zy, row_a)
        turn(0, jnp.minimum(zy + 1, ZY - 1), row_a)
        collect(1, zy, row_b)
        return carry

    lax.fori_loop(0, ZY, body, 0)

    lane = lax.broadcasted_iota(jnp.int32, (EB, HALF), 1)
    empty = jnp.where(lane >= 2 * FEATURES, 0.0, FAR)

    def fill(b, carry):
        out[b, :EB, :] = empty
        out[b, EB:, :] = jnp.zeros((SENT - EB, HALF), jnp.float32)
        return carry

    lax.fori_loop(0, BLOCKS, fill, 0)
    lane = lax.broadcasted_iota(jnp.int32, (EB // 4, HALF), 1)

    def place(i, carry):
        for k in range(2 * EB // 16):
            rows = pl.ds(pl.multiple_of(i * 2 * EB + k * 16, 16), 16)
            total = accs[0][rows, :]
            for acc in accs[1:]:
                more = acc[rows, :]
                total = jnp.where(tile, total + more, jnp.maximum(total, more))
            merged[pl.ds(k * 16, 16), :] = total
        to = owner[touched[i]]
        out[to, :EB, :] = merged[pl.ds(0, EB, stride=2), :]
        sums = merged[pl.ds(1, EB, stride=2), :]
        packed = jnp.zeros((EB // 4, HALF), jnp.float32)
        for j in range(4):
            group = pltpu.roll(sums[j * 16 : (j + 1) * 16], (32 * j - 16) % HALF, 1)
            packed = jnp.where((lane >= 32 * j) & (lane < 32 * j + 32), group, packed)
        out[to, EB:, :] = packed
        return carry

    lax.fori_loop(0, TOUCH, place, 0)


def pooled(features, index, touched, owner):
    vmem, smem = pl.BlockSpec(memory_space=pltpu.VMEM), pl.BlockSpec(memory_space=pltpu.SMEM)
    return pl.pallas_call(
        pool_kernel,
        out_shape=jax.ShapeDtypeStruct((BLOCKS, SENT, HALF), jnp.float32),
        in_specs=[vmem, smem, smem, smem],
        out_specs=vmem,
        scratch_shapes=[pltpu.VMEM((HALF, HALF), jnp.float32)] * 3
        + [pltpu.VMEM((ROWS, HALF), jnp.float32)] * ACCS,
        compiler_params=pltpu.CompilerParams(vmem_limit_bytes=40 * 2**20),
    )(features, index, touched, owner)


def merge_kernel(mine, out, got, send, recv):
    g, t = lax.axis_index("gz"), lax.axis_index("xy")
    barrier = pltpu.get_barrier_semaphore()

    def peer(k):
        return lax.rem(t + k, TILES)

    def greet(k, carry):
        pl.semaphore_signal(barrier, inc=1, device_id=(g, peer(k)), device_id_type=MESH)
        return carry

    lax.fori_loop(1, TILES, greet, 0)
    pl.semaphore_wait(barrier, TILES - 1)

    def copy(k):
        return pltpu.make_async_remote_copy(
            src_ref=mine.at[peer(k)],
            dst_ref=got.at[k],
            send_sem=send.at[k],
            recv_sem=recv.at[k],
            device_id=(g, peer(k)),
            device_id_type=MESH,
        )

    def start(k, carry):
        copy(k).start()
        return carry

    lax.fori_loop(1, TILES, start, 0)
    lane = lax.broadcasted_iota(jnp.int32, (SENT, HALF), 1)
    row = lax.broadcasted_iota(jnp.int32, (SENT, HALF), 0)
    summed = (lane >= 2 * FEATURES) | (row >= EB)

    def join(k, total):
        copy(k).wait_recv()
        more = got[k]
        return jnp.where(summed, total + more, jnp.maximum(total, more))

    total = lax.fori_loop(1, TILES, join, mine[t])
    extremes = total[:EB]
    packed = total[EB:]
    rest = jnp.concatenate([pltpu.roll(packed, (HALF - 32 * j) % HALF, 1) for j in range(4)], axis=0)
    both = jnp.concatenate([extremes, rest], axis=0).T
    left, right = both[:, :EB], both[:, EB:]
    count = left[HALF - 1 :]
    present = count > 0.0
    share = 1.0 / jnp.maximum(count, 1.0)
    out[:31, :] = left[2 * FEATURES : HALF - 1] * share
    out[31:FEATURES, :] = right[15:32] * share
    out[FEATURES : 2 * FEATURES, :] = jnp.where(present, left[:FEATURES], 0.0)
    out[2 * FEATURES :, :] = jnp.where(present, -left[FEATURES : 2 * FEATURES], 0.0)

    def finish(k, carry):
        copy(k).wait_send()
        return carry

    lax.fori_loop(1, TILES, finish, 0)


def merged_stats(stats):
    vmem = pl.BlockSpec(memory_space=pltpu.VMEM)
    return pl.pallas_call(
        merge_kernel,
        out_shape=jax.ShapeDtypeStruct((3 * FEATURES, EB), jnp.float32),
        in_specs=[vmem],
        out_specs=vmem,
        scratch_shapes=[
            pltpu.VMEM((TILES, SENT, HALF), jnp.float32),
            pltpu.SemaphoreType.DMA((TILES,)),
            pltpu.SemaphoreType.DMA((TILES,)),
        ],
        compiler_params=pltpu.CompilerParams(
            collective_id=1, has_side_effects=True, vmem_limit_bytes=20 * 2**20
        ),
    )(stats)


def per_device(raw_volume, face_slot, touched, block_owner):
    features, index = filtered(raw_volume.reshape(C, ZY, X), face_slot.reshape(ZY, X))
    stats = pooled(features, index.reshape(2 * ZY, HALF), touched.reshape(-1), block_owner.reshape(-1))
    return merged_stats(stats)[None, None]


def solution(mesh):
    placed = (P(None, "gz", "xy", None), P("gz", "xy", None), P("gz", "xy", None), P("gz", None))
    return jax.shard_map(
        per_device, mesh=mesh, in_specs=placed, out_specs=P("gz", "xy", None, None), check_vma=False
    )
```

```python
import functools

import jax
import jax.numpy as jnp
import ml_dtypes
import numpy as np
from jax import lax
from jax.experimental import pallas as pl
from jax.experimental.pallas import tpu as pltpu
from jax.sharding import PartitionSpec as P

RADIUS = 8
C = 12
Z = 8
Y = 8
X = 256
EB = 64
TOUCH = 16
BLOCKS = 32
TILES = 32
SLABS = 4
ZY = Z * Y
HALF = X // 2
FEATURES = 4 * C
PARTS = 4
PART = C // PARTS
ACCS = 8
ROW = 4
ROWS = 2 * (TOUCH * EB) + 16
SENT = EB + EB // 4
FAR = -1e30
MESH = pl.DeviceIdType.MESH


def taps():
    sigma = np.float32(RADIUS / 3.0)
    offsets = np.arange(-RADIUS, RADIUS + 1).astype(np.float32)
    gauss = np.exp(-offsets * offsets / (2.0 * sigma * sigma)).astype(np.float32)
    gauss = gauss / gauss.sum()
    slope = -(offsets / sigma) * gauss
    curve = (offsets * offsets / (sigma * sigma) - 1.0) * gauss
    return [tap.astype(np.float64) for tap in (gauss, slope, curve)]


def two_terms(table):
    table = table.astype(np.float32)
    high = table.astype(ml_dtypes.bfloat16)
    low = (table - high.astype(np.float32)).astype(ml_dtypes.bfloat16)
    return high, low


def band(tap, size, start, stop):
    offset = np.arange(start, stop)[None, :] - np.arange(size)[:, None]
    return np.where(np.abs(offset) <= RADIUS, tap[np.clip(offset + RADIUS, 0, 2 * RADIUS)], 0.0)


def tables():
    gauss, slope, curve = taps()
    rows = []
    for kz, ky in ((gauss, gauss), (gauss, slope), (gauss, curve), (slope, gauss)):
        bz = band(kz, Z, -Z, 2 * Z).reshape(Z, 3, Z)
        by = band(ky, Y, -Y, 2 * Y).reshape(Y, 3, Y)
        rows.append(np.einsum("pdz,qey->pqdezy", bz, by).reshape(ZY, 9 * ZY))
    weights = np.concatenate(rows, axis=0).reshape(4 * ZY, 3, 3 * ZY)

    def both_terms(*blocks):
        return np.concatenate(two_terms(np.concatenate([weights[:, d + 1] for d in blocks], axis=1)), axis=0)

    near = np.stack([both_terms(0, 1), both_terms(0, -1)])
    far = np.stack([both_terms(-1), both_terms(1)])
    along = [two_terms(band(tap, X, 0, X).T) for tap in (gauss, slope, curve)]
    return near, far, np.concatenate([t[0] for t in along], 1), np.concatenate([t[1] for t in along], 1)


def split(values):
    high = values.astype(jnp.bfloat16)
    return high, (values - high.astype(jnp.float32)).astype(jnp.bfloat16)


def slot(dz, dt):
    return (dz + 1) * 3 + (dt + 1)


def filter_kernel(
    raw, faces_in, near_in, far_in, along_hi_in, along_lo_in, out, index,
    win, faces, partial, features, near, far, along_hi, along_lo, mixed_hi, mixed_lo, send, recv, local, stored,
):
    g, t = lax.axis_index("gz"), lax.axis_index("xy")
    odd = lax.rem(g, 2)
    mate = g + 1 - 2 * odd
    inner = (g == 1) | (g == 2)
    other = 3 - g
    has_left, has_right = t > 0, t < TILES - 1
    column = lax.rem(t, ROW)
    first_x, last_x = column == 0, column == ROW - 1
    second_x, third_x = column == 1, column == 2
    cross_left, cross_right = inner & first_x & has_left, inner & last_x & has_right

    loads = [
        pltpu.make_async_copy(source, target, local.at[k])
        for k, (source, target) in enumerate(
            (
                (raw, win.at[slot(0, 0)]),
                (faces_in, faces),
                (near_in.at[odd], near),
                (far_in.at[odd], far),
                (along_hi_in, along_hi),
                (along_lo_in, along_lo),
            )
        )
    ]
    for load in loads:
        load.start()

    barrier = pltpu.get_barrier_semaphore()
    greeted = 0
    for condition, dg, dt in (
        (has_left, g, t - 1),
        (has_right, g, t + 1),
        (inner, other, t),
        (cross_left, other, t - 1),
        (cross_right, other, t + 1),
    ):
        @pl.when(condition)
        def _():
            pl.semaphore_signal(barrier, inc=1, device_id=(dg, dt), device_id_type=MESH)

        greeted += condition.astype(jnp.int32)
    pl.semaphore_signal(barrier, inc=1, device_id=(mate, t), device_id_type=MESH)
    pl.semaphore_wait(barrier, greeted + 1)

    def part(ref, q):
        return ref.at[pl.ds(q * PART, PART)]

    def copy(kind, q, source, target, dg, dt):
        return pltpu.make_async_remote_copy(
            src_ref=part(source, q),
            dst_ref=part(win.at[target], q),
            send_sem=send.at[kind, q],
            recv_sem=recv.at[kind, q],
            device_id=(dg, dt),
            device_id_type=MESH,
        )

    def copies(q):
        up = other - g

        def made(*args):
            return lambda: copy(*args)

        middle = inner & (second_x | third_x)
        left, right = win.at[slot(0, -1)], win.at[slot(0, 1)]
        third = win.at[slot(up, 0)]
        return (
            (made(0, q, raw, slot(0, -1), g, t + 1), has_right, has_left),
            (made(1, q, raw, slot(0, 1), g, t - 1), has_left, has_right),
            (made(2, q, raw, slot(g - mate, 0), mate, t), True, True),
            (made(3, q, raw, slot(g - other, 0), other, t), inner, inner),
            (made(4, q, left, slot(g - mate, -1), mate, t), has_left, has_left),
            (made(5, q, right, slot(g - mate, 1), mate, t), has_right, has_right),
            (made(6, q, third, slot(up, -1), g, t + 1), middle, inner & (third_x | last_x)),
            (made(7, q, third, slot(up, 1), g, t - 1), middle, inner & (first_x | second_x)),
            (made(8, q, raw, slot(g - other, -1), other, t + 1), cross_right, cross_left),
            (made(9, q, raw, slot(g - other, 1), other, t - 1), cross_left, cross_right),
            (made(10, q, left, slot(g - other, -1), other, t), inner & second_x, inner & second_x),
            (made(11, q, right, slot(g - other, 1), other, t), inner & third_x, inner & third_x),
        )

    def start(q, kinds):
        for made, sent, _ in [copies(q)[k] for k in kinds]:
            pl.when(sent)(lambda made=made: made().start())

    def arrived(q, kinds, where=True):
        for made, _, received in [copies(q)[k] for k in kinds]:
            pl.when(received & where)(lambda made=made: made().wait_recv())

    def first(q, carry):
        start(q, (3, 0, 1, 8, 9, 2))
        return carry

    lax.fori_loop(0, PARTS, first, 0)

    def clear(target):
        def one(c, carry):
            win[target, c] = jnp.zeros((ZY, X), jnp.float32)
            return carry

        lax.fori_loop(0, C, one, 0)

    for d in (0, mate - g):
        pl.when(t == 0)(lambda d=d: clear(slot(d, -1)))
        pl.when(t == TILES - 1)(lambda d=d: clear(slot(d, 1)))
    pl.when(inner & (t == 0))(lambda: clear(slot(other - g, -1)))
    pl.when(inner & (t == TILES - 1))(lambda: clear(slot(other - g, 1)))
    for load in loads:
        load.wait()
    for half in range(2):
        found = faces[:, half * HALF : (half + 1) * HALF]
        index[half] = jnp.where(found < 0, TOUCH * EB, found) * 2

    def dot(a, b):
        return jnp.dot(a, b, preferred_element_type=jnp.float32)

    def across(weights, blocks, c):
        high, low = split(jnp.concatenate([win[block, c] for block in blocks], axis=0))
        both = dot(weights[...], high)
        return both[: 4 * ZY] + both[4 * ZY :] + dot(weights[: 4 * ZY], low)

    def forward(q):
        arrived(q, (0, 1))
        start(q, (4, 5, 10, 11))
        arrived(q, (3,), second_x | third_x)
        start(q, (6, 7))

    def begin(q):
        arrived(q, (2, 4, 5))
        for j in range(PART):
            c = q * PART + j
            partial[c] = across(near, [slot(d, dt) for d in (0, mate - g) for dt in (-1, 0, 1)], c)

    rows = PART * ZY

    def store(q, half, k):
        at = pl.ds(pl.multiple_of(k * C * ZY + q * rows, 8), rows)
        return pltpu.make_async_copy(features.at[half, at], out.at[half, at], stored.at[q, half * 4 + k])

    def work(q, carry):
        arrived(q, (3,), first_x | last_x)
        arrived(q, (6, 7, 8, 9, 10, 11))

        @pl.when(inner)
        def _():
            for j in range(PART):
                c = q * PART + j
                partial[c] += across(far, [slot(other - g, dt) for dt in (-1, 0, 1)], c)

        for j in range(PART):
            high, low = split(partial[q * PART + j])
            for k in range(4):
                mixed_hi[k, j * ZY : (j + 1) * ZY, :] = high[k * ZY : (k + 1) * ZY]
                mixed_lo[k, j * ZY : (j + 1) * ZY, :] = low[k * ZY : (k + 1) * ZY]
        high, low = mixed_hi[...].reshape(4 * rows, X), mixed_lo[...].reshape(4 * rows, X)

        def along(n, k):
            columns = slice(k * X, (k + 1) * X)
            return (
                dot(high[:n], along_hi[:, columns])
                + dot(low[:n], along_hi[:, columns])
                + dot(high[:n], along_lo[:, columns])
            )

        by_gauss, by_slope, by_curve = along(4 * rows, 0), along(2 * rows, 1), along(rows, 2)
        smooth, grad_y, hess_yy, grad_z = (by_gauss[k * rows : (k + 1) * rows] for k in range(4))
        grad_x, hess_xy = by_slope[:rows], by_slope[rows:]
        half_trace = (hess_yy + by_curve) * 0.5
        spread = (hess_yy - by_curve) * 0.5
        deviation = jnp.sqrt(spread * spread + hess_xy * hess_xy)
        magnitude = jnp.sqrt(grad_z * grad_z + grad_y * grad_y + grad_x * grad_x)
        for k, value in enumerate((smooth, magnitude, half_trace + deviation, half_trace - deviation)):
            at = pl.ds(pl.multiple_of(k * C * ZY + q * rows, 8), rows)
            features[0, at, :] = value[:, :HALF]
            features[1, at, :] = value[:, HALF:]
            store(q, 0, k).start()
            store(q, 1, k).start()
        return carry

    forward(0)

    def near_work(q, carry):
        forward(q)
        begin(q - 1)
        return carry

    lax.fori_loop(1, PARTS, near_work, 0)
    begin(PARTS - 1)
    lax.fori_loop(0, PARTS, work, 0)

    def finish(q, carry):
        for made, sent, _ in copies(q):
            pl.when(sent)(lambda made=made: made().wait_send())
        for k in range(4):
            store(q, 0, k).wait()
            store(q, 1, k).wait()
        return carry

    lax.fori_loop(0, PARTS, finish, 0)


def filtered(raw, faces):
    near, far, along_hi, along_lo = tables()
    hbm = pl.BlockSpec(memory_space=pltpu.HBM)
    return pl.pallas_call(
        filter_kernel,
        out_shape=(
            jax.ShapeDtypeStruct((2, FEATURES * ZY, HALF), jnp.float32),
            jax.ShapeDtypeStruct((2, ZY, HALF), jnp.int32),
        ),
        in_specs=[hbm] * 6,
        out_specs=(pl.BlockSpec(memory_space=pl.ANY), pl.BlockSpec(memory_space=pltpu.VMEM)),
        scratch_shapes=[
            pltpu.VMEM((9, C, ZY, X), jnp.float32),
            pltpu.VMEM((ZY, X), jnp.int32),
            pltpu.VMEM((C, 4 * ZY, X), jnp.float32),
            pltpu.VMEM((2, FEATURES * ZY, HALF), jnp.float32),
            pltpu.VMEM(near.shape[1:], jnp.bfloat16),
            pltpu.VMEM(far.shape[1:], jnp.bfloat16),
            pltpu.VMEM(along_hi.shape, jnp.bfloat16),
            pltpu.VMEM(along_lo.shape, jnp.bfloat16),
            pltpu.VMEM((4, PART * ZY, X), jnp.bfloat16),
            pltpu.VMEM((4, PART * ZY, X), jnp.bfloat16),
            pltpu.SemaphoreType.DMA((12, PARTS)),
            pltpu.SemaphoreType.DMA((12, PARTS)),
            pltpu.SemaphoreType.DMA((6,)),
            pltpu.SemaphoreType.DMA((PARTS, 8)),
        ],
        compiler_params=pltpu.CompilerParams(
            collective_id=0, has_side_effects=True, vmem_limit_bytes=40 * 2**20
        ),
    )(raw, faces, *(jnp.asarray(table) for table in (near, far, along_hi, along_lo)))


def pool_kernel(features, index, touched, owner, out, row_a, row_b, merged, *accs):
    def summed(rows):
        sub = lax.broadcasted_iota(jnp.int32, (rows, HALF), 0)
        lane = lax.broadcasted_iota(jnp.int32, (rows, HALF), 1)
        return (lax.rem(sub, 2) == 1) | (lane >= 2 * FEATURES)

    pair, tile = summed(2), summed(16)
    start = jnp.where(tile, 0.0, FAR)

    def reset(i, carry):
        for acc in accs:
            acc[pl.ds(i * 16, 16), :] = start
        return carry

    lax.fori_loop(0, ROWS // 16, reset, 0)
    ones = jnp.ones((1, HALF), jnp.float32)

    def turn(half, zy, row):
        values = features[half, pl.ds(zy, FEATURES, stride=ZY), :]
        row[...] = jnp.concatenate([values, -values, values[:31], ones], axis=0).T

    def collect(half, zy, row):
        targets = index.at[half * ZY + zy]
        for v in range(HALF):
            acc = accs[v % ACCS]
            at = pl.ds(targets[v], 2)
            value = jnp.broadcast_to(row[v : v + 1, :], (2, HALF))
            old = acc[at, :]
            acc[at, :] = jnp.where(pair, old + value, jnp.maximum(old, value))

    turn(0, 0, row_a)

    def body(zy, carry):
        turn(1, zy, row_b)
        collect(0, zy, row_a)
        turn(0, jnp.minimum(zy + 1, ZY - 1), row_a)
        collect(1, zy, row_b)
        return carry

    lax.fori_loop(0, ZY, body, 0)

    lane = lax.broadcasted_iota(jnp.int32, (EB, HALF), 1)
    empty = jnp.where(lane >= 2 * FEATURES, 0.0, FAR)

    def fill(b, carry):
        out[b, :EB, :] = empty
        out[b, EB:, :] = jnp.zeros((SENT - EB, HALF), jnp.float32)
        return carry

    lax.fori_loop(0, BLOCKS, fill, 0)
    lane = lax.broadcasted_iota(jnp.int32, (EB // 4, HALF), 1)

    def place(i, carry):
        for k in range(2 * EB // 16):
            rows = pl.ds(pl.multiple_of(i * 2 * EB + k * 16, 16), 16)
            total = accs[0][rows, :]
            for acc in accs[1:]:
                more = acc[rows, :]
                total = jnp.where(tile, total + more, jnp.maximum(total, more))
            merged[pl.ds(k * 16, 16), :] = total
        to = owner[touched[i]]
        out[to, :EB, :] = merged[pl.ds(0, EB, stride=2), :]
        sums = merged[pl.ds(1, EB, stride=2), :]
        packed = jnp.zeros((EB // 4, HALF), jnp.float32)
        for j in range(4):
            group = pltpu.roll(sums[j * 16 : (j + 1) * 16], (32 * j - 16) % HALF, 1)
            packed = jnp.where((lane >= 32 * j) & (lane < 32 * j + 32), group, packed)
        out[to, EB:, :] = packed
        return carry

    lax.fori_loop(0, TOUCH, place, 0)


def pooled(features, index, touched, owner):
    vmem, smem = pl.BlockSpec(memory_space=pltpu.VMEM), pl.BlockSpec(memory_space=pltpu.SMEM)
    return pl.pallas_call(
        pool_kernel,
        out_shape=jax.ShapeDtypeStruct((BLOCKS, SENT, HALF), jnp.float32),
        in_specs=[vmem, smem, smem, smem],
        out_specs=vmem,
        scratch_shapes=[pltpu.VMEM((HALF, HALF), jnp.float32)] * 3
        + [pltpu.VMEM((ROWS, HALF), jnp.float32)] * ACCS,
        compiler_params=pltpu.CompilerParams(vmem_limit_bytes=40 * 2**20),
    )(features, index, touched, owner)


def merge_kernel(mine, out, got, send, recv):
    g, t = lax.axis_index("gz"), lax.axis_index("xy")
    barrier = pltpu.get_barrier_semaphore()

    def peer(k):
        return lax.rem(t + k, TILES)

    def greet(k, carry):
        pl.semaphore_signal(barrier, inc=1, device_id=(g, peer(k)), device_id_type=MESH)
        return carry

    lax.fori_loop(1, TILES, greet, 0)
    pl.semaphore_wait(barrier, TILES - 1)

    def copy(k):
        return pltpu.make_async_remote_copy(
            src_ref=mine.at[peer(k)],
            dst_ref=got.at[k],
            send_sem=send.at[k],
            recv_sem=recv.at[k],
            device_id=(g, peer(k)),
            device_id_type=MESH,
        )

    def start(k, carry):
        copy(k).start()
        return carry

    lax.fori_loop(1, TILES, start, 0)
    lane = lax.broadcasted_iota(jnp.int32, (SENT, HALF), 1)
    row = lax.broadcasted_iota(jnp.int32, (SENT, HALF), 0)
    summed = (lane >= 2 * FEATURES) | (row >= EB)

    def join(k, total):
        copy(k).wait_recv()
        more = got[k]
        return jnp.where(summed, total + more, jnp.maximum(total, more))

    total = lax.fori_loop(1, TILES, join, mine[t])
    extremes, packed = total[:EB], total[EB:]
    rest = jnp.concatenate([pltpu.roll(packed, (HALF + 16 - 32 * j) % HALF, 1) for j in range(4)], axis=0)
    count = extremes[:, HALF - 1 :]
    present = count > 0.0
    lane = lax.broadcasted_iota(jnp.int32, (EB, HALF), 1)
    means = jnp.where(lane < 31, pltpu.roll(extremes, HALF - 2 * FEATURES, 1), rest) / jnp.maximum(count, 1.0)
    signed = jnp.where(present, jnp.where(lane < FEATURES, extremes, -extremes), 0.0)
    shifted = pltpu.roll(signed, FEATURES, 1)
    out[:, :HALF] = jnp.where(lane < FEATURES, means, shifted)
    out[:, HALF:] = shifted[:, : 3 * FEATURES - HALF]

    def finish(k, carry):
        copy(k).wait_send()
        return carry

    lax.fori_loop(1, TILES, finish, 0)


def merged_stats(stats):
    vmem = pl.BlockSpec(memory_space=pltpu.VMEM)
    return pl.pallas_call(
        merge_kernel,
        out_shape=jax.ShapeDtypeStruct((EB, 3 * FEATURES), jnp.float32),
        in_specs=[vmem],
        out_specs=vmem,
        scratch_shapes=[
            pltpu.VMEM((TILES, SENT, HALF), jnp.float32),
            pltpu.SemaphoreType.DMA((TILES,)),
            pltpu.SemaphoreType.DMA((TILES,)),
        ],
        compiler_params=pltpu.CompilerParams(
            collective_id=1, has_side_effects=True, vmem_limit_bytes=20 * 2**20
        ),
    )(stats)


def per_device(raw_volume, face_slot, touched, block_owner):
    features, index = filtered(raw_volume.reshape(C, ZY, X), face_slot.reshape(ZY, X))
    stats = pooled(features, index.reshape(2 * ZY, HALF), touched.reshape(-1), block_owner.reshape(-1))
    return merged_stats(stats).T[None, None]


def solution(mesh):
    placed = (P(None, "gz", "xy", None), P("gz", "xy", None), P("gz", "xy", None), P("gz", None))
    return jax.shard_map(
        per_device, mesh=mesh, in_specs=placed, out_specs=P("gz", "xy", None, None), check_vma=False
    )
```

```python
import functools

import jax
import jax.numpy as jnp
import ml_dtypes
import numpy as np
from jax import lax
from jax.experimental import pallas as pl
from jax.experimental.pallas import tpu as pltpu
from jax.sharding import PartitionSpec as P

RADIUS = 8
C = 12
Z = 8
Y = 8
X = 256
EB = 64
TOUCH = 16
BLOCKS = 32
TILES = 32
SLABS = 4
ZY = Z * Y
HALF = X // 2
FEATURES = 4 * C
PARTS = 4
PART = C // PARTS
ACCS = 8
ROW = 4
ROWS = 2 * (TOUCH * EB) + 16
SENT = EB + EB // 4
FAR = -1e30
STEP = ZY + 1
AHEAD = 4
VMEM_BYTES = 62 * 2**20
MESH = pl.DeviceIdType.MESH


def taps():
    sigma = np.float32(RADIUS / 3.0)
    offsets = np.arange(-RADIUS, RADIUS + 1).astype(np.float32)
    gauss = np.exp(-offsets * offsets / (2.0 * sigma * sigma)).astype(np.float32)
    gauss = gauss / gauss.sum()
    slope = -(offsets / sigma) * gauss
    curve = (offsets * offsets / (sigma * sigma) - 1.0) * gauss
    return [tap.astype(np.float64) for tap in (gauss, slope, curve)]


def two_terms(table):
    table = table.astype(np.float32)
    high = table.astype(ml_dtypes.bfloat16)
    low = (table - high.astype(np.float32)).astype(ml_dtypes.bfloat16)
    return high, low


def band(tap, size, start, stop):
    offset = np.arange(start, stop)[None, :] - np.arange(size)[:, None]
    return np.where(np.abs(offset) <= RADIUS, tap[np.clip(offset + RADIUS, 0, 2 * RADIUS)], 0.0)


def tables():
    gauss, slope, curve = taps()
    rows = []
    for kz, ky in ((gauss, gauss), (gauss, slope), (gauss, curve), (slope, gauss)):
        bz = band(kz, Z, -Z, 2 * Z).reshape(Z, 3, Z)
        by = band(ky, Y, -Y, 2 * Y).reshape(Y, 3, Y)
        rows.append(np.einsum("pdz,qey->pqdezy", bz, by).reshape(ZY, 9 * ZY))
    weights = np.concatenate(rows, axis=0).reshape(4 * ZY, 3, 3 * ZY)

    def both_terms(*blocks):
        return np.concatenate(two_terms(np.concatenate([weights[:, d + 1] for d in blocks], axis=1)), axis=0)

    near = np.stack([both_terms(0, 1), both_terms(0, -1)])
    far = np.stack([both_terms(-1), both_terms(1)])
    along = [two_terms(band(tap, X, 0, X).T) for tap in (gauss, slope, curve)]
    return near, far, np.concatenate([t[0] for t in along], 1), np.concatenate([t[1] for t in along], 1)


def split(values):
    high = values.astype(jnp.bfloat16)
    return high, (values - high.astype(jnp.float32)).astype(jnp.bfloat16)


def slot(dz, dt):
    return (dz + 1) * 3 + (dt + 1)


def filter_kernel(
    raw, faces_in, near_in, far_in, along_hi_in, along_lo_in, out, index,
    win, faces, partial, features, near, far, along_hi, along_lo, mixed_hi, mixed_lo, send, recv, local, stored,
):
    g, t = lax.axis_index("gz"), lax.axis_index("xy")
    odd = lax.rem(g, 2)
    mate = g + 1 - 2 * odd
    inner = (g == 1) | (g == 2)
    other = 3 - g
    has_left, has_right = t > 0, t < TILES - 1
    column = lax.rem(t, ROW)
    first_x, last_x = column == 0, column == ROW - 1
    second_x, third_x = column == 1, column == 2
    cross_left, cross_right = inner & first_x & has_left, inner & last_x & has_right

    loads = [
        pltpu.make_async_copy(source, target, local.at[k])
        for k, (source, target) in enumerate(
            (
                (raw, win.at[slot(0, 0)]),
                (faces_in.at[:, pl.ds(0, HALF)], faces.at[0]),
                (faces_in.at[:, pl.ds(HALF, HALF)], faces.at[1]),
                (near_in.at[odd], near),
                (far_in.at[odd], far),
                (along_hi_in, along_hi),
                (along_lo_in, along_lo),
            )
        )
    ]
    for load in loads:
        load.start()

    barrier = pltpu.get_barrier_semaphore()
    greeted = 0
    for condition, dg, dt in (
        (has_left, g, t - 1),
        (has_right, g, t + 1),
        (inner, other, t),
        (cross_left, other, t - 1),
        (cross_right, other, t + 1),
    ):
        @pl.when(condition)
        def _():
            pl.semaphore_signal(barrier, inc=1, device_id=(dg, dt), device_id_type=MESH)

        greeted += condition.astype(jnp.int32)
    pl.semaphore_signal(barrier, inc=1, device_id=(mate, t), device_id_type=MESH)
    pl.semaphore_wait(barrier, greeted + 1)

    def part(ref, q):
        return ref.at[pl.ds(q * PART, PART)]

    def copy(kind, q, source, target, dg, dt):
        return pltpu.make_async_remote_copy(
            src_ref=part(source, q),
            dst_ref=part(win.at[target], q),
            send_sem=send.at[kind, q],
            recv_sem=recv.at[kind, q],
            device_id=(dg, dt),
            device_id_type=MESH,
        )

    def copies(q):
        up = other - g

        def made(*args):
            return lambda: copy(*args)

        middle = inner & (second_x | third_x)
        left, right = win.at[slot(0, -1)], win.at[slot(0, 1)]
        third = win.at[slot(up, 0)]
        return (
            (made(0, q, raw, slot(0, -1), g, t + 1), has_right, has_left),
            (made(1, q, raw, slot(0, 1), g, t - 1), has_left, has_right),
            (made(2, q, raw, slot(g - mate, 0), mate, t), True, True),
            (made(3, q, raw, slot(g - other, 0), other, t), inner, inner),
            (made(4, q, left, slot(g - mate, -1), mate, t), has_left, has_left),
            (made(5, q, right, slot(g - mate, 1), mate, t), has_right, has_right),
            (made(6, q, third, slot(up, -1), g, t + 1), middle, inner & (third_x | last_x)),
            (made(7, q, third, slot(up, 1), g, t - 1), middle, inner & (first_x | second_x)),
            (made(8, q, raw, slot(g - other, -1), other, t + 1), cross_right, cross_left),
            (made(9, q, raw, slot(g - other, 1), other, t - 1), cross_left, cross_right),
            (made(10, q, left, slot(g - other, -1), other, t), inner & second_x, inner & second_x),
            (made(11, q, right, slot(g - other, 1), other, t), inner & third_x, inner & third_x),
        )

    def start(q, kinds):
        for made, sent, _ in [copies(q)[k] for k in kinds]:
            pl.when(sent)(lambda made=made: made().start())

    def arrived(q, kinds, where=True):
        for made, _, received in [copies(q)[k] for k in kinds]:
            pl.when(received & where)(lambda made=made: made().wait_recv())

    def first(q, carry):
        start(q, (3, 0, 1, 8, 9, 2))
        return carry

    lax.fori_loop(0, PARTS, first, 0)

    def clear(target):
        def one(c, carry):
            win[target, c] = jnp.zeros((ZY, X), jnp.float32)
            return carry

        lax.fori_loop(0, C, one, 0)

    for d in (0, mate - g):
        pl.when(t == 0)(lambda d=d: clear(slot(d, -1)))
        pl.when(t == TILES - 1)(lambda d=d: clear(slot(d, 1)))
    pl.when(inner & (t == 0))(lambda: clear(slot(other - g, -1)))
    pl.when(inner & (t == TILES - 1))(lambda: clear(slot(other - g, 1)))
    for load in loads:
        load.wait()
    for half in range(2):
        for k in range(2):
            found = faces[half, pl.ds(k, ZY // 2, stride=2), :]
            index[half, :, k * HALF : (k + 1) * HALF] = jnp.where(found < 0, TOUCH * EB, found) * 2

    def dot(a, b):
        return jnp.dot(a, b, preferred_element_type=jnp.float32)

    def across(weights, blocks, c):
        high, low = split(jnp.concatenate([win[block, c] for block in blocks], axis=0))
        both = dot(weights[...], high)
        return both[: 4 * ZY] + both[4 * ZY :] + dot(weights[: 4 * ZY], low)

    def forward(q):
        arrived(q, (0, 1))
        start(q, (4, 5, 10, 11))
        arrived(q, (3,), second_x | third_x)
        start(q, (6, 7))

    def begin(q):
        arrived(q, (2, 4, 5))
        for j in range(PART):
            c = q * PART + j
            partial[c] = across(near, [slot(d, dt) for d in (0, mate - g) for dt in (-1, 0, 1)], c)

    rows = PART * ZY

    def store(half):
        return pltpu.make_async_copy(features.at[half], out.at[half], stored.at[half])

    def add_third(q):
        arrived(q, (3,), first_x | last_x)
        arrived(q, (6, 7, 8, 9, 10, 11))
        for j in range(PART):
            c = q * PART + j
            partial[c] += across(far, [slot(other - g, dt) for dt in (-1, 0, 1)], c)

    def end(q):
        for j in range(PART):
            high, low = split(partial[q * PART + j])
            for k in range(4):
                mixed_hi[k, j * ZY : (j + 1) * ZY, :] = high[k * ZY : (k + 1) * ZY]
                mixed_lo[k, j * ZY : (j + 1) * ZY, :] = low[k * ZY : (k + 1) * ZY]
        high, low = mixed_hi[...].reshape(4 * rows, X), mixed_lo[...].reshape(4 * rows, X)

        def along(n, k):
            columns = slice(k * X, (k + 1) * X)
            return (
                dot(high[:n], along_hi[:, columns])
                + dot(low[:n], along_hi[:, columns])
                + dot(high[:n], along_lo[:, columns])
            )

        by_gauss, by_slope, by_curve = along(4 * rows, 0), along(2 * rows, 1), along(rows, 2)
        smooth, grad_y, hess_yy, grad_z = (by_gauss[k * rows : (k + 1) * rows] for k in range(4))
        grad_x, hess_xy = by_slope[:rows], by_slope[rows:]
        half_trace = (hess_yy + by_curve) * 0.5
        spread = (hess_yy - by_curve) * 0.5
        deviation = jnp.sqrt(spread * spread + hess_xy * hess_xy)
        magnitude = jnp.sqrt(grad_z * grad_z + grad_y * grad_y + grad_x * grad_x)
        for k, value in enumerate((smooth, magnitude, half_trace + deviation, half_trace - deviation)):
            for j in range(PART):
                at = pl.ds((k * C + q * PART + j) * STEP, ZY)
                features[0, at, :] = value[j * ZY : (j + 1) * ZY, :HALF]
                features[1, at, :] = value[j * ZY : (j + 1) * ZY, HALF:]

    forward(0)

    def near_work(q, carry):
        pl.when(q < PARTS)(lambda: forward(q))
        begin(q - 1)
        pl.when(~inner)(lambda: end(q - 1))
        return carry

    lax.fori_loop(1, PARTS + 1, near_work, 0)

    @pl.when(inner)
    def _():
        def far_work(q, carry):
            add_third(q)
            end(q)
            return carry

        lax.fori_loop(0, PARTS, far_work, 0)

    for half in range(2):
        store(half).start()

    def finish(q, carry):
        for made, sent, _ in copies(q):
            pl.when(sent)(lambda made=made: made().wait_send())
        return carry

    lax.fori_loop(0, PARTS, finish, 0)
    for half in range(2):
        store(half).wait()


def filtered(raw, faces):
    near, far, along_hi, along_lo = tables()
    hbm = pl.BlockSpec(memory_space=pltpu.HBM)
    return pl.pallas_call(
        filter_kernel,
        out_shape=(
            jax.ShapeDtypeStruct((2, FEATURES * STEP, HALF), jnp.float32),
            jax.ShapeDtypeStruct((2, ZY // 2, X), jnp.int32),
        ),
        in_specs=[hbm] * 6,
        out_specs=(hbm, pl.BlockSpec(memory_space=pltpu.VMEM)),
        scratch_shapes=[
            pltpu.VMEM((9, C, ZY, X), jnp.float32),
            pltpu.VMEM((2, ZY, HALF), jnp.int32),
            pltpu.VMEM((C, 4 * ZY, X), jnp.float32),
            pltpu.VMEM((2, FEATURES * STEP, HALF), jnp.float32),
            pltpu.VMEM(near.shape[1:], jnp.bfloat16),
            pltpu.VMEM(far.shape[1:], jnp.bfloat16),
            pltpu.VMEM(along_hi.shape, jnp.bfloat16),
            pltpu.VMEM(along_lo.shape, jnp.bfloat16),
            pltpu.VMEM((4, PART * ZY, X), jnp.bfloat16),
            pltpu.VMEM((4, PART * ZY, X), jnp.bfloat16),
            pltpu.SemaphoreType.DMA((12, PARTS)),
            pltpu.SemaphoreType.DMA((12, PARTS)),
            pltpu.SemaphoreType.DMA((7,)),
            pltpu.SemaphoreType.DMA((2,)),
        ],
        compiler_params=pltpu.CompilerParams(
            collective_id=0, has_side_effects=True, vmem_limit_bytes=VMEM_BYTES
        ),
    )(raw, faces, *(jnp.asarray(table) for table in (near, far, along_hi, along_lo)))


def pool_kernel(
    features_in, index_in, touched_in, owner_in, out,
    features, index, touched, owner, row_a, row_b, merged, local, ahead, *rest,
):
    accs, targets = rest[:ACCS], rest[ACCS:]
    loads = [
        pltpu.make_async_copy(source, target, local.at[k])
        for k, (source, target) in enumerate(
            (
                (index_in, index),
                (features_in.at[0], features.at[pl.ds(0, FEATURES * STEP)]),
                (features_in.at[1], features.at[pl.ds(FEATURES * STEP, FEATURES * STEP)]),
                (touched_in, touched),
                (owner_in, owner),
            )
        )
    ]
    for load in loads:
        load.start()

    def summed(rows):
        sub = lax.broadcasted_iota(jnp.int32, (rows, HALF), 0)
        lane = lax.broadcasted_iota(jnp.int32, (rows, HALF), 1)
        return (lax.rem(sub, 2) == 1) | (lane >= 2 * FEATURES)

    pair, tile = summed(2), summed(16)
    start = jnp.where(tile, 0.0, FAR)

    def reset(i, carry):
        for acc in accs:
            acc[pl.ds(i * 16, 16), :] = start
        return carry

    def fetch(k, row):
        return pltpu.make_async_copy(index.at[row], targets[k], ahead.at[k])

    loads[0].wait()
    for k in range(AHEAD):
        fetch(k, k).start()
    lax.fori_loop(0, ROWS // 16, reset, 0)
    ones = jnp.ones((1, HALF), jnp.float32)

    def turn(n, row):
        at = n + lax.div(n, ZY) * (FEATURES * STEP - ZY)
        values = features[pl.ds(at, FEATURES, stride=STEP), :]
        row[...] = jnp.concatenate([values, -values, values[:31], ones], axis=0).T

    def collect(target, first, row):
        for v in range(HALF):
            acc = accs[v % ACCS]
            at = pl.ds(target[first + v], 2)
            value = jnp.broadcast_to(row[v : v + 1, :], (2, HALF))
            old = acc[at, :]
            acc[at, :] = jnp.where(pair, old + value, jnp.maximum(old, value))

    loads[1].wait()
    turn(0, row_a)

    def body(i, carry):
        pl.when(i == ZY // (2 * AHEAD) - 1)(lambda: loads[2].wait())
        for k in range(AHEAD):
            n = i * AHEAD + k
            fetch(k, n).wait()
            turn(2 * n + 1, row_b)
            collect(targets[k], 0, row_a)
            turn(jnp.minimum(2 * n + 2, 2 * ZY - 1), row_a)
            collect(targets[k], HALF, row_b)
            pl.when(n + AHEAD < ZY)(lambda: fetch(k, n + AHEAD).start())
        return carry

    lax.fori_loop(0, ZY // AHEAD, body, 0)
    loads[3].wait()
    loads[4].wait()

    lane = lax.broadcasted_iota(jnp.int32, (EB, HALF), 1)
    empty = jnp.where(lane >= 2 * FEATURES, 0.0, FAR)

    def fill(b, carry):
        out[b, :EB, :] = empty
        out[b, EB:, :] = jnp.zeros((SENT - EB, HALF), jnp.float32)
        return carry

    lax.fori_loop(0, BLOCKS, fill, 0)
    lane = lax.broadcasted_iota(jnp.int32, (EB // 4, HALF), 1)

    def place(i, carry):
        for k in range(2 * EB // 16):
            rows = pl.ds(pl.multiple_of(i * 2 * EB + k * 16, 16), 16)
            total = accs[0][rows, :]
            for acc in accs[1:]:
                more = acc[rows, :]
                total = jnp.where(tile, total + more, jnp.maximum(total, more))
            merged[pl.ds(k * 16, 16), :] = total
        to = owner[touched[i]]
        out[to, :EB, :] = merged[pl.ds(0, EB, stride=2), :]
        sums = merged[pl.ds(1, EB, stride=2), :]
        packed = jnp.zeros((EB // 4, HALF), jnp.float32)
        for j in range(4):
            group = pltpu.roll(sums[j * 16 : (j + 1) * 16], (32 * j - 16) % HALF, 1)
            packed = jnp.where((lane >= 32 * j) & (lane < 32 * j + 32), group, packed)
        out[to, EB:, :] = packed
        return carry

    lax.fori_loop(0, TOUCH, place, 0)


def pooled(features, index, touched, owner):
    hbm = pl.BlockSpec(memory_space=pltpu.HBM)
    return pl.pallas_call(
        pool_kernel,
        out_shape=jax.ShapeDtypeStruct((BLOCKS, SENT, HALF), jnp.float32),
        in_specs=[hbm] * 4,
        out_specs=pl.BlockSpec(memory_space=pltpu.VMEM),
        scratch_shapes=[
            pltpu.VMEM((2 * FEATURES * STEP, HALF), jnp.float32),
            pltpu.VMEM((ZY, X), jnp.int32),
            pltpu.SMEM((TOUCH,), jnp.int32),
            pltpu.SMEM((BLOCKS,), jnp.int32),
        ]
        + [pltpu.VMEM((HALF, HALF), jnp.float32)] * 3
        + [pltpu.SemaphoreType.DMA((5,)), pltpu.SemaphoreType.DMA((AHEAD,))]
        + [pltpu.VMEM((ROWS, HALF), jnp.float32)] * ACCS
        + [pltpu.SMEM((X,), jnp.int32)] * AHEAD,
        compiler_params=pltpu.CompilerParams(vmem_limit_bytes=VMEM_BYTES),
    )(features, index, touched, owner)


def merge_kernel(mine, out, got, send, recv):
    g, t = lax.axis_index("gz"), lax.axis_index("xy")
    barrier = pltpu.get_barrier_semaphore()

    def peer(k):
        return lax.rem(t + k, TILES)

    def greet(k, carry):
        pl.semaphore_signal(barrier, inc=1, device_id=(g, peer(k)), device_id_type=MESH)
        return carry

    lax.fori_loop(1, TILES, greet, 0)
    pl.semaphore_wait(barrier, TILES - 1)

    def copy(k):
        return pltpu.make_async_remote_copy(
            src_ref=mine.at[peer(k)],
            dst_ref=got.at[k],
            send_sem=send.at[k],
            recv_sem=recv.at[k],
            device_id=(g, peer(k)),
            device_id_type=MESH,
        )

    def start(k, carry):
        copy(k).start()
        return carry

    lax.fori_loop(1, TILES, start, 0)
    lane = lax.broadcasted_iota(jnp.int32, (SENT, HALF), 1)
    row = lax.broadcasted_iota(jnp.int32, (SENT, HALF), 0)
    summed = (lane >= 2 * FEATURES) | (row >= EB)

    def join(k, total):
        copy(k).wait_recv()
        more = got[k]
        return jnp.where(summed, total + more, jnp.maximum(total, more))

    total = lax.fori_loop(1, TILES, join, mine[t])
    extremes, packed = total[:EB], total[EB:]
    rest = jnp.concatenate([pltpu.roll(packed, (HALF + 16 - 32 * j) % HALF, 1) for j in range(4)], axis=0)
    count = extremes[:, HALF - 1 :]
    present = count > 0.0
    lane = lax.broadcasted_iota(jnp.int32, (EB, HALF), 1)
    means = jnp.where(lane < 31, pltpu.roll(extremes, HALF - 2 * FEATURES, 1), rest) / jnp.maximum(count, 1.0)
    signed = jnp.where(present, jnp.where(lane < FEATURES, extremes, -extremes), 0.0)
    shifted = pltpu.roll(signed, FEATURES, 1)
    out[:, :HALF] = jnp.where(lane < FEATURES, means, shifted)
    out[:, HALF:] = shifted[:, : 3 * FEATURES - HALF]

    def finish(k, carry):
        copy(k).wait_send()
        return carry

    lax.fori_loop(1, TILES, finish, 0)


def merged_stats(stats):
    vmem = pl.BlockSpec(memory_space=pltpu.VMEM)
    return pl.pallas_call(
        merge_kernel,
        out_shape=jax.ShapeDtypeStruct((EB, 3 * FEATURES), jnp.float32),
        in_specs=[vmem],
        out_specs=vmem,
        scratch_shapes=[
            pltpu.VMEM((TILES, SENT, HALF), jnp.float32),
            pltpu.SemaphoreType.DMA((TILES,)),
            pltpu.SemaphoreType.DMA((TILES,)),
        ],
        compiler_params=pltpu.CompilerParams(
            collective_id=1, has_side_effects=True, vmem_limit_bytes=VMEM_BYTES
        ),
    )(stats)


def per_device(raw_volume, face_slot, touched, block_owner):
    features, index = filtered(raw_volume.reshape(C, ZY, X), face_slot.reshape(ZY, X))
    stats = pooled(features, index.reshape(ZY, X), touched.reshape(-1), block_owner.reshape(-1))
    return merged_stats(stats).T[None, None]


def solution(mesh):
    placed = (P(None, "gz", "xy", None), P("gz", "xy", None), P("gz", "xy", None), P("gz", None))
    return jax.shard_map(
        per_device, mesh=mesh, in_specs=placed, out_specs=P("gz", "xy", None, None), check_vma=False
    )
```

```python
import functools

import jax
import jax.numpy as jnp
import ml_dtypes
import numpy as np
from jax import lax
from jax.experimental import pallas as pl
from jax.experimental.pallas import tpu as pltpu
from jax.sharding import PartitionSpec as P

RADIUS = 8
C = 12
Z = 8
Y = 8
X = 256
EB = 64
TOUCH = 16
BLOCKS = 32
TILES = 32
SLABS = 4
ZY = Z * Y
HALF = X // 2
FEATURES = 4 * C
PARTS = 6
PART = C // PARTS
ACCS = 8
ROW = 4
ROWS = 2 * (TOUCH * EB) + 16
SENT = EB + EB // 4
PIECE = SENT // 2
GROUP = 8
FAR = -1e30
STEP = ZY + 1
AHEAD = 4
VMEM_BYTES = 62 * 2**20
MESH = pl.DeviceIdType.MESH


def taps():
    sigma = np.float32(RADIUS / 3.0)
    offsets = np.arange(-RADIUS, RADIUS + 1).astype(np.float32)
    gauss = np.exp(-offsets * offsets / (2.0 * sigma * sigma)).astype(np.float32)
    gauss = gauss / gauss.sum()
    slope = -(offsets / sigma) * gauss
    curve = (offsets * offsets / (sigma * sigma) - 1.0) * gauss
    return [tap.astype(np.float64) for tap in (gauss, slope, curve)]


def two_terms(table):
    table = table.astype(np.float32)
    high = table.astype(ml_dtypes.bfloat16)
    low = (table - high.astype(np.float32)).astype(ml_dtypes.bfloat16)
    return high, low


def band(tap, size, start, stop):
    offset = np.arange(start, stop)[None, :] - np.arange(size)[:, None]
    return np.where(np.abs(offset) <= RADIUS, tap[np.clip(offset + RADIUS, 0, 2 * RADIUS)], 0.0)


def tables():
    gauss, slope, curve = taps()
    rows = []
    for kz, ky in ((gauss, gauss), (gauss, slope), (gauss, curve), (slope, gauss)):
        bz = band(kz, Z, -Z, 2 * Z).reshape(Z, 3, Z)
        by = band(ky, Y, -Y, 2 * Y).reshape(Y, 3, Y)
        rows.append(np.einsum("pdz,qey->pqdezy", bz, by).reshape(ZY, 9 * ZY))
    weights = np.concatenate(rows, axis=0).reshape(4 * ZY, 3, 3 * ZY)

    def both_terms(*blocks):
        return np.concatenate(two_terms(np.concatenate([weights[:, d + 1] for d in blocks], axis=1)), axis=0)

    near = np.stack([both_terms(0, 1), both_terms(0, -1)])
    far = np.stack([both_terms(-1), both_terms(1)])
    along = [two_terms(band(tap, X, 0, X).T) for tap in (gauss, slope, curve)]
    return near, far, np.concatenate([t[0] for t in along], 1), np.concatenate([t[1] for t in along], 1)


def split(values):
    high = values.astype(jnp.bfloat16)
    return high, (values - high.astype(jnp.float32)).astype(jnp.bfloat16)


def slot(dz, dt):
    return (dz + 1) * 3 + (dt + 1)


def filter_kernel(
    raw, faces_in, near_in, far_in, along_hi_in, along_lo_in, out, index,
    win, faces, partial, features, near, far, along_hi, along_lo, mixed_hi, mixed_lo, send, recv, local, stored,
):
    g, t = lax.axis_index("gz"), lax.axis_index("xy")
    odd = lax.rem(g, 2)
    mate = g + 1 - 2 * odd
    inner = (g == 1) | (g == 2)
    other = 3 - g
    has_left, has_right = t > 0, t < TILES - 1
    column = lax.rem(t, ROW)
    first_x, last_x = column == 0, column == ROW - 1
    second_x, third_x = column == 1, column == 2
    cross_left, cross_right = inner & first_x & has_left, inner & last_x & has_right

    loads = [
        pltpu.make_async_copy(source, target, local.at[k])
        for k, (source, target) in enumerate(
            (
                (raw, win.at[slot(0, 0)]),
                (faces_in.at[:, pl.ds(0, HALF)], faces.at[0]),
                (faces_in.at[:, pl.ds(HALF, HALF)], faces.at[1]),
                (near_in.at[odd], near),
                (far_in.at[odd], far),
                (along_hi_in, along_hi),
                (along_lo_in, along_lo),
            )
        )
    ]
    for load in loads:
        load.start()

    barrier = pltpu.get_barrier_semaphore()
    greeted = 0
    for condition, dg, dt in (
        (has_left, g, t - 1),
        (has_right, g, t + 1),
        (inner, other, t),
        (cross_left, other, t - 1),
        (cross_right, other, t + 1),
    ):
        @pl.when(condition)
        def _():
            pl.semaphore_signal(barrier, inc=1, device_id=(dg, dt), device_id_type=MESH)

        greeted += condition.astype(jnp.int32)
    pl.semaphore_signal(barrier, inc=1, device_id=(mate, t), device_id_type=MESH)
    pl.semaphore_wait(barrier, greeted + 1)

    def part(ref, q):
        return ref.at[pl.ds(q * PART, PART)]

    def copy(kind, q, source, target, dg, dt):
        return pltpu.make_async_remote_copy(
            src_ref=part(source, q),
            dst_ref=part(win.at[target], q),
            send_sem=send.at[kind, q],
            recv_sem=recv.at[kind, q],
            device_id=(dg, dt),
            device_id_type=MESH,
        )

    def copies(q):
        up = other - g

        def made(*args):
            return lambda: copy(*args)

        middle = inner & (second_x | third_x)
        left, right = win.at[slot(0, -1)], win.at[slot(0, 1)]
        third = win.at[slot(up, 0)]
        return (
            (made(0, q, raw, slot(0, -1), g, t + 1), has_right, has_left),
            (made(1, q, raw, slot(0, 1), g, t - 1), has_left, has_right),
            (made(2, q, raw, slot(g - mate, 0), mate, t), True, True),
            (made(3, q, raw, slot(g - other, 0), other, t), inner, inner),
            (made(4, q, left, slot(g - mate, -1), mate, t), has_left, has_left),
            (made(5, q, right, slot(g - mate, 1), mate, t), has_right, has_right),
            (made(6, q, third, slot(up, -1), g, t + 1), middle, inner & (third_x | last_x)),
            (made(7, q, third, slot(up, 1), g, t - 1), middle, inner & (first_x | second_x)),
            (made(8, q, raw, slot(g - other, -1), other, t + 1), cross_right, cross_left),
            (made(9, q, raw, slot(g - other, 1), other, t - 1), cross_left, cross_right),
            (made(10, q, left, slot(g - other, -1), other, t), inner & second_x, inner & second_x),
            (made(11, q, right, slot(g - other, 1), other, t), inner & third_x, inner & third_x),
        )

    def start(q, kinds):
        for made, sent, _ in [copies(q)[k] for k in kinds]:
            pl.when(sent)(lambda made=made: made().start())

    def arrived(q, kinds, where=True):
        for made, _, received in [copies(q)[k] for k in kinds]:
            pl.when(received & where)(lambda made=made: made().wait_recv())

    def first(q, carry):
        start(q, (3, 0, 1, 8, 9, 2))
        return carry

    lax.fori_loop(0, PARTS, first, 0)

    def clear(target):
        def one(c, carry):
            win[target, c] = jnp.zeros((ZY, X), jnp.float32)
            return carry

        lax.fori_loop(0, C, one, 0)

    for d in (0, mate - g):
        pl.when(t == 0)(lambda d=d: clear(slot(d, -1)))
        pl.when(t == TILES - 1)(lambda d=d: clear(slot(d, 1)))
    pl.when(inner & (t == 0))(lambda: clear(slot(other - g, -1)))
    pl.when(inner & (t == TILES - 1))(lambda: clear(slot(other - g, 1)))
    for load in loads:
        load.wait()
    for half in range(2):
        for k in range(2):
            found = faces[half, pl.ds(k, ZY // 2, stride=2), :]
            index[half, :, k * HALF : (k + 1) * HALF] = jnp.where(found < 0, TOUCH * EB, found) * 2

    def dot(a, b):
        return jnp.dot(a, b, preferred_element_type=jnp.float32)

    def across(weights, blocks, c):
        high, low = split(jnp.concatenate([win[block, c] for block in blocks], axis=0))
        both = dot(weights[...], high)
        return both[: 4 * ZY] + both[4 * ZY :] + dot(weights[: 4 * ZY], low)

    def forward(q):
        arrived(q, (0, 1))
        start(q, (4, 5, 10, 11))
        arrived(q, (3,), second_x | third_x)
        start(q, (6, 7))

    def begin(q):
        arrived(q, (2, 4, 5))
        for j in range(PART):
            c = q * PART + j
            partial[c] = across(near, [slot(d, dt) for d in (0, mate - g) for dt in (-1, 0, 1)], c)

    rows = PART * ZY

    def store(half):
        return pltpu.make_async_copy(features.at[half], out.at[half], stored.at[half])

    def add_third(q):
        arrived(q, (3,), first_x | last_x)
        arrived(q, (6, 7, 8, 9, 10, 11))
        for j in range(PART):
            c = q * PART + j
            partial[c] += across(far, [slot(other - g, dt) for dt in (-1, 0, 1)], c)

    def end(q):
        for j in range(PART):
            high, low = split(partial[q * PART + j])
            for k in range(4):
                mixed_hi[k, j * ZY : (j + 1) * ZY, :] = high[k * ZY : (k + 1) * ZY]
                mixed_lo[k, j * ZY : (j + 1) * ZY, :] = low[k * ZY : (k + 1) * ZY]
        high, low = mixed_hi[...].reshape(4 * rows, X), mixed_lo[...].reshape(4 * rows, X)

        def along(n, k):
            columns = slice(k * X, (k + 1) * X)
            return (
                dot(high[:n], along_hi[:, columns])
                + dot(low[:n], along_hi[:, columns])
                + dot(high[:n], along_lo[:, columns])
            )

        by_gauss, by_slope, by_curve = along(4 * rows, 0), along(2 * rows, 1), along(rows, 2)
        smooth, grad_y, hess_yy, grad_z = (by_gauss[k * rows : (k + 1) * rows] for k in range(4))
        grad_x, hess_xy = by_slope[:rows], by_slope[rows:]
        half_trace = (hess_yy + by_curve) * 0.5
        spread = (hess_yy - by_curve) * 0.5
        deviation = jnp.sqrt(spread * spread + hess_xy * hess_xy)
        magnitude = jnp.sqrt(grad_z * grad_z + grad_y * grad_y + grad_x * grad_x)
        for k, value in enumerate((smooth, magnitude, half_trace + deviation, half_trace - deviation)):
            for j in range(PART):
                at = pl.ds((k * C + q * PART + j) * STEP, ZY)
                features[0, at, :] = value[j * ZY : (j + 1) * ZY, :HALF]
                features[1, at, :] = value[j * ZY : (j + 1) * ZY, HALF:]

    forward(0)

    def near_work(q, carry):
        pl.when(q < PARTS)(lambda: forward(q))
        begin(q - 1)
        pl.when(~inner)(lambda: end(q - 1))
        return carry

    lax.fori_loop(1, PARTS + 1, near_work, 0)

    @pl.when(inner)
    def _():
        def far_work(q, carry):
            add_third(q)
            end(q)
            return carry

        lax.fori_loop(0, PARTS, far_work, 0)

    for half in range(2):
        store(half).start()

    def finish(q, carry):
        for made, sent, _ in copies(q):
            pl.when(sent)(lambda made=made: made().wait_send())
        return carry

    lax.fori_loop(0, PARTS, finish, 0)
    for half in range(2):
        store(half).wait()


def filtered(raw, faces):
    near, far, along_hi, along_lo = tables()
    hbm = pl.BlockSpec(memory_space=pltpu.HBM)
    return pl.pallas_call(
        filter_kernel,
        out_shape=(
            jax.ShapeDtypeStruct((2, FEATURES * STEP, HALF), jnp.float32),
            jax.ShapeDtypeStruct((2, ZY // 2, X), jnp.int32),
        ),
        in_specs=[hbm] * 6,
        out_specs=(hbm, pl.BlockSpec(memory_space=pltpu.VMEM)),
        scratch_shapes=[
            pltpu.VMEM((9, C, ZY, X), jnp.float32),
            pltpu.VMEM((2, ZY, HALF), jnp.int32),
            pltpu.VMEM((C, 4 * ZY, X), jnp.float32),
            pltpu.VMEM((2, FEATURES * STEP, HALF), jnp.float32),
            pltpu.VMEM(near.shape[1:], jnp.bfloat16),
            pltpu.VMEM(far.shape[1:], jnp.bfloat16),
            pltpu.VMEM(along_hi.shape, jnp.bfloat16),
            pltpu.VMEM(along_lo.shape, jnp.bfloat16),
            pltpu.VMEM((4, PART * ZY, X), jnp.bfloat16),
            pltpu.VMEM((4, PART * ZY, X), jnp.bfloat16),
            pltpu.SemaphoreType.DMA((12, PARTS)),
            pltpu.SemaphoreType.DMA((12, PARTS)),
            pltpu.SemaphoreType.DMA((7,)),
            pltpu.SemaphoreType.DMA((2,)),
        ],
        compiler_params=pltpu.CompilerParams(
            collective_id=0, has_side_effects=True, vmem_limit_bytes=VMEM_BYTES
        ),
    )(raw, faces, *(jnp.asarray(table) for table in (near, far, along_hi, along_lo)))


def pool_kernel(
    features_in, index_in, touched_in, owner_in, upper, lower,
    features, index, touched, owner, row_a, row_b, merged, local, ahead, *rest,
):
    accs, targets = rest[:ACCS], rest[ACCS:]
    loads = [
        pltpu.make_async_copy(source, target, local.at[k])
        for k, (source, target) in enumerate(
            (
                (index_in, index),
                (features_in.at[0], features.at[pl.ds(0, FEATURES * STEP)]),
                (features_in.at[1], features.at[pl.ds(FEATURES * STEP, FEATURES * STEP)]),
                (touched_in, touched),
                (owner_in, owner),
            )
        )
    ]
    for load in loads:
        load.start()

    def summed(rows):
        sub = lax.broadcasted_iota(jnp.int32, (rows, HALF), 0)
        lane = lax.broadcasted_iota(jnp.int32, (rows, HALF), 1)
        return (lax.rem(sub, 2) == 1) | (lane >= 2 * FEATURES)

    pair, tile = summed(2), summed(16)
    start = jnp.where(tile, 0.0, FAR)

    def reset(i, carry):
        for acc in accs:
            acc[pl.ds(i * 16, 16), :] = start
        return carry

    def fetch(k, row):
        return pltpu.make_async_copy(index.at[row], targets[k], ahead.at[k])

    loads[0].wait()
    for k in range(AHEAD):
        fetch(k, k).start()
    lax.fori_loop(0, ROWS // 16, reset, 0)
    ones = jnp.ones((1, HALF), jnp.float32)

    def turn(n, row):
        at = n + lax.div(n, ZY) * (FEATURES * STEP - ZY)
        values = features[pl.ds(at, FEATURES, stride=STEP), :]
        row[...] = jnp.concatenate([values, -values, values[:31], ones], axis=0).T

    def collect(target, first, row):
        for v in range(HALF):
            acc = accs[v % ACCS]
            at = pl.ds(target[first + v], 2)
            value = jnp.broadcast_to(row[v : v + 1, :], (2, HALF))
            old = acc[at, :]
            acc[at, :] = jnp.where(pair, old + value, jnp.maximum(old, value))

    loads[1].wait()
    turn(0, row_a)

    def body(i, carry):
        pl.when(i == ZY // (2 * AHEAD) - 1)(lambda: loads[2].wait())
        for k in range(AHEAD):
            n = i * AHEAD + k
            fetch(k, n).wait()
            turn(2 * n + 1, row_b)
            collect(targets[k], 0, row_a)
            turn(jnp.minimum(2 * n + 2, 2 * ZY - 1), row_a)
            collect(targets[k], HALF, row_b)
            pl.when(n + AHEAD < ZY)(lambda: fetch(k, n + AHEAD).start())
        return carry

    lax.fori_loop(0, ZY // AHEAD, body, 0)
    loads[3].wait()
    loads[4].wait()

    lane = lax.broadcasted_iota(jnp.int32, (EB, HALF), 1)
    empty = jnp.where(lane >= 2 * FEATURES, 0.0, FAR)

    def fill(b, carry):
        upper[b] = empty[:PIECE]
        lower[b, : EB - PIECE, :] = empty[PIECE:]
        lower[b, EB - PIECE :, :] = jnp.zeros((SENT - EB, HALF), jnp.float32)
        return carry

    lax.fori_loop(0, BLOCKS, fill, 0)
    lane = lax.broadcasted_iota(jnp.int32, (EB // 4, HALF), 1)

    def place(i, carry):
        for k in range(2 * EB // 16):
            rows = pl.ds(pl.multiple_of(i * 2 * EB + k * 16, 16), 16)
            total = accs[0][rows, :]
            for acc in accs[1:]:
                more = acc[rows, :]
                total = jnp.where(tile, total + more, jnp.maximum(total, more))
            merged[pl.ds(k * 16, 16), :] = total
        to = owner[touched[i]]
        tile_x, tile_yz = lax.rem(to, ROW), lax.div(to, ROW)
        extremes = merged[pl.ds(0, EB, stride=2), :]
        upper[tile_x * GROUP + tile_yz] = extremes[:PIECE]
        lower[to, : EB - PIECE, :] = extremes[PIECE:]
        sums = merged[pl.ds(1, EB, stride=2), :]
        packed = jnp.zeros((EB // 4, HALF), jnp.float32)
        for j in range(4):
            group = pltpu.roll(sums[j * 16 : (j + 1) * 16], (32 * j - 16) % HALF, 1)
            packed = jnp.where((lane >= 32 * j) & (lane < 32 * j + 32), group, packed)
        lower[to, EB - PIECE :, :] = packed
        return carry

    lax.fori_loop(0, TOUCH, place, 0)


def pooled(features, index, touched, owner):
    hbm = pl.BlockSpec(memory_space=pltpu.HBM)
    return pl.pallas_call(
        pool_kernel,
        out_shape=[jax.ShapeDtypeStruct((BLOCKS, PIECE, HALF), jnp.float32)] * 2,
        in_specs=[hbm] * 4,
        out_specs=[pl.BlockSpec(memory_space=pltpu.VMEM)] * 2,
        scratch_shapes=[
            pltpu.VMEM((2 * FEATURES * STEP, HALF), jnp.float32),
            pltpu.VMEM((ZY, X), jnp.int32),
            pltpu.SMEM((TOUCH,), jnp.int32),
            pltpu.SMEM((BLOCKS,), jnp.int32),
        ]
        + [pltpu.VMEM((HALF, HALF), jnp.float32)] * 3
        + [pltpu.SemaphoreType.DMA((5,)), pltpu.SemaphoreType.DMA((AHEAD,))]
        + [pltpu.VMEM((ROWS, HALF), jnp.float32)] * ACCS
        + [pltpu.SMEM((X,), jnp.int32)] * AHEAD,
        compiler_params=pltpu.CompilerParams(vmem_limit_bytes=VMEM_BYTES),
    )(features, index, touched, owner)


def merge_kernel(
    upper, lower, out, upper_sum, lower_sum, upper_got, lower_got, upper_last, lower_last, send, recv, local
):
    g, t = lax.axis_index("gz"), lax.axis_index("xy")
    x, yz = lax.rem(t, ROW), lax.div(t, ROW)
    z, y = lax.rem(yz, 2), lax.div(yz, 2)
    zx = lax.rem(t, GROUP)
    loads = [
        pltpu.make_async_copy(upper.at[pl.ds(x * GROUP, GROUP)], upper_sum, local.at[0]),
        pltpu.make_async_copy(lower.at[pl.ds(y * GROUP, GROUP)], lower_sum, local.at[1]),
    ]
    for load in loads:
        load.start()

    def along_x(k):
        return lax.rem(x + k, ROW)

    def along_y(k):
        return lax.rem(y + k, ROW)

    def along_yz(k):
        return lax.rem(yz + k, GROUP)

    def along_zx(k):
        return lax.rem(zx + k, GROUP)

    barrier = pltpu.get_barrier_semaphore()

    def greet(peer):
        pl.semaphore_signal(barrier, inc=1, device_id=(g, peer), device_id_type=MESH)

    for k in range(1, ROW):
        greet(yz * ROW + along_x(k))
        greet(along_y(k) * GROUP + zx)
    for k in range(ROW):
        greet(along_y(k) * GROUP + (1 - z) * ROW + x)
    for k in range(1, ROW):
        greet(y * GROUP + (1 - z) * ROW + along_x(k))
    pl.semaphore_wait(barrier, 3 * (ROW - 1) + ROW)

    def copy(source, target, at, peer):
        return pltpu.make_async_remote_copy(
            src_ref=source,
            dst_ref=target,
            send_sem=send.at[at],
            recv_sem=recv.at[at],
            device_id=(g, peer),
            device_id_type=MESH,
        )

    def first_upper(k):
        source = upper.at[pl.ds(along_x(k) * GROUP, GROUP)]
        return copy(source, upper_got.at[k - 1], k - 1, yz * ROW + along_x(k))

    def first_lower(k):
        source = lower.at[pl.ds(along_y(k) * GROUP, GROUP)]
        return copy(source, lower_got.at[k - 1], ROW + k - 2, along_y(k) * GROUP + zx)

    def last_upper(k):
        source = upper_sum.at[along_yz(k)]
        return copy(source, upper_last.at[k - 1], 2 * (ROW - 1) + k - 1, along_yz(k) * ROW + x)

    def last_lower(k):
        source = lower_sum.at[along_zx(k)]
        return copy(source, lower_last.at[k - 1], 2 * (ROW - 1) + GROUP + k - 2, y * GROUP + along_zx(k))

    lane = lax.broadcasted_iota(jnp.int32, (PIECE, HALF), 1)
    row = lax.broadcasted_iota(jnp.int32, (PIECE, HALF), 0)
    upper_adds = lane >= 2 * FEATURES
    lower_adds = upper_adds | (row >= EB - PIECE)

    def join(adds, left, right):
        return jnp.where(adds, left + right, jnp.maximum(left, right))

    order = (2, 1, 3)
    for k in order:
        first_upper(k).start()
        first_lower(k).start()
    for load in loads:
        load.wait()

    def stage(adds, first, got, summed, last):
        for k in order:
            first(k).wait_recv()

        def one(b, carry):
            total = summed[b]
            for k in range(ROW - 1):
                total = join(adds, total, got[k, b])
            summed[b] = total
            return carry

        lax.fori_loop(0, GROUP, one, 0)
        for k in range(1, GROUP):
            last(k).start()

    stage(upper_adds, first_upper, upper_got, upper_sum, last_upper)
    stage(lower_adds, first_lower, lower_got, lower_sum, last_lower)

    def gather(adds, total, got, last):
        for k in range(1, GROUP):
            last(k).wait_recv()
            total = join(adds, total, got[k - 1])
        return total

    total = jnp.concatenate(
        [
            gather(upper_adds, upper_sum[yz], upper_last, last_upper),
            gather(lower_adds, lower_sum[zx], lower_last, last_lower),
        ],
        axis=0,
    )
    extremes, packed = total[:EB], total[EB:]
    rest = jnp.concatenate([pltpu.roll(packed, (HALF + 16 - 32 * j) % HALF, 1) for j in range(4)], axis=0)
    count = extremes[:, HALF - 1 :]
    present = count > 0.0
    lane = lax.broadcasted_iota(jnp.int32, (EB, HALF), 1)
    means = jnp.where(lane < 31, pltpu.roll(extremes, HALF - 2 * FEATURES, 1), rest) / jnp.maximum(count, 1.0)
    signed = jnp.where(present, jnp.where(lane < FEATURES, extremes, -extremes), 0.0)
    shifted = pltpu.roll(signed, FEATURES, 1)
    out[:, :HALF] = jnp.where(lane < FEATURES, means, shifted)
    out[:, HALF:] = shifted[:, : 3 * FEATURES - HALF]

    for k in order:
        first_upper(k).wait_send()
        first_lower(k).wait_send()
    for k in range(1, GROUP):
        last_upper(k).wait_send()
        last_lower(k).wait_send()


def merged_stats(upper, lower):
    hbm = pl.BlockSpec(memory_space=pltpu.HBM)
    copies = 2 * (ROW - 1) + 2 * (GROUP - 1)
    return pl.pallas_call(
        merge_kernel,
        out_shape=jax.ShapeDtypeStruct((EB, 3 * FEATURES), jnp.float32),
        in_specs=[hbm] * 2,
        out_specs=pl.BlockSpec(memory_space=pltpu.VMEM),
        scratch_shapes=[pltpu.VMEM((GROUP, PIECE, HALF), jnp.float32)] * 2
        + [pltpu.VMEM((ROW - 1, GROUP, PIECE, HALF), jnp.float32)] * 2
        + [pltpu.VMEM((GROUP - 1, PIECE, HALF), jnp.float32)] * 2
        + [
            pltpu.SemaphoreType.DMA((copies,)),
            pltpu.SemaphoreType.DMA((copies,)),
            pltpu.SemaphoreType.DMA((2,)),
        ],
        compiler_params=pltpu.CompilerParams(
            collective_id=1, has_side_effects=True, vmem_limit_bytes=VMEM_BYTES
        ),
    )(upper, lower)


def per_device(raw_volume, face_slot, touched, block_owner):
    features, index = filtered(raw_volume.reshape(C, ZY, X), face_slot.reshape(ZY, X))
    upper, lower = pooled(features, index.reshape(ZY, X), touched.reshape(-1), block_owner.reshape(-1))
    return merged_stats(upper, lower).T[None, None]


def solution(mesh):
    placed = (P(None, "gz", "xy", None), P("gz", "xy", None), P("gz", "xy", None), P("gz", None))
    return jax.shard_map(
        per_device, mesh=mesh, in_specs=placed, out_specs=P("gz", "xy", None, None), check_vma=False
    )
```

```python
import functools

import jax
import jax.numpy as jnp
import ml_dtypes
import numpy as np
from jax import lax
from jax.experimental import pallas as pl
from jax.experimental.pallas import tpu as pltpu
from jax.sharding import PartitionSpec as P

RADIUS = 8
C = 12
Z = 8
Y = 8
X = 256
EB = 64
TOUCH = 16
BLOCKS = 32
TILES = 32
SLABS = 4
ZY = Z * Y
HALF = X // 2
FEATURES = 4 * C
PARTS = 6
PART = C // PARTS
ACCS = 8
ROW = 4
SPARE = 8
ROWS = 2 * (TOUCH * EB + SPARE)
SENT = EB + EB // 4
PIECE = SENT // 2
GROUP = 8
FAR = -1e30
STEP = ZY + 1
AHEAD = 4
VMEM_BYTES = 62 * 2**20
MESH = pl.DeviceIdType.MESH


def taps():
    sigma = np.float32(RADIUS / 3.0)
    offsets = np.arange(-RADIUS, RADIUS + 1).astype(np.float32)
    gauss = np.exp(-offsets * offsets / (2.0 * sigma * sigma)).astype(np.float32)
    gauss = gauss / gauss.sum()
    slope = -(offsets / sigma) * gauss
    curve = (offsets * offsets / (sigma * sigma) - 1.0) * gauss
    return [tap.astype(np.float64) for tap in (gauss, slope, curve)]


def two_terms(table):
    table = table.astype(np.float32)
    high = table.astype(ml_dtypes.bfloat16)
    low = (table - high.astype(np.float32)).astype(ml_dtypes.bfloat16)
    return high, low


def band(tap, size, start, stop):
    offset = np.arange(start, stop)[None, :] - np.arange(size)[:, None]
    return np.where(np.abs(offset) <= RADIUS, tap[np.clip(offset + RADIUS, 0, 2 * RADIUS)], 0.0)


def tables():
    gauss, slope, curve = taps()
    rows = []
    for kz, ky in ((gauss, gauss), (gauss, slope), (gauss, curve), (slope, gauss)):
        bz = band(kz, Z, -Z, 2 * Z).reshape(Z, 3, Z)
        by = band(ky, Y, -Y, 2 * Y).reshape(Y, 3, Y)
        rows.append(np.einsum("pdz,qey->pqdezy", bz, by).reshape(ZY, 9 * ZY))
    weights = np.concatenate(rows, axis=0).reshape(4 * ZY, 3, 3 * ZY)

    def both_terms(*blocks):
        return np.concatenate(two_terms(np.concatenate([weights[:, d + 1] for d in blocks], axis=1)), axis=0)

    near = np.stack([both_terms(0, 1), both_terms(0, -1)])
    far = np.stack([both_terms(-1), both_terms(1)])
    along = [two_terms(band(tap, X, 0, X).T) for tap in (gauss, slope, curve)]
    return near, far, np.concatenate([t[0] for t in along], 1), np.concatenate([t[1] for t in along], 1)


def split(values):
    high = values.astype(jnp.bfloat16)
    return high, (values - high.astype(jnp.float32)).astype(jnp.bfloat16)


def slot(dz, dt):
    return (dz + 1) * 3 + (dt + 1)


def filter_kernel(
    raw, faces_in, near_in, far_in, along_hi_in, along_lo_in, out, index,
    win, faces, partial, features, near, far, along_hi, along_lo, mixed_hi, mixed_lo, send, recv, local, stored,
):
    g, t = lax.axis_index("gz"), lax.axis_index("xy")
    odd = lax.rem(g, 2)
    mate = g + 1 - 2 * odd
    inner = (g == 1) | (g == 2)
    other = 3 - g
    has_left, has_right = t > 0, t < TILES - 1
    column = lax.rem(t, ROW)
    first_x, last_x = column == 0, column == ROW - 1
    second_x, third_x = column == 1, column == 2
    cross_left, cross_right = inner & first_x & has_left, inner & last_x & has_right

    loads = [
        pltpu.make_async_copy(source, target, local.at[k])
        for k, (source, target) in enumerate(
            (
                (raw, win.at[slot(0, 0)]),
                (faces_in.at[:, pl.ds(0, HALF)], faces.at[0]),
                (faces_in.at[:, pl.ds(HALF, HALF)], faces.at[1]),
                (near_in.at[odd], near),
                (far_in.at[odd], far),
                (along_hi_in, along_hi),
                (along_lo_in, along_lo),
            )
        )
    ]
    for load in loads:
        load.start()

    barrier = pltpu.get_barrier_semaphore()
    greeted = 0
    for condition, dg, dt in (
        (has_left, g, t - 1),
        (has_right, g, t + 1),
        (inner, other, t),
        (cross_left, other, t - 1),
        (cross_right, other, t + 1),
    ):
        @pl.when(condition)
        def _():
            pl.semaphore_signal(barrier, inc=1, device_id=(dg, dt), device_id_type=MESH)

        greeted += condition.astype(jnp.int32)
    pl.semaphore_signal(barrier, inc=1, device_id=(mate, t), device_id_type=MESH)
    pl.semaphore_wait(barrier, greeted + 1)

    def part(ref, q):
        return ref.at[pl.ds(q * PART, PART)]

    def copy(kind, q, source, target, dg, dt):
        return pltpu.make_async_remote_copy(
            src_ref=part(source, q),
            dst_ref=part(win.at[target], q),
            send_sem=send.at[kind, q],
            recv_sem=recv.at[kind, q],
            device_id=(dg, dt),
            device_id_type=MESH,
        )

    def copies(q):
        up = other - g

        def made(*args):
            return lambda: copy(*args)

        middle = inner & (second_x | third_x)
        left, right = win.at[slot(0, -1)], win.at[slot(0, 1)]
        third = win.at[slot(up, 0)]
        return (
            (made(0, q, raw, slot(0, -1), g, t + 1), has_right, has_left),
            (made(1, q, raw, slot(0, 1), g, t - 1), has_left, has_right),
            (made(2, q, raw, slot(g - mate, 0), mate, t), True, True),
            (made(3, q, raw, slot(g - other, 0), other, t), inner, inner),
            (made(4, q, left, slot(g - mate, -1), mate, t), has_left, has_left),
            (made(5, q, right, slot(g - mate, 1), mate, t), has_right, has_right),
            (made(6, q, third, slot(up, -1), g, t + 1), middle, inner & (third_x | last_x)),
            (made(7, q, third, slot(up, 1), g, t - 1), middle, inner & (first_x | second_x)),
            (made(8, q, raw, slot(g - other, -1), other, t + 1), cross_right, cross_left),
            (made(9, q, raw, slot(g - other, 1), other, t - 1), cross_left, cross_right),
            (made(10, q, left, slot(g - other, -1), other, t), inner & second_x, inner & second_x),
            (made(11, q, right, slot(g - other, 1), other, t), inner & third_x, inner & third_x),
        )

    def start(q, kinds):
        for made, sent, _ in [copies(q)[k] for k in kinds]:
            pl.when(sent)(lambda made=made: made().start())

    def arrived(q, kinds, where=True):
        for made, _, received in [copies(q)[k] for k in kinds]:
            pl.when(received & where)(lambda made=made: made().wait_recv())

    def first(q, carry):
        start(q, (3, 8, 9, 0, 1, 2))
        return carry

    lax.fori_loop(0, PARTS, first, 0)

    def clear(target):
        def one(c, carry):
            win[target, c] = jnp.zeros((ZY, X), jnp.float32)
            return carry

        lax.fori_loop(0, C, one, 0)

    for d in (0, mate - g):
        pl.when(t == 0)(lambda d=d: clear(slot(d, -1)))
        pl.when(t == TILES - 1)(lambda d=d: clear(slot(d, 1)))
    pl.when(inner & (t == 0))(lambda: clear(slot(other - g, -1)))
    pl.when(inner & (t == TILES - 1))(lambda: clear(slot(other - g, 1)))
    for load in loads:
        load.wait()
    lane = lax.broadcasted_iota(jnp.int32, (ZY // 2, HALF), 1)
    spare = TOUCH * EB + lax.rem(lax.div(lane, ACCS), SPARE)
    for half in range(2):
        for k in range(2):
            found = faces[half, pl.ds(k, ZY // 2, stride=2), :]
            index[half, :, k * HALF : (k + 1) * HALF] = jnp.where(found < 0, spare, found) * 2

    def dot(a, b):
        return jnp.dot(a, b, preferred_element_type=jnp.float32)

    def across(weights, blocks, c):
        high, low = split(jnp.concatenate([win[block, c] for block in blocks], axis=0))
        both = dot(weights[...], high)
        return both[: 4 * ZY] + both[4 * ZY :] + dot(weights[: 4 * ZY], low)

    def forward(q):
        arrived(q, (0, 1))
        start(q, (4, 5, 10, 11))
        arrived(q, (3,), second_x | third_x)
        start(q, (6, 7))

    def begin(q):
        arrived(q, (2, 4, 5))
        for j in range(PART):
            c = q * PART + j
            partial[c] = across(near, [slot(d, dt) for d in (0, mate - g) for dt in (-1, 0, 1)], c)

    rows = PART * ZY

    def edge(k, q):
        row = (k * C + q * PART) * STEP
        return row // 8 * 8 if 0 < q < PARTS else (row + 7) // 8 * 8

    def stores(q):
        made = []
        for k in range(4):
            rows = pl.ds(edge(k, q), edge(k, q + 1) - edge(k, q))
            for half in range(2):
                made.append(
                    pltpu.make_async_copy(
                        features.at[half, rows], out.at[half, rows], stored.at[q, 2 * k + half]
                    )
                )
        return made

    def leave(q):
        for part_done in range(PARTS):
            @pl.when(q == part_done)
            def _():
                for made in stores(part_done):
                    made.start()

    def add_third(q):
        arrived(q, (3,), first_x | last_x)
        arrived(q, (6, 7, 8, 9, 10, 11))
        for j in range(PART):
            c = q * PART + j
            partial[c] += across(far, [slot(other - g, dt) for dt in (-1, 0, 1)], c)

    def end(q):
        for j in range(PART):
            high, low = split(partial[q * PART + j])
            for k in range(4):
                mixed_hi[k, j * ZY : (j + 1) * ZY, :] = high[k * ZY : (k + 1) * ZY]
                mixed_lo[k, j * ZY : (j + 1) * ZY, :] = low[k * ZY : (k + 1) * ZY]
        high, low = mixed_hi[...].reshape(4 * rows, X), mixed_lo[...].reshape(4 * rows, X)

        def along(n, k):
            columns = slice(k * X, (k + 1) * X)
            return (
                dot(high[:n], along_hi[:, columns])
                + dot(low[:n], along_hi[:, columns])
                + dot(high[:n], along_lo[:, columns])
            )

        by_gauss, by_slope, by_curve = along(4 * rows, 0), along(2 * rows, 1), along(rows, 2)
        smooth, grad_y, hess_yy, grad_z = (by_gauss[k * rows : (k + 1) * rows] for k in range(4))
        grad_x, hess_xy = by_slope[:rows], by_slope[rows:]
        half_trace = (hess_yy + by_curve) * 0.5
        spread = (hess_yy - by_curve) * 0.5
        deviation = jnp.sqrt(spread * spread + hess_xy * hess_xy)
        magnitude = jnp.sqrt(grad_z * grad_z + grad_y * grad_y + grad_x * grad_x)
        for k, value in enumerate((smooth, magnitude, half_trace + deviation, half_trace - deviation)):
            for j in range(PART):
                at = pl.ds((k * C + q * PART + j) * STEP, ZY)
                features[0, at, :] = value[j * ZY : (j + 1) * ZY, :HALF]
                features[1, at, :] = value[j * ZY : (j + 1) * ZY, HALF:]
        leave(q)

    forward(0)

    def near_work(q, carry):
        pl.when(q < PARTS)(lambda: forward(q))
        begin(q - 1)
        pl.when(~inner)(lambda: end(q - 1))
        return carry

    lax.fori_loop(1, PARTS + 1, near_work, 0)

    @pl.when(inner)
    def _():
        def far_work(q, carry):
            add_third(q)
            end(q)
            return carry

        lax.fori_loop(0, PARTS, far_work, 0)

    def finish(q, carry):
        for made, sent, _ in copies(q):
            pl.when(sent)(lambda made=made: made().wait_send())
        return carry

    lax.fori_loop(0, PARTS, finish, 0)
    for q in range(PARTS):
        for made in stores(q):
            made.wait()


def filtered(raw, faces):
    near, far, along_hi, along_lo = tables()
    hbm = pl.BlockSpec(memory_space=pltpu.HBM)
    return pl.pallas_call(
        filter_kernel,
        out_shape=(
            jax.ShapeDtypeStruct((2, FEATURES * STEP, HALF), jnp.float32),
            jax.ShapeDtypeStruct((2, ZY // 2, X), jnp.int32),
        ),
        in_specs=[hbm] * 6,
        out_specs=(hbm, pl.BlockSpec(memory_space=pltpu.VMEM)),
        scratch_shapes=[
            pltpu.VMEM((9, C, ZY, X), jnp.float32),
            pltpu.VMEM((2, ZY, HALF), jnp.int32),
            pltpu.VMEM((C, 4 * ZY, X), jnp.float32),
            pltpu.VMEM((2, FEATURES * STEP, HALF), jnp.float32),
            pltpu.VMEM(near.shape[1:], jnp.bfloat16),
            pltpu.VMEM(far.shape[1:], jnp.bfloat16),
            pltpu.VMEM(along_hi.shape, jnp.bfloat16),
            pltpu.VMEM(along_lo.shape, jnp.bfloat16),
            pltpu.VMEM((4, PART * ZY, X), jnp.bfloat16),
            pltpu.VMEM((4, PART * ZY, X), jnp.bfloat16),
            pltpu.SemaphoreType.DMA((12, PARTS)),
            pltpu.SemaphoreType.DMA((12, PARTS)),
            pltpu.SemaphoreType.DMA((7,)),
            pltpu.SemaphoreType.DMA((PARTS, 8)),
        ],
        compiler_params=pltpu.CompilerParams(
            collective_id=0, has_side_effects=True, vmem_limit_bytes=VMEM_BYTES
        ),
    )(raw, faces, *(jnp.asarray(table) for table in (near, far, along_hi, along_lo)))


def pool_kernel(
    features_in, index_in, touched_in, owner_in, upper, lower,
    features, index, touched, owner, row_a, row_b, merged, local, ahead, *rest,
):
    accs, targets = rest[:ACCS], rest[ACCS:]
    loads = [
        pltpu.make_async_copy(source, target, local.at[k])
        for k, (source, target) in enumerate(
            (
                (index_in, index),
                (features_in.at[0], features.at[pl.ds(0, FEATURES * STEP)]),
                (features_in.at[1], features.at[pl.ds(FEATURES * STEP, FEATURES * STEP)]),
                (touched_in, touched),
                (owner_in, owner),
            )
        )
    ]
    for load in loads:
        load.start()

    def summed(rows):
        sub = lax.broadcasted_iota(jnp.int32, (rows, HALF), 0)
        lane = lax.broadcasted_iota(jnp.int32, (rows, HALF), 1)
        return (lax.rem(sub, 2) == 1) | (lane >= 2 * FEATURES)

    pair, tile = summed(2), summed(16)
    start = jnp.where(tile, 0.0, FAR)

    def reset(i, carry):
        for acc in accs:
            acc[pl.ds(i * 16, 16), :] = start
        return carry

    def fetch(k, row):
        return pltpu.make_async_copy(index.at[row], targets[k], ahead.at[k])

    lax.fori_loop(0, ROWS // 32, reset, 0)
    loads[0].wait()
    for k in range(AHEAD):
        fetch(k, k).start()
    lax.fori_loop(ROWS // 32, ROWS // 16, reset, 0)
    ones = jnp.ones((1, HALF), jnp.float32)

    def turn(n, row):
        at = n + lax.div(n, ZY) * (FEATURES * STEP - ZY)
        values = features[pl.ds(at, FEATURES, stride=STEP), :]
        row[...] = jnp.concatenate([values, -values, values[:31], ones], axis=0).T

    def collect(target, first, row):
        for v in range(HALF):
            acc = accs[v % ACCS]
            at = pl.ds(target[first + v], 2)
            value = jnp.broadcast_to(row[v : v + 1, :], (2, HALF))
            old = acc[at, :]
            acc[at, :] = jnp.where(pair, old + value, jnp.maximum(old, value))

    loads[1].wait()
    turn(0, row_a)

    def body(i, carry):
        pl.when(i == ZY // (2 * AHEAD) - 1)(lambda: loads[2].wait())
        for k in range(AHEAD):
            n = i * AHEAD + k
            fetch(k, n).wait()
            turn(2 * n + 1, row_b)
            collect(targets[k], 0, row_a)
            turn(jnp.minimum(2 * n + 2, 2 * ZY - 1), row_a)
            collect(targets[k], HALF, row_b)
            pl.when(n + AHEAD < ZY)(lambda: fetch(k, n + AHEAD).start())
        return carry

    lax.fori_loop(0, ZY // AHEAD, body, 0)
    loads[3].wait()
    loads[4].wait()

    lane = lax.broadcasted_iota(jnp.int32, (EB, HALF), 1)
    empty = jnp.where(lane >= 2 * FEATURES, 0.0, FAR)

    def fill(b, carry):
        upper[b] = empty[:PIECE]
        lower[b, : EB - PIECE, :] = empty[PIECE:]
        lower[b, EB - PIECE :, :] = jnp.zeros((SENT - EB, HALF), jnp.float32)
        return carry

    lax.fori_loop(0, BLOCKS, fill, 0)
    lane = lax.broadcasted_iota(jnp.int32, (EB // 4, HALF), 1)

    def place(i, carry):
        for k in range(2 * EB // 16):
            rows = pl.ds(pl.multiple_of(i * 2 * EB + k * 16, 16), 16)
            total = accs[0][rows, :]
            for acc in accs[1:]:
                more = acc[rows, :]
                total = jnp.where(tile, total + more, jnp.maximum(total, more))
            merged[pl.ds(k * 16, 16), :] = total
        to = owner[touched[i]]
        tile_x, tile_yz = lax.rem(to, ROW), lax.div(to, ROW)
        extremes = merged[pl.ds(0, EB, stride=2), :]
        upper[tile_x * GROUP + tile_yz] = extremes[:PIECE]
        lower[to, : EB - PIECE, :] = extremes[PIECE:]
        sums = merged[pl.ds(1, EB, stride=2), :]
        packed = jnp.zeros((EB // 4, HALF), jnp.float32)
        for j in range(4):
            group = pltpu.roll(sums[j * 16 : (j + 1) * 16], (32 * j - 16) % HALF, 1)
            packed = jnp.where((lane >= 32 * j) & (lane < 32 * j + 32), group, packed)
        lower[to, EB - PIECE :, :] = packed
        return carry

    lax.fori_loop(0, TOUCH, place, 0)


def pooled(features, index, touched, owner):
    hbm = pl.BlockSpec(memory_space=pltpu.HBM)
    return pl.pallas_call(
        pool_kernel,
        out_shape=[jax.ShapeDtypeStruct((BLOCKS, PIECE, HALF), jnp.float32)] * 2,
        in_specs=[hbm] * 4,
        out_specs=[pl.BlockSpec(memory_space=pltpu.VMEM)] * 2,
        scratch_shapes=[
            pltpu.VMEM((2 * FEATURES * STEP, HALF), jnp.float32),
            pltpu.VMEM((ZY, X), jnp.int32),
            pltpu.SMEM((TOUCH,), jnp.int32),
            pltpu.SMEM((BLOCKS,), jnp.int32),
        ]
        + [pltpu.VMEM((HALF, HALF), jnp.float32)] * 3
        + [pltpu.SemaphoreType.DMA((5,)), pltpu.SemaphoreType.DMA((AHEAD,))]
        + [pltpu.VMEM((ROWS, HALF), jnp.float32)] * ACCS
        + [pltpu.SMEM((X,), jnp.int32)] * AHEAD,
        compiler_params=pltpu.CompilerParams(vmem_limit_bytes=VMEM_BYTES),
    )(features, index, touched, owner)


def merge_kernel(
    upper, lower, out, upper_sum, lower_sum, upper_got, lower_got, upper_last, lower_last, send, recv, local
):
    g, t = lax.axis_index("gz"), lax.axis_index("xy")
    x, yz = lax.rem(t, ROW), lax.div(t, ROW)
    z, y = lax.rem(yz, 2), lax.div(yz, 2)
    zx = lax.rem(t, GROUP)
    loads = [
        pltpu.make_async_copy(upper.at[pl.ds(x * GROUP, GROUP)], upper_sum, local.at[0]),
        pltpu.make_async_copy(lower.at[pl.ds(y * GROUP, GROUP)], lower_sum, local.at[1]),
    ]
    for load in loads:
        load.start()

    def along_x(k):
        return lax.rem(x + k, ROW)

    def along_y(k):
        return lax.rem(y + k, ROW)

    def along_yz(k):
        return lax.rem(yz + k, GROUP)

    def along_zx(k):
        return lax.rem(zx + k, GROUP)

    barrier = pltpu.get_barrier_semaphore()

    def greet(peer):
        pl.semaphore_signal(barrier, inc=1, device_id=(g, peer), device_id_type=MESH)

    for k in range(1, ROW):
        greet(yz * ROW + along_x(k))
        greet(along_y(k) * GROUP + zx)
    for k in range(ROW):
        greet(along_y(k) * GROUP + (1 - z) * ROW + x)
    for k in range(1, ROW):
        greet(y * GROUP + (1 - z) * ROW + along_x(k))
    pl.semaphore_wait(barrier, 3 * (ROW - 1) + ROW)

    def copy(source, target, at, peer):
        return pltpu.make_async_remote_copy(
            src_ref=source,
            dst_ref=target,
            send_sem=send.at[at],
            recv_sem=recv.at[at],
            device_id=(g, peer),
            device_id_type=MESH,
        )

    def first_upper(k):
        source = upper.at[pl.ds(along_x(k) * GROUP, GROUP)]
        return copy(source, upper_got.at[k - 1], k - 1, yz * ROW + along_x(k))

    def first_lower(k):
        source = lower.at[pl.ds(along_y(k) * GROUP, GROUP)]
        return copy(source, lower_got.at[k - 1], ROW + k - 2, along_y(k) * GROUP + zx)

    def last_upper(k):
        source = upper_sum.at[along_yz(k)]
        return copy(source, upper_last.at[k - 1], 2 * (ROW - 1) + k - 1, along_yz(k) * ROW + x)

    def last_lower(k):
        source = lower_sum.at[along_zx(k)]
        return copy(source, lower_last.at[k - 1], 2 * (ROW - 1) + GROUP + k - 2, y * GROUP + along_zx(k))

    lane = lax.broadcasted_iota(jnp.int32, (PIECE, HALF), 1)
    row = lax.broadcasted_iota(jnp.int32, (PIECE, HALF), 0)
    upper_adds = lane >= 2 * FEATURES
    lower_adds = upper_adds | (row >= EB - PIECE)

    def join(adds, left, right):
        return jnp.where(adds, left + right, jnp.maximum(left, right))

    order = (2, 1, 3)
    for k in order:
        first_upper(k).start()
        first_lower(k).start()
    for load in loads:
        load.wait()

    def stage(adds, first, got, summed, last):
        for k in order:
            first(k).wait_recv()

        def one(b, carry):
            total = summed[b]
            for k in range(ROW - 1):
                total = join(adds, total, got[k, b])
            summed[b] = total
            return carry

        lax.fori_loop(0, GROUP, one, 0)
        for k in range(1, GROUP):
            last(k).start()

    stage(upper_adds, first_upper, upper_got, upper_sum, last_upper)
    stage(lower_adds, first_lower, lower_got, lower_sum, last_lower)

    def gather(adds, total, got, last):
        for k in range(1, GROUP):
            last(k).wait_recv()
            total = join(adds, total, got[k - 1])
        return total

    total = jnp.concatenate(
        [
            gather(upper_adds, upper_sum[yz], upper_last, last_upper),
            gather(lower_adds, lower_sum[zx], lower_last, last_lower),
        ],
        axis=0,
    )
    extremes, packed = total[:EB], total[EB:]
    rest = jnp.concatenate([pltpu.roll(packed, (HALF + 16 - 32 * j) % HALF, 1) for j in range(4)], axis=0)
    count = extremes[:, HALF - 1 :]
    present = count > 0.0
    lane = lax.broadcasted_iota(jnp.int32, (EB, HALF), 1)
    means = jnp.where(lane < 31, pltpu.roll(extremes, HALF - 2 * FEATURES, 1), rest) / jnp.maximum(count, 1.0)
    signed = jnp.where(present, jnp.where(lane < FEATURES, extremes, -extremes), 0.0)
    shifted = pltpu.roll(signed, FEATURES, 1)
    out[:, :HALF] = jnp.where(lane < FEATURES, means, shifted)
    out[:, HALF:] = shifted[:, : 3 * FEATURES - HALF]

    for k in order:
        first_upper(k).wait_send()
        first_lower(k).wait_send()
    for k in range(1, GROUP):
        last_upper(k).wait_send()
        last_lower(k).wait_send()


def merged_stats(upper, lower):
    hbm = pl.BlockSpec(memory_space=pltpu.HBM)
    copies = 2 * (ROW - 1) + 2 * (GROUP - 1)
    return pl.pallas_call(
        merge_kernel,
        out_shape=jax.ShapeDtypeStruct((EB, 3 * FEATURES), jnp.float32),
        in_specs=[hbm] * 2,
        out_specs=pl.BlockSpec(memory_space=pltpu.VMEM),
        scratch_shapes=[pltpu.VMEM((GROUP, PIECE, HALF), jnp.float32)] * 2
        + [pltpu.VMEM((ROW - 1, GROUP, PIECE, HALF), jnp.float32)] * 2
        + [pltpu.VMEM((GROUP - 1, PIECE, HALF), jnp.float32)] * 2
        + [
            pltpu.SemaphoreType.DMA((copies,)),
            pltpu.SemaphoreType.DMA((copies,)),
            pltpu.SemaphoreType.DMA((2,)),
        ],
        compiler_params=pltpu.CompilerParams(
            collective_id=1, has_side_effects=True, vmem_limit_bytes=VMEM_BYTES
        ),
    )(upper, lower)


def per_device(raw_volume, face_slot, touched, block_owner):
    features, index = filtered(raw_volume.reshape(C, ZY, X), face_slot.reshape(ZY, X))
    upper, lower = pooled(features, index.reshape(ZY, X), touched.reshape(-1), block_owner.reshape(-1))
    return merged_stats(upper, lower).T[None, None]


def solution(mesh):
    placed = (P(None, "gz", "xy", None), P("gz", "xy", None), P("gz", "xy", None), P("gz", None))
    return jax.shard_map(
        per_device, mesh=mesh, in_specs=placed, out_specs=P("gz", "xy", None, None), check_vma=False
    )
```

```python
import functools

import jax
import jax.numpy as jnp
import ml_dtypes
import numpy as np
from jax import lax
from jax.experimental import pallas as pl
from jax.experimental.pallas import tpu as pltpu
from jax.sharding import PartitionSpec as P

RADIUS = 8
C = 12
Z = 8
Y = 8
X = 256
EB = 64
TOUCH = 16
BLOCKS = 32
TILES = 32
SLABS = 4
ZY = Z * Y
HALF = X // 2
FEATURES = 4 * C
PARTS = 6
PART = C // PARTS
DIRECT = 4
ACCS = 8
ROW = 4
SPARE = 8
ROWS = 2 * (TOUCH * EB + SPARE)
SENT = EB + EB // 4
PIECE = SENT // 2
GROUP = 8
FAR = -1e30
STEP = ZY + 1
AHEAD = 4
VMEM_BYTES = 62 * 2**20
MESH = pl.DeviceIdType.MESH


def taps():
    sigma = np.float32(RADIUS / 3.0)
    offsets = np.arange(-RADIUS, RADIUS + 1).astype(np.float32)
    gauss = np.exp(-offsets * offsets / (2.0 * sigma * sigma)).astype(np.float32)
    gauss = gauss / gauss.sum()
    slope = -(offsets / sigma) * gauss
    curve = (offsets * offsets / (sigma * sigma) - 1.0) * gauss
    return [tap.astype(np.float64) for tap in (gauss, slope, curve)]


def two_terms(table):
    table = table.astype(np.float32)
    high = table.astype(ml_dtypes.bfloat16)
    low = (table - high.astype(np.float32)).astype(ml_dtypes.bfloat16)
    return high, low


def band(tap, size, start, stop):
    offset = np.arange(start, stop)[None, :] - np.arange(size)[:, None]
    return np.where(np.abs(offset) <= RADIUS, tap[np.clip(offset + RADIUS, 0, 2 * RADIUS)], 0.0)


def tables():
    gauss, slope, curve = taps()
    rows = []
    for kz, ky in ((gauss, gauss), (gauss, slope), (gauss, curve), (slope, gauss)):
        bz = band(kz, Z, -Z, 2 * Z).reshape(Z, 3, Z)
        by = band(ky, Y, -Y, 2 * Y).reshape(Y, 3, Y)
        rows.append(np.einsum("pdz,qey->pqdezy", bz, by).reshape(ZY, 9 * ZY))
    weights = np.concatenate(rows, axis=0).reshape(4 * ZY, 3, 3 * ZY)

    def both_terms(*blocks):
        return np.concatenate(two_terms(np.concatenate([weights[:, d + 1] for d in blocks], axis=1)), axis=0)

    near = np.stack([both_terms(0, 1), both_terms(0, -1)])
    far = np.stack([both_terms(-1), both_terms(1)])
    along = [two_terms(band(tap, X, 0, X).T) for tap in (gauss, slope, curve)]
    return near, far, np.concatenate([t[0] for t in along], 1), np.concatenate([t[1] for t in along], 1)


def split(values):
    high = values.astype(jnp.bfloat16)
    return high, (values - high.astype(jnp.float32)).astype(jnp.bfloat16)


def slot(dz, dt):
    return (dz + 1) * 3 + (dt + 1)


def filter_kernel(
    raw, faces_in, near_in, far_in, along_hi_in, along_lo_in, out, index,
    win, faces, partial, features, near, far, along_hi, along_lo, mixed_hi, mixed_lo, send, recv, local, stored,
):
    g, t = lax.axis_index("gz"), lax.axis_index("xy")
    odd = lax.rem(g, 2)
    mate = g + 1 - 2 * odd
    inner = (g == 1) | (g == 2)
    other = 3 - g
    has_left, has_right = t > 0, t < TILES - 1
    column = lax.rem(t, ROW)
    first_x, last_x = column == 0, column == ROW - 1
    second_x, third_x = column == 1, column == 2
    cross_left, cross_right = inner & first_x & has_left, inner & last_x & has_right

    loads = [
        pltpu.make_async_copy(source, target, local.at[k])
        for k, (source, target) in enumerate(
            (
                (raw, win.at[slot(0, 0)]),
                (faces_in.at[:, pl.ds(0, HALF)], faces.at[0]),
                (faces_in.at[:, pl.ds(HALF, HALF)], faces.at[1]),
                (near_in.at[odd], near),
                (far_in.at[odd], far),
                (along_hi_in, along_hi),
                (along_lo_in, along_lo),
            )
        )
    ]
    for load in loads:
        load.start()

    barrier = pltpu.get_barrier_semaphore()
    greeted = 0
    for condition, dg, dt in (
        (has_left, g, t - 1),
        (has_right, g, t + 1),
        (inner, other, t),
        (cross_left, other, t - 1),
        (cross_right, other, t + 1),
    ):
        @pl.when(condition)
        def _():
            pl.semaphore_signal(barrier, inc=1, device_id=(dg, dt), device_id_type=MESH)

        greeted += condition.astype(jnp.int32)
    pl.semaphore_signal(barrier, inc=1, device_id=(mate, t), device_id_type=MESH)
    pl.semaphore_wait(barrier, greeted + 1)

    def part(ref, q):
        return ref.at[pl.ds(q * PART, PART)]

    def copy(kind, q, source, target, dg, dt):
        return pltpu.make_async_remote_copy(
            src_ref=part(source, q),
            dst_ref=part(win.at[target], q),
            send_sem=send.at[kind, q],
            recv_sem=recv.at[kind, q],
            device_id=(dg, dt),
            device_id_type=MESH,
        )

    def copies(q):
        up = other - g

        def made(*args):
            return lambda: copy(*args)

        middle = inner & (second_x | third_x)
        direct = q < DIRECT
        left, right = win.at[slot(0, -1)], win.at[slot(0, 1)]
        third = win.at[slot(up, 0)]
        return (
            (made(0, q, raw, slot(0, -1), g, t + 1), has_right, has_left),
            (made(1, q, raw, slot(0, 1), g, t - 1), has_left, has_right),
            (made(2, q, raw, slot(g - mate, 0), mate, t), True, True),
            (made(3, q, raw, slot(g - other, 0), other, t), middle | (inner & direct), middle | (inner & direct)),
            (made(4, q, left, slot(g - mate, -1), mate, t), has_left, has_left),
            (made(5, q, right, slot(g - mate, 1), mate, t), has_right, has_right),
            (made(6, q, third, slot(up, -1), g, t + 1), middle, inner & (third_x | last_x)),
            (made(7, q, third, slot(up, 1), g, t - 1), middle, inner & (first_x | second_x)),
            (made(8, q, raw, slot(g - other, -1), other, t + 1), cross_right, cross_left),
            (made(9, q, raw, slot(g - other, 1), other, t - 1), cross_left, cross_right),
            (made(10, q, left, slot(g - other, -1), other, t), inner & second_x, inner & second_x),
            (made(11, q, right, slot(g - other, 1), other, t), inner & third_x, inner & third_x),
            (made(12, q, win.at[slot(up, -1)], slot(up, 0), g, t - 1), inner & second_x & ~direct, inner & first_x & ~direct),
            (made(13, q, win.at[slot(up, 1)], slot(up, 0), g, t + 1), inner & third_x & ~direct, inner & last_x & ~direct),
        )

    def start(q, kinds):
        for made, sent, _ in [copies(q)[k] for k in kinds]:
            pl.when(sent)(lambda made=made: made().start())

    def arrived(q, kinds, where=True):
        for made, _, received in [copies(q)[k] for k in kinds]:
            pl.when(received & where)(lambda made=made: made().wait_recv())

    def first(q, carry):
        start(q, (3, 0, 1, 8, 9, 2))
        return carry

    lax.fori_loop(0, PARTS, first, 0)

    def clear(target):
        def one(c, carry):
            win[target, c] = jnp.zeros((ZY, X), jnp.float32)
            return carry

        lax.fori_loop(0, C, one, 0)

    for d in (0, mate - g):
        pl.when(t == 0)(lambda d=d: clear(slot(d, -1)))
        pl.when(t == TILES - 1)(lambda d=d: clear(slot(d, 1)))
    pl.when(inner & (t == 0))(lambda: clear(slot(other - g, -1)))
    pl.when(inner & (t == TILES - 1))(lambda: clear(slot(other - g, 1)))
    for load in loads:
        load.wait()
    lane = lax.broadcasted_iota(jnp.int32, (ZY // 2, HALF), 1)
    spare = TOUCH * EB + lax.rem(lax.div(lane, ACCS), SPARE)
    for half in range(2):
        for k in range(2):
            found = faces[half, pl.ds(k, ZY // 2, stride=2), :]
            index[half, :, k * HALF : (k + 1) * HALF] = jnp.where(found < 0, spare, found) * 2

    def dot(a, b):
        return jnp.dot(a, b, preferred_element_type=jnp.float32)

    def across(weights, blocks, c):
        high, low = split(jnp.concatenate([win[block, c] for block in blocks], axis=0))
        both = dot(weights[...], high)
        return both[: 4 * ZY] + both[4 * ZY :] + dot(weights[: 4 * ZY], low)

    def forward(q):
        arrived(q, (0, 1))
        start(q, (4, 5, 10, 11))
        arrived(q, (3,), second_x | third_x)
        start(q, (6, 7))

    def begin(q):
        arrived(q, (2, 4, 5))
        for j in range(PART):
            c = q * PART + j
            partial[c] = across(near, [slot(d, dt) for d in (0, mate - g) for dt in (-1, 0, 1)], c)

    rows = PART * ZY

    def edge(k, q):
        row = (k * C + q * PART) * STEP
        return row // 8 * 8 if 0 < q < PARTS else (row + 7) // 8 * 8

    def stores(q):
        made = []
        for k in range(4):
            rows = pl.ds(edge(k, q), edge(k, q + 1) - edge(k, q))
            for half in range(2):
                made.append(
                    pltpu.make_async_copy(
                        features.at[half, rows], out.at[half, rows], stored.at[q, 2 * k + half]
                    )
                )
        return made

    def leave(q):
        for part_done in range(PARTS):
            @pl.when(q == part_done)
            def _():
                for made in stores(part_done):
                    made.start()

    def add_third(q):
        arrived(q, (3,), first_x | last_x)
        arrived(q, (6, 7, 8, 9, 12, 13))
        arrived(q, (10, 11), q < DIRECT)
        for j in range(PART):
            c = q * PART + j
            partial[c] += across(far, [slot(other - g, dt) for dt in (-1, 0, 1)], c)

    def end(q):
        for j in range(PART):
            high, low = split(partial[q * PART + j])
            for k in range(4):
                mixed_hi[k, j * ZY : (j + 1) * ZY, :] = high[k * ZY : (k + 1) * ZY]
                mixed_lo[k, j * ZY : (j + 1) * ZY, :] = low[k * ZY : (k + 1) * ZY]
        high, low = mixed_hi[...].reshape(4 * rows, X), mixed_lo[...].reshape(4 * rows, X)

        def along(n, k):
            columns = slice(k * X, (k + 1) * X)
            return (
                dot(high[:n], along_hi[:, columns])
                + dot(low[:n], along_hi[:, columns])
                + dot(high[:n], along_lo[:, columns])
            )

        by_gauss, by_slope, by_curve = along(4 * rows, 0), along(2 * rows, 1), along(rows, 2)
        smooth, grad_y, hess_yy, grad_z = (by_gauss[k * rows : (k + 1) * rows] for k in range(4))
        grad_x, hess_xy = by_slope[:rows], by_slope[rows:]
        half_trace = (hess_yy + by_curve) * 0.5
        spread = (hess_yy - by_curve) * 0.5
        deviation = jnp.sqrt(spread * spread + hess_xy * hess_xy)
        magnitude = jnp.sqrt(grad_z * grad_z + grad_y * grad_y + grad_x * grad_x)
        for k, value in enumerate((smooth, magnitude, half_trace + deviation, half_trace - deviation)):
            for j in range(PART):
                at = pl.ds((k * C + q * PART + j) * STEP, ZY)
                features[0, at, :] = value[j * ZY : (j + 1) * ZY, :HALF]
                features[1, at, :] = value[j * ZY : (j + 1) * ZY, HALF:]
        leave(q)

    forward(0)

    def near_work(q, carry):
        pl.when(q < PARTS)(lambda: forward(q))
        begin(q - 1)
        pl.when(~inner)(lambda: end(q - 1))
        return carry

    lax.fori_loop(1, PARTS + 1, near_work, 0)

    @pl.when(inner)
    def _():
        def pass_on(q, carry):
            arrived(q, (10, 11))
            start(q, (12, 13))
            return carry

        lax.fori_loop(DIRECT, PARTS, pass_on, 0)

        def far_work(q, carry):
            add_third(q)
            end(q)
            return carry

        lax.fori_loop(0, PARTS, far_work, 0)

    def finish(q, carry):
        for made, sent, _ in copies(q):
            pl.when(sent)(lambda made=made: made().wait_send())
        return carry

    lax.fori_loop(0, PARTS, finish, 0)
    for q in range(PARTS):
        for made in stores(q):
            made.wait()


def filtered(raw, faces):
    near, far, along_hi, along_lo = tables()
    hbm = pl.BlockSpec(memory_space=pltpu.HBM)
    return pl.pallas_call(
        filter_kernel,
        out_shape=(
            jax.ShapeDtypeStruct((2, FEATURES * STEP, HALF), jnp.float32),
            jax.ShapeDtypeStruct((2, ZY // 2, X), jnp.int32),
        ),
        in_specs=[hbm] * 6,
        out_specs=(hbm, pl.BlockSpec(memory_space=pltpu.VMEM)),
        scratch_shapes=[
            pltpu.VMEM((9, C, ZY, X), jnp.float32),
            pltpu.VMEM((2, ZY, HALF), jnp.int32),
            pltpu.VMEM((C, 4 * ZY, X), jnp.float32),
            pltpu.VMEM((2, FEATURES * STEP, HALF), jnp.float32),
            pltpu.VMEM(near.shape[1:], jnp.bfloat16),
            pltpu.VMEM(far.shape[1:], jnp.bfloat16),
            pltpu.VMEM(along_hi.shape, jnp.bfloat16),
            pltpu.VMEM(along_lo.shape, jnp.bfloat16),
            pltpu.VMEM((4, PART * ZY, X), jnp.bfloat16),
            pltpu.VMEM((4, PART * ZY, X), jnp.bfloat16),
            pltpu.SemaphoreType.DMA((14, PARTS)),
            pltpu.SemaphoreType.DMA((14, PARTS)),
            pltpu.SemaphoreType.DMA((7,)),
            pltpu.SemaphoreType.DMA((PARTS, 8)),
        ],
        compiler_params=pltpu.CompilerParams(
            collective_id=0, has_side_effects=True, vmem_limit_bytes=VMEM_BYTES
        ),
    )(raw, faces, *(jnp.asarray(table) for table in (near, far, along_hi, along_lo)))


def pool_kernel(
    features_in, index_in, touched_in, owner_in, upper, lower,
    features, index, touched, owner, row_a, row_b, merged, local, ahead, *rest,
):
    accs, targets = rest[:ACCS], rest[ACCS:]
    loads = [
        pltpu.make_async_copy(source, target, local.at[k])
        for k, (source, target) in enumerate(
            (
                (index_in, index),
                (features_in.at[0], features.at[pl.ds(0, FEATURES * STEP)]),
                (features_in.at[1], features.at[pl.ds(FEATURES * STEP, FEATURES * STEP)]),
                (touched_in, touched),
                (owner_in, owner),
            )
        )
    ]
    for load in loads:
        load.start()

    def summed(rows):
        sub = lax.broadcasted_iota(jnp.int32, (rows, HALF), 0)
        lane = lax.broadcasted_iota(jnp.int32, (rows, HALF), 1)
        return (lax.rem(sub, 2) == 1) | (lane >= 2 * FEATURES)

    pair, tile = summed(2), summed(16)
    start = jnp.where(tile, 0.0, FAR)

    def reset(i, carry):
        for acc in accs:
            acc[pl.ds(i * 16, 16), :] = start
        return carry

    def fetch(k, row):
        return pltpu.make_async_copy(index.at[row], targets[k], ahead.at[k])

    lax.fori_loop(0, ROWS // 32, reset, 0)
    loads[0].wait()
    for k in range(AHEAD):
        fetch(k, k).start()
    lax.fori_loop(ROWS // 32, ROWS // 16, reset, 0)
    ones = jnp.ones((1, HALF), jnp.float32)

    def turn(n, row):
        at = n + lax.div(n, ZY) * (FEATURES * STEP - ZY)
        values = features[pl.ds(at, FEATURES, stride=STEP), :]
        row[...] = jnp.concatenate([values, -values, values[:31], ones], axis=0).T

    def collect(target, first, row):
        for v in range(HALF):
            acc = accs[v % ACCS]
            at = pl.ds(target[first + v], 2)
            value = jnp.broadcast_to(row[v : v + 1, :], (2, HALF))
            old = acc[at, :]
            acc[at, :] = jnp.where(pair, old + value, jnp.maximum(old, value))

    loads[1].wait()
    turn(0, row_a)

    def body(i, carry):
        pl.when(i == ZY // (2 * AHEAD) - 1)(lambda: loads[2].wait())
        for k in range(AHEAD):
            n = i * AHEAD + k
            fetch(k, n).wait()
            turn(2 * n + 1, row_b)
            collect(targets[k], 0, row_a)
            turn(jnp.minimum(2 * n + 2, 2 * ZY - 1), row_a)
            collect(targets[k], HALF, row_b)
            pl.when(n + AHEAD < ZY)(lambda: fetch(k, n + AHEAD).start())
        return carry

    lax.fori_loop(0, ZY // AHEAD, body, 0)
    loads[3].wait()
    loads[4].wait()

    lane = lax.broadcasted_iota(jnp.int32, (EB, HALF), 1)
    empty = jnp.where(lane >= 2 * FEATURES, 0.0, FAR)

    def fill(b, carry):
        upper[b] = empty[:PIECE]
        lower[b, : EB - PIECE, :] = empty[PIECE:]
        lower[b, EB - PIECE :, :] = jnp.zeros((SENT - EB, HALF), jnp.float32)
        return carry

    lax.fori_loop(0, BLOCKS, fill, 0)
    lane = lax.broadcasted_iota(jnp.int32, (EB // 4, HALF), 1)

    def place(i, carry):
        for k in range(2 * EB // 16):
            rows = pl.ds(pl.multiple_of(i * 2 * EB + k * 16, 16), 16)
            total = accs[0][rows, :]
            for acc in accs[1:]:
                more = acc[rows, :]
                total = jnp.where(tile, total + more, jnp.maximum(total, more))
            merged[pl.ds(k * 16, 16), :] = total
        to = owner[touched[i]]
        tile_x, tile_yz = lax.rem(to, ROW), lax.div(to, ROW)
        extremes = merged[pl.ds(0, EB, stride=2), :]
        upper[tile_x * GROUP + tile_yz] = extremes[:PIECE]
        lower[to, : EB - PIECE, :] = extremes[PIECE:]
        sums = merged[pl.ds(1, EB, stride=2), :]
        packed = jnp.zeros((EB // 4, HALF), jnp.float32)
        for j in range(4):
            group = pltpu.roll(sums[j * 16 : (j + 1) * 16], (32 * j - 16) % HALF, 1)
            packed = jnp.where((lane >= 32 * j) & (lane < 32 * j + 32), group, packed)
        lower[to, EB - PIECE :, :] = packed
        return carry

    lax.fori_loop(0, TOUCH, place, 0)


def pooled(features, index, touched, owner):
    hbm = pl.BlockSpec(memory_space=pltpu.HBM)
    return pl.pallas_call(
        pool_kernel,
        out_shape=[jax.ShapeDtypeStruct((BLOCKS, PIECE, HALF), jnp.float32)] * 2,
        in_specs=[hbm] * 4,
        out_specs=[pl.BlockSpec(memory_space=pltpu.VMEM)] * 2,
        scratch_shapes=[
            pltpu.VMEM((2 * FEATURES * STEP, HALF), jnp.float32),
            pltpu.VMEM((ZY, X), jnp.int32),
            pltpu.SMEM((TOUCH,), jnp.int32),
            pltpu.SMEM((BLOCKS,), jnp.int32),
        ]
        + [pltpu.VMEM((HALF, HALF), jnp.float32)] * 3
        + [pltpu.SemaphoreType.DMA((5,)), pltpu.SemaphoreType.DMA((AHEAD,))]
        + [pltpu.VMEM((ROWS, HALF), jnp.float32)] * ACCS
        + [pltpu.SMEM((X,), jnp.int32)] * AHEAD,
        compiler_params=pltpu.CompilerParams(vmem_limit_bytes=VMEM_BYTES),
    )(features, index, touched, owner)


def merge_kernel(
    upper, lower, out, upper_sum, lower_sum, upper_got, lower_got, upper_last, lower_last, send, recv, local
):
    g, t = lax.axis_index("gz"), lax.axis_index("xy")
    x, yz = lax.rem(t, ROW), lax.div(t, ROW)
    z, y = lax.rem(yz, 2), lax.div(yz, 2)
    zx = lax.rem(t, GROUP)
    loads = [
        pltpu.make_async_copy(upper.at[pl.ds(x * GROUP, GROUP)], upper_sum, local.at[0]),
        pltpu.make_async_copy(lower.at[pl.ds(y * GROUP, GROUP)], lower_sum, local.at[1]),
    ]
    for load in loads:
        load.start()

    def along_x(k):
        return lax.rem(x + k, ROW)

    def along_y(k):
        return lax.rem(y + k, ROW)

    def along_yz(k):
        return lax.rem(yz + k, GROUP)

    def along_zx(k):
        return lax.rem(zx + k, GROUP)

    barrier = pltpu.get_barrier_semaphore()

    def greet(peer):
        pl.semaphore_signal(barrier, inc=1, device_id=(g, peer), device_id_type=MESH)

    for k in range(1, ROW):
        greet(yz * ROW + along_x(k))
        greet(along_y(k) * GROUP + zx)
    for k in range(ROW):
        greet(along_y(k) * GROUP + (1 - z) * ROW + x)
    for k in range(1, ROW):
        greet(y * GROUP + (1 - z) * ROW + along_x(k))
    pl.semaphore_wait(barrier, 3 * (ROW - 1) + ROW)

    def copy(source, target, at, peer):
        return pltpu.make_async_remote_copy(
            src_ref=source,
            dst_ref=target,
            send_sem=send.at[at],
            recv_sem=recv.at[at],
            device_id=(g, peer),
            device_id_type=MESH,
        )

    def first_upper(k):
        source = upper.at[pl.ds(along_x(k) * GROUP, GROUP)]
        return copy(source, upper_got.at[k - 1], k - 1, yz * ROW + along_x(k))

    def first_lower(k):
        source = lower.at[pl.ds(along_y(k) * GROUP, GROUP)]
        return copy(source, lower_got.at[k - 1], ROW + k - 2, along_y(k) * GROUP + zx)

    def last_upper(k):
        source = upper_sum.at[along_yz(k)]
        return copy(source, upper_last.at[k - 1], 2 * (ROW - 1) + k - 1, along_yz(k) * ROW + x)

    def last_lower(k):
        source = lower_sum.at[along_zx(k)]
        return copy(source, lower_last.at[k - 1], 2 * (ROW - 1) + GROUP + k - 2, y * GROUP + along_zx(k))

    lane = lax.broadcasted_iota(jnp.int32, (PIECE, HALF), 1)
    row = lax.broadcasted_iota(jnp.int32, (PIECE, HALF), 0)
    upper_adds = lane >= 2 * FEATURES
    lower_adds = upper_adds | (row >= EB - PIECE)

    def join(adds, left, right):
        return jnp.where(adds, left + right, jnp.maximum(left, right))

    order = (2, 1, 3)
    for k in order:
        first_upper(k).start()
        first_lower(k).start()
    for load in loads:
        load.wait()

    def stage(adds, first, got, summed, last):
        for k in order:
            first(k).wait_recv()

        def one(b, carry):
            total = summed[b]
            for k in range(ROW - 1):
                total = join(adds, total, got[k, b])
            summed[b] = total
            return carry

        lax.fori_loop(0, GROUP, one, 0)
        for k in range(1, GROUP):
            last(k).start()

    stage(upper_adds, first_upper, upper_got, upper_sum, last_upper)
    stage(lower_adds, first_lower, lower_got, lower_sum, last_lower)

    def gather(adds, total, got, last):
        for k in range(1, GROUP):
            last(k).wait_recv()
            total = join(adds, total, got[k - 1])
        return total

    total = jnp.concatenate(
        [
            gather(upper_adds, upper_sum[yz], upper_last, last_upper),
            gather(lower_adds, lower_sum[zx], lower_last, last_lower),
        ],
        axis=0,
    )
    extremes, packed = total[:EB], total[EB:]
    rest = jnp.concatenate([pltpu.roll(packed, (HALF + 16 - 32 * j) % HALF, 1) for j in range(4)], axis=0)
    count = extremes[:, HALF - 1 :]
    present = count > 0.0
    lane = lax.broadcasted_iota(jnp.int32, (EB, HALF), 1)
    means = jnp.where(lane < 31, pltpu.roll(extremes, HALF - 2 * FEATURES, 1), rest) / jnp.maximum(count, 1.0)
    signed = jnp.where(present, jnp.where(lane < FEATURES, extremes, -extremes), 0.0)
    shifted = pltpu.roll(signed, FEATURES, 1)
    out[:, :HALF] = jnp.where(lane < FEATURES, means, shifted)
    out[:, HALF:] = shifted[:, : 3 * FEATURES - HALF]

    for k in order:
        first_upper(k).wait_send()
        first_lower(k).wait_send()
    for k in range(1, GROUP):
        last_upper(k).wait_send()
        last_lower(k).wait_send()


def merged_stats(upper, lower):
    hbm = pl.BlockSpec(memory_space=pltpu.HBM)
    copies = 2 * (ROW - 1) + 2 * (GROUP - 1)
    return pl.pallas_call(
        merge_kernel,
        out_shape=jax.ShapeDtypeStruct((EB, 3 * FEATURES), jnp.float32),
        in_specs=[hbm] * 2,
        out_specs=pl.BlockSpec(memory_space=pltpu.VMEM),
        scratch_shapes=[pltpu.VMEM((GROUP, PIECE, HALF), jnp.float32)] * 2
        + [pltpu.VMEM((ROW - 1, GROUP, PIECE, HALF), jnp.float32)] * 2
        + [pltpu.VMEM((GROUP - 1, PIECE, HALF), jnp.float32)] * 2
        + [
            pltpu.SemaphoreType.DMA((copies,)),
            pltpu.SemaphoreType.DMA((copies,)),
            pltpu.SemaphoreType.DMA((2,)),
        ],
        compiler_params=pltpu.CompilerParams(
            collective_id=1, has_side_effects=True, vmem_limit_bytes=VMEM_BYTES
        ),
    )(upper, lower)


def per_device(raw_volume, face_slot, touched, block_owner):
    features, index = filtered(raw_volume.reshape(C, ZY, X), face_slot.reshape(ZY, X))
    upper, lower = pooled(features, index.reshape(ZY, X), touched.reshape(-1), block_owner.reshape(-1))
    return merged_stats(upper, lower).T[None, None]


def solution(mesh):
    placed = (P(None, "gz", "xy", None), P("gz", "xy", None), P("gz", "xy", None), P("gz", None))
    return jax.shard_map(
        per_device, mesh=mesh, in_specs=placed, out_specs=P("gz", "xy", None, None), check_vma=False
    )
```

```python
import functools

import jax
import jax.numpy as jnp
import ml_dtypes
import numpy as np
from jax import lax
from jax.experimental import pallas as pl
from jax.experimental.pallas import tpu as pltpu
from jax.sharding import PartitionSpec as P

RADIUS = 8
C = 12
Z = 8
Y = 8
X = 256
EB = 64
TOUCH = 16
BLOCKS = 32
TILES = 32
SLABS = 4
ZY = Z * Y
HALF = X // 2
FEATURES = 4 * C
PARTS = 6
PART = C // PARTS
DIRECT = 3
CROSSED = 2
ACCS = 8
ROW = 4
SPARE = 8
ROWS = 2 * (TOUCH * EB + SPARE)
SENT = EB + EB // 4
PIECE = SENT // 2
GROUP = 8
FAR = -1e30
STEP = ZY + 1
AHEAD = 4
VMEM_BYTES = 62 * 2**20
MESH = pl.DeviceIdType.MESH


def taps():
    sigma = np.float32(RADIUS / 3.0)
    offsets = np.arange(-RADIUS, RADIUS + 1).astype(np.float32)
    gauss = np.exp(-offsets * offsets / (2.0 * sigma * sigma)).astype(np.float32)
    gauss = gauss / gauss.sum()
    slope = -(offsets / sigma) * gauss
    curve = (offsets * offsets / (sigma * sigma) - 1.0) * gauss
    return [tap.astype(np.float64) for tap in (gauss, slope, curve)]


def two_terms(table):
    table = table.astype(np.float32)
    high = table.astype(ml_dtypes.bfloat16)
    low = (table - high.astype(np.float32)).astype(ml_dtypes.bfloat16)
    return high, low


def band(tap, size, start, stop):
    offset = np.arange(start, stop)[None, :] - np.arange(size)[:, None]
    return np.where(np.abs(offset) <= RADIUS, tap[np.clip(offset + RADIUS, 0, 2 * RADIUS)], 0.0)


def tables():
    gauss, slope, curve = taps()
    rows = []
    for kz, ky in ((gauss, gauss), (gauss, slope), (gauss, curve), (slope, gauss)):
        bz = band(kz, Z, -Z, 2 * Z).reshape(Z, 3, Z)
        by = band(ky, Y, -Y, 2 * Y).reshape(Y, 3, Y)
        rows.append(np.einsum("pdz,qey->pqdezy", bz, by).reshape(ZY, 9 * ZY))
    weights = np.concatenate(rows, axis=0).reshape(4 * ZY, 3, 3 * ZY)

    def both_terms(*blocks):
        return np.concatenate(two_terms(np.concatenate([weights[:, d + 1] for d in blocks], axis=1)), axis=0)

    near = np.stack([both_terms(0, 1), both_terms(0, -1)])
    far = np.stack([both_terms(-1), both_terms(1)])
    along = [two_terms(band(tap, X, 0, X).T) for tap in (gauss, slope, curve)]
    return near, far, np.concatenate([t[0] for t in along], 1), np.concatenate([t[1] for t in along], 1)


def split(values):
    high = values.astype(jnp.bfloat16)
    return high, (values - high.astype(jnp.float32)).astype(jnp.bfloat16)


def slot(dz, dt):
    return (dz + 1) * 3 + (dt + 1)


def filter_kernel(
    raw, faces_in, near_in, far_in, along_hi_in, along_lo_in, out, index,
    win, faces, partial, features, near, far, along_hi, along_lo, mixed_hi, mixed_lo, send, recv, local, stored,
):
    g, t = lax.axis_index("gz"), lax.axis_index("xy")
    odd = lax.rem(g, 2)
    mate = g + 1 - 2 * odd
    inner = (g == 1) | (g == 2)
    other = 3 - g
    has_left, has_right = t > 0, t < TILES - 1
    column = lax.rem(t, ROW)
    first_x, last_x = column == 0, column == ROW - 1
    second_x, third_x = column == 1, column == 2
    cross_left, cross_right = inner & first_x & has_left, inner & last_x & has_right

    loads = [
        pltpu.make_async_copy(source, target, local.at[k])
        for k, (source, target) in enumerate(
            (
                (raw, win.at[slot(0, 0)]),
                (faces_in.at[:, pl.ds(0, HALF)], faces.at[0]),
                (faces_in.at[:, pl.ds(HALF, HALF)], faces.at[1]),
                (near_in.at[odd], near),
                (far_in.at[odd], far),
                (along_hi_in, along_hi),
                (along_lo_in, along_lo),
            )
        )
    ]
    for load in loads:
        load.start()

    barrier = pltpu.get_barrier_semaphore()
    greeted = 0
    for condition, dg, dt in (
        (has_left, g, t - 1),
        (has_right, g, t + 1),
        (inner, other, t),
        (cross_left, other, t - 1),
        (cross_right, other, t + 1),
    ):
        @pl.when(condition)
        def _():
            pl.semaphore_signal(barrier, inc=1, device_id=(dg, dt), device_id_type=MESH)

        greeted += condition.astype(jnp.int32)
    pl.semaphore_signal(barrier, inc=1, device_id=(mate, t), device_id_type=MESH)
    pl.semaphore_wait(barrier, greeted + 1)

    def part(ref, q):
        return ref.at[pl.ds(q * PART, PART)]

    def copy(kind, q, source, target, dg, dt):
        return pltpu.make_async_remote_copy(
            src_ref=part(source, q),
            dst_ref=part(win.at[target], q),
            send_sem=send.at[kind, q],
            recv_sem=recv.at[kind, q],
            device_id=(dg, dt),
            device_id_type=MESH,
        )

    def copies(q):
        up = other - g

        def made(*args):
            return lambda: copy(*args)

        middle = inner & (second_x | third_x)
        direct, crossed = q < DIRECT, q < CROSSED
        from_left = inner & has_left & (second_x | (first_x & ~crossed))
        from_right = inner & has_right & (third_x | (last_x & ~crossed))
        left, right = win.at[slot(0, -1)], win.at[slot(0, 1)]
        third = win.at[slot(up, 0)]
        return (
            (made(0, q, raw, slot(0, -1), g, t + 1), has_right, has_left),
            (made(1, q, raw, slot(0, 1), g, t - 1), has_left, has_right),
            (made(2, q, raw, slot(g - mate, 0), mate, t), True, True),
            (made(3, q, raw, slot(g - other, 0), other, t), middle | (inner & direct), middle | (inner & direct)),
            (made(4, q, left, slot(g - mate, -1), mate, t), has_left, has_left),
            (made(5, q, right, slot(g - mate, 1), mate, t), has_right, has_right),
            (made(6, q, third, slot(up, -1), g, t + 1), middle, inner & (third_x | last_x)),
            (made(7, q, third, slot(up, 1), g, t - 1), middle, inner & (first_x | second_x)),
            (made(8, q, raw, slot(g - other, -1), other, t + 1), cross_right & crossed, cross_left & crossed),
            (made(9, q, raw, slot(g - other, 1), other, t - 1), cross_left & crossed, cross_right & crossed),
            (made(10, q, left, slot(g - other, -1), other, t), from_left, from_left),
            (made(11, q, right, slot(g - other, 1), other, t), from_right, from_right),
            (made(12, q, win.at[slot(up, -1)], slot(up, 0), g, t - 1), inner & second_x & ~direct, inner & first_x & ~direct),
            (made(13, q, win.at[slot(up, 1)], slot(up, 0), g, t + 1), inner & third_x & ~direct, inner & last_x & ~direct),
        )

    def start(q, kinds):
        for made, sent, _ in [copies(q)[k] for k in kinds]:
            pl.when(sent)(lambda made=made: made().start())

    def arrived(q, kinds, where=True):
        for made, _, received in [copies(q)[k] for k in kinds]:
            pl.when(received & where)(lambda made=made: made().wait_recv())

    def first(q, carry):
        start(q, (3, 0, 1, 8, 9, 2))
        return carry

    lax.fori_loop(0, PARTS, first, 0)

    def clear(target):
        def one(c, carry):
            win[target, c] = jnp.zeros((ZY, X), jnp.float32)
            return carry

        lax.fori_loop(0, C, one, 0)

    for d in (0, mate - g):
        pl.when(t == 0)(lambda d=d: clear(slot(d, -1)))
        pl.when(t == TILES - 1)(lambda d=d: clear(slot(d, 1)))
    pl.when(inner & (t == 0))(lambda: clear(slot(other - g, -1)))
    pl.when(inner & (t == TILES - 1))(lambda: clear(slot(other - g, 1)))
    for load in loads:
        load.wait()
    lane = lax.broadcasted_iota(jnp.int32, (ZY // 2, HALF), 1)
    spare = TOUCH * EB + lax.rem(lax.div(lane, ACCS), SPARE)
    for half in range(2):
        for k in range(2):
            found = faces[half, pl.ds(k, ZY // 2, stride=2), :]
            index[half, :, k * HALF : (k + 1) * HALF] = jnp.where(found < 0, spare, found) * 2

    def dot(a, b):
        return jnp.dot(a, b, preferred_element_type=jnp.float32)

    def across(weights, blocks, c):
        high, low = split(jnp.concatenate([win[block, c] for block in blocks], axis=0))
        both = dot(weights[...], high)
        return both[: 4 * ZY] + both[4 * ZY :] + dot(weights[: 4 * ZY], low)

    def forward(q):
        arrived(q, (0, 1))
        start(q, (4, 5, 10, 11))
        arrived(q, (3,), second_x | third_x)
        start(q, (6, 7))

    def begin(q):
        arrived(q, (2, 4, 5))
        for j in range(PART):
            c = q * PART + j
            partial[c] = across(near, [slot(d, dt) for d in (0, mate - g) for dt in (-1, 0, 1)], c)

    rows = PART * ZY

    def edge(k, q):
        row = (k * C + q * PART) * STEP
        return row // 8 * 8 if 0 < q < PARTS else (row + 7) // 8 * 8

    def stores(q):
        made = []
        for k in range(4):
            rows = pl.ds(edge(k, q), edge(k, q + 1) - edge(k, q))
            for half in range(2):
                made.append(
                    pltpu.make_async_copy(
                        features.at[half, rows], out.at[half, rows], stored.at[q, 2 * k + half]
                    )
                )
        return made

    def leave(q):
        for part_done in range(PARTS):
            @pl.when(q == part_done)
            def _():
                for made in stores(part_done):
                    made.start()

    def add_third(q):
        arrived(q, (3,), first_x | last_x)
        arrived(q, (6, 7, 8, 9, 12, 13))
        arrived(q, (10, 11), (q < DIRECT) | first_x | last_x)
        for j in range(PART):
            c = q * PART + j
            partial[c] += across(far, [slot(other - g, dt) for dt in (-1, 0, 1)], c)

    def end(q):
        for j in range(PART):
            high, low = split(partial[q * PART + j])
            for k in range(4):
                mixed_hi[k, j * ZY : (j + 1) * ZY, :] = high[k * ZY : (k + 1) * ZY]
                mixed_lo[k, j * ZY : (j + 1) * ZY, :] = low[k * ZY : (k + 1) * ZY]
        high, low = mixed_hi[...].reshape(4 * rows, X), mixed_lo[...].reshape(4 * rows, X)

        def along(n, k):
            columns = slice(k * X, (k + 1) * X)
            return (
                dot(high[:n], along_hi[:, columns])
                + dot(low[:n], along_hi[:, columns])
                + dot(high[:n], along_lo[:, columns])
            )

        by_gauss, by_slope, by_curve = along(4 * rows, 0), along(2 * rows, 1), along(rows, 2)
        smooth, grad_y, hess_yy, grad_z = (by_gauss[k * rows : (k + 1) * rows] for k in range(4))
        grad_x, hess_xy = by_slope[:rows], by_slope[rows:]
        half_trace = (hess_yy + by_curve) * 0.5
        spread = (hess_yy - by_curve) * 0.5
        deviation = jnp.sqrt(spread * spread + hess_xy * hess_xy)
        magnitude = jnp.sqrt(grad_z * grad_z + grad_y * grad_y + grad_x * grad_x)
        for k, value in enumerate((smooth, magnitude, half_trace + deviation, half_trace - deviation)):
            for j in range(PART):
                at = pl.ds((k * C + q * PART + j) * STEP, ZY)
                features[0, at, :] = value[j * ZY : (j + 1) * ZY, :HALF]
                features[1, at, :] = value[j * ZY : (j + 1) * ZY, HALF:]
        leave(q)

    forward(0)

    def near_work(q, carry):
        pl.when(q < PARTS)(lambda: forward(q))
        begin(q - 1)
        pl.when(~inner)(lambda: end(q - 1))
        return carry

    lax.fori_loop(1, PARTS + 1, near_work, 0)

    @pl.when(inner)
    def _():
        def pass_on(q, carry):
            arrived(q, (10, 11), second_x | third_x)
            start(q, (12, 13))
            return carry

        lax.fori_loop(DIRECT, PARTS, pass_on, 0)

        def far_work(q, carry):
            add_third(q)
            end(q)
            return carry

        lax.fori_loop(0, PARTS, far_work, 0)

    def finish(q, carry):
        for made, sent, _ in copies(q):
            pl.when(sent)(lambda made=made: made().wait_send())
        return carry

    lax.fori_loop(0, PARTS, finish, 0)
    for q in range(PARTS):
        for made in stores(q):
            made.wait()


def filtered(raw, faces):
    near, far, along_hi, along_lo = tables()
    hbm = pl.BlockSpec(memory_space=pltpu.HBM)
    return pl.pallas_call(
        filter_kernel,
        out_shape=(
            jax.ShapeDtypeStruct((2, FEATURES * STEP, HALF), jnp.float32),
            jax.ShapeDtypeStruct((2, ZY // 2, X), jnp.int32),
        ),
        in_specs=[hbm] * 6,
        out_specs=(hbm, pl.BlockSpec(memory_space=pltpu.VMEM)),
        scratch_shapes=[
            pltpu.VMEM((9, C, ZY, X), jnp.float32),
            pltpu.VMEM((2, ZY, HALF), jnp.int32),
            pltpu.VMEM((C, 4 * ZY, X), jnp.float32),
            pltpu.VMEM((2, FEATURES * STEP, HALF), jnp.float32),
            pltpu.VMEM(near.shape[1:], jnp.bfloat16),
            pltpu.VMEM(far.shape[1:], jnp.bfloat16),
            pltpu.VMEM(along_hi.shape, jnp.bfloat16),
            pltpu.VMEM(along_lo.shape, jnp.bfloat16),
            pltpu.VMEM((4, PART * ZY, X), jnp.bfloat16),
            pltpu.VMEM((4, PART * ZY, X), jnp.bfloat16),
            pltpu.SemaphoreType.DMA((14, PARTS)),
            pltpu.SemaphoreType.DMA((14, PARTS)),
            pltpu.SemaphoreType.DMA((7,)),
            pltpu.SemaphoreType.DMA((PARTS, 8)),
        ],
        compiler_params=pltpu.CompilerParams(
            collective_id=0, has_side_effects=True, vmem_limit_bytes=VMEM_BYTES
        ),
    )(raw, faces, *(jnp.asarray(table) for table in (near, far, along_hi, along_lo)))


def pool_kernel(
    features_in, index_in, touched_in, owner_in, upper, lower,
    features, index, touched, owner, row_a, row_b, merged, local, ahead, *rest,
):
    accs, targets = rest[:ACCS], rest[ACCS:]
    loads = [
        pltpu.make_async_copy(source, target, local.at[k])
        for k, (source, target) in enumerate(
            (
                (index_in, index),
                (features_in.at[0], features.at[pl.ds(0, FEATURES * STEP)]),
                (features_in.at[1], features.at[pl.ds(FEATURES * STEP, FEATURES * STEP)]),
                (touched_in, touched),
                (owner_in, owner),
            )
        )
    ]
    for load in loads:
        load.start()

    def summed(rows):
        sub = lax.broadcasted_iota(jnp.int32, (rows, HALF), 0)
        lane = lax.broadcasted_iota(jnp.int32, (rows, HALF), 1)
        return (lax.rem(sub, 2) == 1) | (lane >= 2 * FEATURES)

    pair, tile = summed(2), summed(16)
    start = jnp.where(tile, 0.0, FAR)

    def reset(i, carry):
        for acc in accs:
            acc[pl.ds(i * 16, 16), :] = start
        return carry

    def fetch(k, row):
        return pltpu.make_async_copy(index.at[row], targets[k], ahead.at[k])

    lax.fori_loop(0, ROWS // 32, reset, 0)
    loads[0].wait()
    for k in range(AHEAD):
        fetch(k, k).start()
    lax.fori_loop(ROWS // 32, ROWS // 16, reset, 0)
    ones = jnp.ones((1, HALF), jnp.float32)

    def turn(n, row):
        at = n + lax.div(n, ZY) * (FEATURES * STEP - ZY)
        values = features[pl.ds(at, FEATURES, stride=STEP), :]
        row[...] = jnp.concatenate([values, -values, values[:31], ones], axis=0).T

    def collect(target, first, row):
        for v in range(HALF):
            acc = accs[v % ACCS]
            at = pl.ds(target[first + v], 2)
            value = jnp.broadcast_to(row[v : v + 1, :], (2, HALF))
            old = acc[at, :]
            acc[at, :] = jnp.where(pair, old + value, jnp.maximum(old, value))

    loads[1].wait()
    turn(0, row_a)

    def body(i, carry):
        pl.when(i == ZY // (2 * AHEAD) - 1)(lambda: loads[2].wait())
        for k in range(AHEAD):
            n = i * AHEAD + k
            fetch(k, n).wait()
            turn(2 * n + 1, row_b)
            collect(targets[k], 0, row_a)
            turn(jnp.minimum(2 * n + 2, 2 * ZY - 1), row_a)
            collect(targets[k], HALF, row_b)
            pl.when(n + AHEAD < ZY)(lambda: fetch(k, n + AHEAD).start())
        return carry

    lax.fori_loop(0, ZY // AHEAD, body, 0)
    loads[3].wait()
    loads[4].wait()

    lane = lax.broadcasted_iota(jnp.int32, (EB, HALF), 1)
    empty = jnp.where(lane >= 2 * FEATURES, 0.0, FAR)

    def fill(b, carry):
        upper[b] = empty[:PIECE]
        lower[b, : EB - PIECE, :] = empty[PIECE:]
        lower[b, EB - PIECE :, :] = jnp.zeros((SENT - EB, HALF), jnp.float32)
        return carry

    lax.fori_loop(0, BLOCKS, fill, 0)
    lane = lax.broadcasted_iota(jnp.int32, (EB // 4, HALF), 1)

    def place(i, carry):
        for k in range(2 * EB // 16):
            rows = pl.ds(pl.multiple_of(i * 2 * EB + k * 16, 16), 16)
            total = accs[0][rows, :]
            for acc in accs[1:]:
                more = acc[rows, :]
                total = jnp.where(tile, total + more, jnp.maximum(total, more))
            merged[pl.ds(k * 16, 16), :] = total
        to = owner[touched[i]]
        tile_x, tile_yz = lax.rem(to, ROW), lax.div(to, ROW)
        extremes = merged[pl.ds(0, EB, stride=2), :]
        upper[tile_x * GROUP + tile_yz] = extremes[:PIECE]
        lower[to, : EB - PIECE, :] = extremes[PIECE:]
        sums = merged[pl.ds(1, EB, stride=2), :]
        packed = jnp.zeros((EB // 4, HALF), jnp.float32)
        for j in range(4):
            group = pltpu.roll(sums[j * 16 : (j + 1) * 16], (32 * j - 16) % HALF, 1)
            packed = jnp.where((lane >= 32 * j) & (lane < 32 * j + 32), group, packed)
        lower[to, EB - PIECE :, :] = packed
        return carry

    lax.fori_loop(0, TOUCH, place, 0)


def pooled(features, index, touched, owner):
    hbm = pl.BlockSpec(memory_space=pltpu.HBM)
    return pl.pallas_call(
        pool_kernel,
        out_shape=[jax.ShapeDtypeStruct((BLOCKS, PIECE, HALF), jnp.float32)] * 2,
        in_specs=[hbm] * 4,
        out_specs=[pl.BlockSpec(memory_space=pltpu.VMEM)] * 2,
        scratch_shapes=[
            pltpu.VMEM((2 * FEATURES * STEP, HALF), jnp.float32),
            pltpu.VMEM((ZY, X), jnp.int32),
            pltpu.SMEM((TOUCH,), jnp.int32),
            pltpu.SMEM((BLOCKS,), jnp.int32),
        ]
        + [pltpu.VMEM((HALF, HALF), jnp.float32)] * 3
        + [pltpu.SemaphoreType.DMA((5,)), pltpu.SemaphoreType.DMA((AHEAD,))]
        + [pltpu.VMEM((ROWS, HALF), jnp.float32)] * ACCS
        + [pltpu.SMEM((X,), jnp.int32)] * AHEAD,
        compiler_params=pltpu.CompilerParams(vmem_limit_bytes=VMEM_BYTES),
    )(features, index, touched, owner)


def merge_kernel(
    upper, lower, out, upper_sum, lower_sum, upper_got, lower_got, upper_last, lower_last, send, recv, local
):
    g, t = lax.axis_index("gz"), lax.axis_index("xy")
    x, yz = lax.rem(t, ROW), lax.div(t, ROW)
    z, y = lax.rem(yz, 2), lax.div(yz, 2)
    zx = lax.rem(t, GROUP)
    loads = [
        pltpu.make_async_copy(upper.at[pl.ds(x * GROUP, GROUP)], upper_sum, local.at[0]),
        pltpu.make_async_copy(lower.at[pl.ds(y * GROUP, GROUP)], lower_sum, local.at[1]),
    ]
    for load in loads:
        load.start()

    def along_x(k):
        return lax.rem(x + k, ROW)

    def along_y(k):
        return lax.rem(y + k, ROW)

    def along_yz(k):
        return lax.rem(yz + k, GROUP)

    def along_zx(k):
        return lax.rem(zx + k, GROUP)

    barrier = pltpu.get_barrier_semaphore()

    def greet(peer):
        pl.semaphore_signal(barrier, inc=1, device_id=(g, peer), device_id_type=MESH)

    for k in range(1, ROW):
        greet(yz * ROW + along_x(k))
        greet(along_y(k) * GROUP + zx)
    for k in range(ROW):
        greet(along_y(k) * GROUP + (1 - z) * ROW + x)
    for k in range(1, ROW):
        greet(y * GROUP + (1 - z) * ROW + along_x(k))
    pl.semaphore_wait(barrier, 3 * (ROW - 1) + ROW)

    def copy(source, target, at, peer):
        return pltpu.make_async_remote_copy(
            src_ref=source,
            dst_ref=target,
            send_sem=send.at[at],
            recv_sem=recv.at[at],
            device_id=(g, peer),
            device_id_type=MESH,
        )

    def first_upper(k):
        source = upper.at[pl.ds(along_x(k) * GROUP, GROUP)]
        return copy(source, upper_got.at[k - 1], k - 1, yz * ROW + along_x(k))

    def first_lower(k):
        source = lower.at[pl.ds(along_y(k) * GROUP, GROUP)]
        return copy(source, lower_got.at[k - 1], ROW + k - 2, along_y(k) * GROUP + zx)

    def last_upper(k):
        source = upper_sum.at[along_yz(k)]
        return copy(source, upper_last.at[k - 1], 2 * (ROW - 1) + k - 1, along_yz(k) * ROW + x)

    def last_lower(k):
        source = lower_sum.at[along_zx(k)]
        return copy(source, lower_last.at[k - 1], 2 * (ROW - 1) + GROUP + k - 2, y * GROUP + along_zx(k))

    lane = lax.broadcasted_iota(jnp.int32, (PIECE, HALF), 1)
    row = lax.broadcasted_iota(jnp.int32, (PIECE, HALF), 0)
    upper_adds = lane >= 2 * FEATURES
    lower_adds = upper_adds | (row >= EB - PIECE)

    def join(adds, left, right):
        return jnp.where(adds, left + right, jnp.maximum(left, right))

    order = (2, 1, 3)
    for k in order:
        first_upper(k).start()
        first_lower(k).start()
    for load in loads:
        load.wait()

    def stage(adds, first, got, summed, last):
        for k in order:
            first(k).wait_recv()

        def one(b, carry):
            total = summed[b]
            for k in range(ROW - 1):
                total = join(adds, total, got[k, b])
            summed[b] = total
            return carry

        lax.fori_loop(0, GROUP, one, 0)
        for k in range(1, GROUP):
            last(k).start()

    stage(upper_adds, first_upper, upper_got, upper_sum, last_upper)
    stage(lower_adds, first_lower, lower_got, lower_sum, last_lower)

    def gather(adds, total, got, last):
        for k in range(1, GROUP):
            last(k).wait_recv()
            total = join(adds, total, got[k - 1])
        return total

    total = jnp.concatenate(
        [
            gather(upper_adds, upper_sum[yz], upper_last, last_upper),
            gather(lower_adds, lower_sum[zx], lower_last, last_lower),
        ],
        axis=0,
    )
    extremes, packed = total[:EB], total[EB:]
    rest = jnp.concatenate([pltpu.roll(packed, (HALF + 16 - 32 * j) % HALF, 1) for j in range(4)], axis=0)
    count = extremes[:, HALF - 1 :]
    present = count > 0.0
    lane = lax.broadcasted_iota(jnp.int32, (EB, HALF), 1)
    means = jnp.where(lane < 31, pltpu.roll(extremes, HALF - 2 * FEATURES, 1), rest) / jnp.maximum(count, 1.0)
    signed = jnp.where(present, jnp.where(lane < FEATURES, extremes, -extremes), 0.0)
    shifted = pltpu.roll(signed, FEATURES, 1)
    out[:, :HALF] = jnp.where(lane < FEATURES, means, shifted)
    out[:, HALF:] = shifted[:, : 3 * FEATURES - HALF]

    for k in order:
        first_upper(k).wait_send()
        first_lower(k).wait_send()
    for k in range(1, GROUP):
        last_upper(k).wait_send()
        last_lower(k).wait_send()


def merged_stats(upper, lower):
    hbm = pl.BlockSpec(memory_space=pltpu.HBM)
    copies = 2 * (ROW - 1) + 2 * (GROUP - 1)
    return pl.pallas_call(
        merge_kernel,
        out_shape=jax.ShapeDtypeStruct((EB, 3 * FEATURES), jnp.float32),
        in_specs=[hbm] * 2,
        out_specs=pl.BlockSpec(memory_space=pltpu.VMEM),
        scratch_shapes=[pltpu.VMEM((GROUP, PIECE, HALF), jnp.float32)] * 2
        + [pltpu.VMEM((ROW - 1, GROUP, PIECE, HALF), jnp.float32)] * 2
        + [pltpu.VMEM((GROUP - 1, PIECE, HALF), jnp.float32)] * 2
        + [
            pltpu.SemaphoreType.DMA((copies,)),
            pltpu.SemaphoreType.DMA((copies,)),
            pltpu.SemaphoreType.DMA((2,)),
        ],
        compiler_params=pltpu.CompilerParams(
            collective_id=1, has_side_effects=True, vmem_limit_bytes=VMEM_BYTES
        ),
    )(upper, lower)


def per_device(raw_volume, face_slot, touched, block_owner):
    features, index = filtered(raw_volume.reshape(C, ZY, X), face_slot.reshape(ZY, X))
    upper, lower = pooled(features, index.reshape(ZY, X), touched.reshape(-1), block_owner.reshape(-1))
    return merged_stats(upper, lower).T[None, None]


def solution(mesh):
    placed = (P(None, "gz", "xy", None), P("gz", "xy", None), P("gz", "xy", None), P("gz", None))
    return jax.shard_map(
        per_device, mesh=mesh, in_specs=placed, out_specs=P("gz", "xy", None, None), check_vma=False
    )
```

```python
import functools

import jax
import jax.numpy as jnp
import ml_dtypes
import numpy as np
from jax import lax
from jax.experimental import pallas as pl
from jax.experimental.pallas import tpu as pltpu
from jax.sharding import PartitionSpec as P

RADIUS = 8
C = 12
Z = 8
Y = 8
X = 256
EB = 64
TOUCH = 16
BLOCKS = 32
TILES = 32
SLABS = 4
ZY = Z * Y
HALF = X // 2
FEATURES = 4 * C
PARTS = 6
PART = C // PARTS
DIRECT = 3
CROSSED = 2
ACCS = 8
ROW = 4
SPARE = 8
ROWS = 2 * (TOUCH * EB + SPARE)
SENT = EB + EB // 4
PIECE = SENT // 2
GROUP = 8
CHUNK = 4
FAR = -1e30
STEP = ZY + 1
AHEAD = 4
VMEM_BYTES = 62 * 2**20
MESH = pl.DeviceIdType.MESH


def taps():
    sigma = np.float32(RADIUS / 3.0)
    offsets = np.arange(-RADIUS, RADIUS + 1).astype(np.float32)
    gauss = np.exp(-offsets * offsets / (2.0 * sigma * sigma)).astype(np.float32)
    gauss = gauss / gauss.sum()
    slope = -(offsets / sigma) * gauss
    curve = (offsets * offsets / (sigma * sigma) - 1.0) * gauss
    return [tap.astype(np.float64) for tap in (gauss, slope, curve)]


def two_terms(table):
    table = table.astype(np.float32)
    high = table.astype(ml_dtypes.bfloat16)
    low = (table - high.astype(np.float32)).astype(ml_dtypes.bfloat16)
    return high, low


def band(tap, size, start, stop):
    offset = np.arange(start, stop)[None, :] - np.arange(size)[:, None]
    return np.where(np.abs(offset) <= RADIUS, tap[np.clip(offset + RADIUS, 0, 2 * RADIUS)], 0.0)


def tables():
    gauss, slope, curve = taps()
    rows = []
    for kz, ky in ((gauss, gauss), (gauss, slope), (gauss, curve), (slope, gauss)):
        bz = band(kz, Z, -Z, 2 * Z).reshape(Z, 3, Z)
        by = band(ky, Y, -Y, 2 * Y).reshape(Y, 3, Y)
        rows.append(np.einsum("pdz,qey->pqdezy", bz, by).reshape(ZY, 9 * ZY))
    weights = np.concatenate(rows, axis=0).reshape(4 * ZY, 3, 3 * ZY)

    def both_terms(*blocks):
        return np.concatenate(two_terms(np.concatenate([weights[:, d + 1] for d in blocks], axis=1)), axis=0)

    near = np.stack([both_terms(0, 1), both_terms(0, -1)])
    far = np.stack([both_terms(-1), both_terms(1)])
    along = [two_terms(band(tap, X, 0, X).T) for tap in (gauss, slope, curve)]
    return near, far, np.concatenate([t[0] for t in along], 1), np.concatenate([t[1] for t in along], 1)


def split(values):
    high = values.astype(jnp.bfloat16)
    return high, (values - high.astype(jnp.float32)).astype(jnp.bfloat16)


def slot(dz, dt):
    return (dz + 1) * 3 + (dt + 1)


def filter_kernel(
    raw, faces_in, near_in, far_in, along_hi_in, along_lo_in, out, index,
    win, faces, partial, features, near, far, along_hi, along_lo, mixed_hi, mixed_lo, send, recv, local, stored,
):
    g, t = lax.axis_index("gz"), lax.axis_index("xy")
    odd = lax.rem(g, 2)
    mate = g + 1 - 2 * odd
    inner = (g == 1) | (g == 2)
    other = 3 - g
    has_left, has_right = t > 0, t < TILES - 1
    column = lax.rem(t, ROW)
    first_x, last_x = column == 0, column == ROW - 1
    second_x, third_x = column == 1, column == 2
    cross_left, cross_right = inner & first_x & has_left, inner & last_x & has_right

    loads = [
        pltpu.make_async_copy(source, target, local.at[k])
        for k, (source, target) in enumerate(
            (
                (raw, win.at[slot(0, 0)]),
                (faces_in.at[:, pl.ds(0, HALF)], faces.at[0]),
                (faces_in.at[:, pl.ds(HALF, HALF)], faces.at[1]),
                (near_in.at[odd], near),
                (far_in.at[odd], far),
                (along_hi_in, along_hi),
                (along_lo_in, along_lo),
            )
        )
    ]
    for load in loads:
        load.start()

    barrier = pltpu.get_barrier_semaphore()
    greeted = 0
    for condition, dg, dt in (
        (has_left, g, t - 1),
        (has_right, g, t + 1),
        (inner, other, t),
        (cross_left, other, t - 1),
        (cross_right, other, t + 1),
    ):
        @pl.when(condition)
        def _():
            pl.semaphore_signal(barrier, inc=1, device_id=(dg, dt), device_id_type=MESH)

        greeted += condition.astype(jnp.int32)
    pl.semaphore_signal(barrier, inc=1, device_id=(mate, t), device_id_type=MESH)
    pl.semaphore_wait(barrier, greeted + 1)

    def part(ref, q):
        return ref.at[pl.ds(q * PART, PART)]

    def copy(kind, q, source, target, dg, dt):
        return pltpu.make_async_remote_copy(
            src_ref=part(source, q),
            dst_ref=part(win.at[target], q),
            send_sem=send.at[kind, q],
            recv_sem=recv.at[kind, q],
            device_id=(dg, dt),
            device_id_type=MESH,
        )

    def copies(q):
        up = other - g

        def made(*args):
            return lambda: copy(*args)

        middle = inner & (second_x | third_x)
        direct, crossed = q < DIRECT, q < CROSSED
        from_left = inner & has_left & (second_x | (first_x & ~crossed))
        from_right = inner & has_right & (third_x | (last_x & ~crossed))
        left, right = win.at[slot(0, -1)], win.at[slot(0, 1)]
        third = win.at[slot(up, 0)]
        return (
            (made(0, q, raw, slot(0, -1), g, t + 1), has_right, has_left),
            (made(1, q, raw, slot(0, 1), g, t - 1), has_left, has_right),
            (made(2, q, raw, slot(g - mate, 0), mate, t), True, True),
            (made(3, q, raw, slot(g - other, 0), other, t), middle | (inner & direct), middle | (inner & direct)),
            (made(4, q, left, slot(g - mate, -1), mate, t), has_left, has_left),
            (made(5, q, right, slot(g - mate, 1), mate, t), has_right, has_right),
            (made(6, q, third, slot(up, -1), g, t + 1), middle, inner & (third_x | last_x)),
            (made(7, q, third, slot(up, 1), g, t - 1), middle, inner & (first_x | second_x)),
            (made(8, q, raw, slot(g - other, -1), other, t + 1), cross_right & crossed, cross_left & crossed),
            (made(9, q, raw, slot(g - other, 1), other, t - 1), cross_left & crossed, cross_right & crossed),
            (made(10, q, left, slot(g - other, -1), other, t), from_left, from_left),
            (made(11, q, right, slot(g - other, 1), other, t), from_right, from_right),
            (made(12, q, win.at[slot(up, -1)], slot(up, 0), g, t - 1), inner & second_x & ~direct, inner & first_x & ~direct),
            (made(13, q, win.at[slot(up, 1)], slot(up, 0), g, t + 1), inner & third_x & ~direct, inner & last_x & ~direct),
        )

    def start(q, kinds):
        for made, sent, _ in [copies(q)[k] for k in kinds]:
            pl.when(sent)(lambda made=made: made().start())

    def arrived(q, kinds, where=True):
        for made, _, received in [copies(q)[k] for k in kinds]:
            pl.when(received & where)(lambda made=made: made().wait_recv())

    def first(q, carry):
        start(q, (3, 0, 1, 8, 9, 2))
        return carry

    lax.fori_loop(0, PARTS, first, 0)

    def clear(target):
        def one(c, carry):
            win[target, c] = jnp.zeros((ZY, X), jnp.float32)
            return carry

        lax.fori_loop(0, C, one, 0)

    for d in (0, mate - g):
        pl.when(t == 0)(lambda d=d: clear(slot(d, -1)))
        pl.when(t == TILES - 1)(lambda d=d: clear(slot(d, 1)))
    pl.when(inner & (t == 0))(lambda: clear(slot(other - g, -1)))
    pl.when(inner & (t == TILES - 1))(lambda: clear(slot(other - g, 1)))
    for load in loads:
        load.wait()
    lane = lax.broadcasted_iota(jnp.int32, (ZY // 2, HALF), 1)
    spare = TOUCH * EB + lax.rem(lax.div(lane, ACCS), SPARE)
    for half in range(2):
        for k in range(2):
            found = faces[half, pl.ds(k, ZY // 2, stride=2), :]
            index[half, :, k * HALF : (k + 1) * HALF] = jnp.where(found < 0, spare, found) * 2

    def dot(a, b):
        return jnp.dot(a, b, preferred_element_type=jnp.float32)

    def across(weights, blocks, c):
        high, low = split(jnp.concatenate([win[block, c] for block in blocks], axis=0))
        both = dot(weights[...], high)
        return both[: 4 * ZY] + both[4 * ZY :] + dot(weights[: 4 * ZY], low)

    def forward(q):
        arrived(q, (0, 1))
        start(q, (4, 5, 10, 11))
        arrived(q, (3,), second_x | third_x)
        start(q, (6, 7))

    def begin(q):
        arrived(q, (2, 4, 5))
        for j in range(PART):
            c = q * PART + j
            partial[c] = across(near, [slot(d, dt) for d in (0, mate - g) for dt in (-1, 0, 1)], c)

    rows = PART * ZY

    def edge(k, q):
        row = (k * C + q * PART) * STEP
        return row // 8 * 8 if 0 < q < PARTS else (row + 7) // 8 * 8

    def stores(q):
        made = []
        for k in range(4):
            rows = pl.ds(edge(k, q), edge(k, q + 1) - edge(k, q))
            for half in range(2):
                made.append(
                    pltpu.make_async_copy(
                        features.at[half, rows], out.at[half, rows], stored.at[q, 2 * k + half]
                    )
                )
        return made

    def leave(q):
        for part_done in range(PARTS):
            @pl.when(q == part_done)
            def _():
                for made in stores(part_done):
                    made.start()

    def add_third(q):
        arrived(q, (3,), first_x | last_x)
        arrived(q, (6, 7, 8, 9, 12, 13))
        arrived(q, (10, 11), (q < DIRECT) | first_x | last_x)
        for j in range(PART):
            c = q * PART + j
            partial[c] += across(far, [slot(other - g, dt) for dt in (-1, 0, 1)], c)

    def end(q):
        for j in range(PART):
            high, low = split(partial[q * PART + j])
            for k in range(4):
                mixed_hi[k, j * ZY : (j + 1) * ZY, :] = high[k * ZY : (k + 1) * ZY]
                mixed_lo[k, j * ZY : (j + 1) * ZY, :] = low[k * ZY : (k + 1) * ZY]
        high, low = mixed_hi[...].reshape(4 * rows, X), mixed_lo[...].reshape(4 * rows, X)

        def along(n, k):
            columns = slice(k * X, (k + 1) * X)
            return (
                dot(high[:n], along_hi[:, columns])
                + dot(low[:n], along_hi[:, columns])
                + dot(high[:n], along_lo[:, columns])
            )

        by_gauss, by_slope, by_curve = along(4 * rows, 0), along(2 * rows, 1), along(rows, 2)
        smooth, grad_y, hess_yy, grad_z = (by_gauss[k * rows : (k + 1) * rows] for k in range(4))
        grad_x, hess_xy = by_slope[:rows], by_slope[rows:]
        half_trace = (hess_yy + by_curve) * 0.5
        spread = (hess_yy - by_curve) * 0.5
        deviation = jnp.sqrt(spread * spread + hess_xy * hess_xy)
        magnitude = jnp.sqrt(grad_z * grad_z + grad_y * grad_y + grad_x * grad_x)
        for k, value in enumerate((smooth, magnitude, half_trace + deviation, half_trace - deviation)):
            for j in range(PART):
                at = pl.ds((k * C + q * PART + j) * STEP, ZY)
                features[0, at, :] = value[j * ZY : (j + 1) * ZY, :HALF]
                features[1, at, :] = value[j * ZY : (j + 1) * ZY, HALF:]
        leave(q)

    forward(0)

    def near_work(q, carry):
        pl.when(q < PARTS)(lambda: forward(q))
        begin(q - 1)
        pl.when(~inner)(lambda: end(q - 1))
        return carry

    lax.fori_loop(1, PARTS + 1, near_work, 0)

    @pl.when(inner)
    def _():
        def pass_on(q, carry):
            arrived(q, (10, 11), second_x | third_x)
            start(q, (12, 13))
            return carry

        lax.fori_loop(DIRECT, PARTS, pass_on, 0)

        def far_work(q, carry):
            add_third(q)
            end(q)
            return carry

        lax.fori_loop(0, PARTS, far_work, 0)

    def finish(q, carry):
        for made, sent, _ in copies(q):
            pl.when(sent)(lambda made=made: made().wait_send())
        return carry

    lax.fori_loop(0, PARTS, finish, 0)
    for q in range(PARTS):
        for made in stores(q):
            made.wait()


def filtered(raw, faces):
    near, far, along_hi, along_lo = tables()
    hbm = pl.BlockSpec(memory_space=pltpu.HBM)
    return pl.pallas_call(
        filter_kernel,
        out_shape=(
            jax.ShapeDtypeStruct((2, FEATURES * STEP, HALF), jnp.float32),
            jax.ShapeDtypeStruct((2, ZY // 2, X), jnp.int32),
        ),
        in_specs=[hbm] * 6,
        out_specs=(hbm, pl.BlockSpec(memory_space=pltpu.VMEM)),
        scratch_shapes=[
            pltpu.VMEM((9, C, ZY, X), jnp.float32),
            pltpu.VMEM((2, ZY, HALF), jnp.int32),
            pltpu.VMEM((C, 4 * ZY, X), jnp.float32),
            pltpu.VMEM((2, FEATURES * STEP, HALF), jnp.float32),
            pltpu.VMEM(near.shape[1:], jnp.bfloat16),
            pltpu.VMEM(far.shape[1:], jnp.bfloat16),
            pltpu.VMEM(along_hi.shape, jnp.bfloat16),
            pltpu.VMEM(along_lo.shape, jnp.bfloat16),
            pltpu.VMEM((4, PART * ZY, X), jnp.bfloat16),
            pltpu.VMEM((4, PART * ZY, X), jnp.bfloat16),
            pltpu.SemaphoreType.DMA((14, PARTS)),
            pltpu.SemaphoreType.DMA((14, PARTS)),
            pltpu.SemaphoreType.DMA((7,)),
            pltpu.SemaphoreType.DMA((PARTS, 8)),
        ],
        compiler_params=pltpu.CompilerParams(
            collective_id=0, has_side_effects=True, vmem_limit_bytes=VMEM_BYTES
        ),
    )(raw, faces, *(jnp.asarray(table) for table in (near, far, along_hi, along_lo)))


def pool_kernel(
    features_in, index_in, touched_in, owner_in, upper, lower,
    empty_upper, empty_lower, full_upper, full_lower, cleared, placed,
    features, index, touched, owner, row_a, row_b, merged, local, ahead, *rest,
):
    accs, targets = rest[:ACCS], rest[ACCS:]
    loads = [
        pltpu.make_async_copy(source, target, local.at[k])
        for k, (source, target) in enumerate(
            (
                (index_in, index),
                (features_in.at[0], features.at[pl.ds(0, FEATURES * STEP)]),
                (features_in.at[1], features.at[pl.ds(FEATURES * STEP, FEATURES * STEP)]),
                (touched_in, touched),
                (owner_in, owner),
            )
        )
    ]
    for load in loads:
        load.start()

    def summed(rows):
        sub = lax.broadcasted_iota(jnp.int32, (rows, HALF), 0)
        lane = lax.broadcasted_iota(jnp.int32, (rows, HALF), 1)
        return (lax.rem(sub, 2) == 1) | (lane >= 2 * FEATURES)

    pair, tile = summed(2), summed(16)
    start = jnp.where(tile, 0.0, FAR)

    def reset(i, carry):
        for acc in accs:
            acc[pl.ds(i * 16, 16), :] = start
        return carry

    def fetch(k, row):
        return pltpu.make_async_copy(index.at[row], targets[k], ahead.at[k])

    lax.fori_loop(0, ROWS // 32, reset, 0)
    loads[0].wait()
    for k in range(AHEAD):
        fetch(k, k).start()
    lax.fori_loop(ROWS // 32, ROWS // 16, reset, 0)
    lane = lax.broadcasted_iota(jnp.int32, (PIECE, HALF), 1)
    row = lax.broadcasted_iota(jnp.int32, (PIECE, HALF), 0)
    empty = jnp.where(lane >= 2 * FEATURES, 0.0, FAR)

    def fill(b, carry):
        empty_upper[b] = empty
        empty_lower[b] = jnp.where(row < EB - PIECE, empty, 0.0)
        return carry

    lax.fori_loop(0, BLOCKS, fill, 0)
    clearings = [
        pltpu.make_async_copy(empty_upper, upper, cleared.at[0]),
        pltpu.make_async_copy(empty_lower, lower, cleared.at[1]),
    ]
    for clearing in clearings:
        clearing.start()
    ones = jnp.ones((1, HALF), jnp.float32)

    def turn(n, row):
        at = n + lax.div(n, ZY) * (FEATURES * STEP - ZY)
        values = features[pl.ds(at, FEATURES, stride=STEP), :]
        row[...] = jnp.concatenate([values, -values, values[:31], ones], axis=0).T

    def collect(target, first, row):
        for v in range(HALF):
            acc = accs[v % ACCS]
            at = pl.ds(target[first + v], 2)
            value = jnp.broadcast_to(row[v : v + 1, :], (2, HALF))
            old = acc[at, :]
            acc[at, :] = jnp.where(pair, old + value, jnp.maximum(old, value))

    loads[1].wait()
    turn(0, row_a)

    def body(i, carry):
        pl.when(i == ZY // (2 * AHEAD) - 1)(lambda: loads[2].wait())
        for k in range(AHEAD):
            n = i * AHEAD + k
            fetch(k, n).wait()
            turn(2 * n + 1, row_b)
            collect(targets[k], 0, row_a)
            turn(jnp.minimum(2 * n + 2, 2 * ZY - 1), row_a)
            collect(targets[k], HALF, row_b)
            pl.when(n + AHEAD < ZY)(lambda: fetch(k, n + AHEAD).start())
        return carry

    lax.fori_loop(0, ZY // AHEAD, body, 0)
    loads[3].wait()
    loads[4].wait()

    for clearing in clearings:
        clearing.wait()
    lane = lax.broadcasted_iota(jnp.int32, (EB // 4, HALF), 1)

    def place(i, carry):
        for k in range(2 * EB // 16):
            rows = pl.ds(pl.multiple_of(i * 2 * EB + k * 16, 16), 16)
            total = accs[0][rows, :]
            for acc in accs[1:]:
                more = acc[rows, :]
                total = jnp.where(tile, total + more, jnp.maximum(total, more))
            merged[pl.ds(k * 16, 16), :] = total
        to = owner[touched[i]]
        tile_x, tile_yz = lax.rem(to, ROW), lax.div(to, ROW)
        extremes = merged[pl.ds(0, EB, stride=2), :]
        full_upper[i] = extremes[:PIECE]
        full_lower[i, : EB - PIECE, :] = extremes[PIECE:]
        sums = merged[pl.ds(1, EB, stride=2), :]
        packed = jnp.zeros((EB // 4, HALF), jnp.float32)
        for j in range(4):
            group = pltpu.roll(sums[j * 16 : (j + 1) * 16], (32 * j - 16) % HALF, 1)
            packed = jnp.where((lane >= 32 * j) & (lane < 32 * j + 32), group, packed)
        full_lower[i, EB - PIECE :, :] = packed
        pltpu.make_async_copy(full_upper.at[i], upper.at[tile_x * GROUP + tile_yz], placed.at[0, i]).start()
        pltpu.make_async_copy(full_lower.at[i], lower.at[to], placed.at[1, i]).start()
        return carry

    lax.fori_loop(0, TOUCH, place, 0)

    def settle(i, carry):
        pltpu.make_async_copy(full_upper.at[i], upper.at[0], placed.at[0, i]).wait()
        pltpu.make_async_copy(full_lower.at[i], lower.at[0], placed.at[1, i]).wait()
        return carry

    lax.fori_loop(0, TOUCH, settle, 0)


def pooled(features, index, touched, owner):
    hbm = pl.BlockSpec(memory_space=pltpu.HBM)
    return pl.pallas_call(
        pool_kernel,
        out_shape=[jax.ShapeDtypeStruct((BLOCKS, PIECE, HALF), jnp.float32)] * 2,
        in_specs=[hbm] * 4,
        out_specs=[hbm] * 2,
        scratch_shapes=[pltpu.VMEM((BLOCKS, PIECE, HALF), jnp.float32)] * 2
        + [pltpu.VMEM((TOUCH, PIECE, HALF), jnp.float32)] * 2
        + [pltpu.SemaphoreType.DMA((2,)), pltpu.SemaphoreType.DMA((2, TOUCH))]
        + [
            pltpu.VMEM((2 * FEATURES * STEP, HALF), jnp.float32),
            pltpu.VMEM((ZY, X), jnp.int32),
            pltpu.SMEM((TOUCH,), jnp.int32),
            pltpu.SMEM((BLOCKS,), jnp.int32),
        ]
        + [pltpu.VMEM((HALF, HALF), jnp.float32)] * 3
        + [pltpu.SemaphoreType.DMA((5,)), pltpu.SemaphoreType.DMA((AHEAD,))]
        + [pltpu.VMEM((ROWS, HALF), jnp.float32)] * ACCS
        + [pltpu.SMEM((X,), jnp.int32)] * AHEAD,
        compiler_params=pltpu.CompilerParams(vmem_limit_bytes=VMEM_BYTES),
    )(features, index, touched, owner)


def merge_kernel(
    upper, lower, out, upper_sum, lower_sum, upper_got, lower_got, upper_last, lower_last, send, recv, local
):
    g, t = lax.axis_index("gz"), lax.axis_index("xy")
    x, yz = lax.rem(t, ROW), lax.div(t, ROW)
    z, y = lax.rem(yz, 2), lax.div(yz, 2)
    zx = lax.rem(t, GROUP)
    loads = [
        pltpu.make_async_copy(upper.at[pl.ds(x * GROUP, GROUP)], upper_sum, local.at[0]),
        pltpu.make_async_copy(lower.at[pl.ds(y * GROUP, GROUP)], lower_sum, local.at[1]),
    ]
    for load in loads:
        load.start()

    def along_x(k):
        return lax.rem(x + k, ROW)

    def along_y(k):
        return lax.rem(y + k, ROW)

    def along_yz(k):
        return lax.rem(yz + k, GROUP)

    def along_zx(k):
        return lax.rem(zx + k, GROUP)

    barrier = pltpu.get_barrier_semaphore()

    def greet(peer):
        pl.semaphore_signal(barrier, inc=1, device_id=(g, peer), device_id_type=MESH)

    for k in range(1, ROW):
        greet(yz * ROW + along_x(k))
        greet(along_y(k) * GROUP + zx)
    for k in range(ROW):
        greet(along_y(k) * GROUP + (1 - z) * ROW + x)
    for k in range(1, ROW):
        greet(y * GROUP + (1 - z) * ROW + along_x(k))
    pl.semaphore_wait(barrier, 3 * (ROW - 1) + ROW)

    def copy(source, target, at, peer):
        return pltpu.make_async_remote_copy(
            src_ref=source,
            dst_ref=target,
            send_sem=send.at[at],
            recv_sem=recv.at[at],
            device_id=(g, peer),
            device_id_type=MESH,
        )

    def first_upper(k, c):
        source = upper.at[pl.ds(along_x(k) * GROUP + c * CHUNK, CHUNK)]
        target = upper_got.at[k - 1, pl.ds(c * CHUNK, CHUNK)]
        return copy(source, target, 2 * (k - 1) + c, yz * ROW + along_x(k))

    def first_lower(k, c):
        source = lower.at[pl.ds(along_y(k) * GROUP + c * CHUNK, CHUNK)]
        target = lower_got.at[k - 1, pl.ds(c * CHUNK, CHUNK)]
        return copy(source, target, 2 * (ROW + k - 2) + c, along_y(k) * GROUP + zx)

    def last_upper(k):
        source = upper_sum.at[along_yz(k)]
        return copy(source, upper_last.at[k - 1], 4 * (ROW - 1) + k - 1, along_yz(k) * ROW + x)

    def last_lower(k):
        source = lower_sum.at[along_zx(k)]
        return copy(source, lower_last.at[k - 1], 4 * (ROW - 1) + GROUP + k - 2, y * GROUP + along_zx(k))

    lane = lax.broadcasted_iota(jnp.int32, (PIECE, HALF), 1)
    row = lax.broadcasted_iota(jnp.int32, (PIECE, HALF), 0)
    upper_adds = lane >= 2 * FEATURES
    lower_adds = upper_adds | (row >= EB - PIECE)

    def join(adds, left, right):
        return jnp.where(adds, left + right, jnp.maximum(left, right))

    order = (2, 1, 3)
    for c in range(2):
        for k in order:
            first_upper(k, c).start()
            first_lower(k, c).start()
    for load in loads:
        load.wait()

    def stage(c, adds, first, got, summed, last, mine):
        for k in order:
            first(k, c).wait_recv()

        def one(b, carry):
            total = summed[b]
            for k in range(ROW - 1):
                total = join(adds, total, got[k, b])
            summed[b] = total
            away = lax.rem(b - mine + GROUP, GROUP)
            pl.when(away != 0)(lambda: last(away).start())
            return carry

        lax.fori_loop(c * CHUNK, (c + 1) * CHUNK, one, 0)

    for c in range(2):
        stage(c, upper_adds, first_upper, upper_got, upper_sum, last_upper, yz)
        stage(c, lower_adds, first_lower, lower_got, lower_sum, last_lower, zx)

    def gather(adds, total, got, last):
        for k in range(1, GROUP):
            last(k).wait_recv()
            total = join(adds, total, got[k - 1])
        return total

    total = jnp.concatenate(
        [
            gather(upper_adds, upper_sum[yz], upper_last, last_upper),
            gather(lower_adds, lower_sum[zx], lower_last, last_lower),
        ],
        axis=0,
    )
    extremes, packed = total[:EB], total[EB:]
    rest = jnp.concatenate([pltpu.roll(packed, (HALF + 16 - 32 * j) % HALF, 1) for j in range(4)], axis=0)
    count = extremes[:, HALF - 1 :]
    present = count > 0.0
    lane = lax.broadcasted_iota(jnp.int32, (EB, HALF), 1)
    means = jnp.where(lane < 31, pltpu.roll(extremes, HALF - 2 * FEATURES, 1), rest) / jnp.maximum(count, 1.0)
    signed = jnp.where(present, jnp.where(lane < FEATURES, extremes, -extremes), 0.0)
    shifted = pltpu.roll(signed, FEATURES, 1)
    out[:, :HALF] = jnp.where(lane < FEATURES, means, shifted)
    out[:, HALF:] = shifted[:, : 3 * FEATURES - HALF]

    for k in order:
        for c in range(2):
            first_upper(k, c).wait_send()
            first_lower(k, c).wait_send()
    for k in range(1, GROUP):
        last_upper(k).wait_send()
        last_lower(k).wait_send()


def merged_stats(upper, lower):
    hbm = pl.BlockSpec(memory_space=pltpu.HBM)
    copies = 4 * (ROW - 1) + 2 * (GROUP - 1)
    return pl.pallas_call(
        merge_kernel,
        out_shape=jax.ShapeDtypeStruct((EB, 3 * FEATURES), jnp.float32),
        in_specs=[hbm] * 2,
        out_specs=pl.BlockSpec(memory_space=pltpu.VMEM),
        scratch_shapes=[pltpu.VMEM((GROUP, PIECE, HALF), jnp.float32)] * 2
        + [pltpu.VMEM((ROW - 1, GROUP, PIECE, HALF), jnp.float32)] * 2
        + [pltpu.VMEM((GROUP - 1, PIECE, HALF), jnp.float32)] * 2
        + [
            pltpu.SemaphoreType.DMA((copies,)),
            pltpu.SemaphoreType.DMA((copies,)),
            pltpu.SemaphoreType.DMA((2,)),
        ],
        compiler_params=pltpu.CompilerParams(
            collective_id=1, has_side_effects=True, vmem_limit_bytes=VMEM_BYTES
        ),
    )(upper, lower)


def per_device(raw_volume, face_slot, touched, block_owner):
    features, index = filtered(raw_volume.reshape(C, ZY, X), face_slot.reshape(ZY, X))
    upper, lower = pooled(features, index.reshape(ZY, X), touched.reshape(-1), block_owner.reshape(-1))
    return merged_stats(upper, lower).T[None, None]


def solution(mesh):
    placed = (P(None, "gz", "xy", None), P("gz", "xy", None), P("gz", "xy", None), P("gz", None))
    return jax.shard_map(
        per_device, mesh=mesh, in_specs=placed, out_specs=P("gz", "xy", None, None), check_vma=False
    )
```

```python
import functools

import jax
import jax.numpy as jnp
import ml_dtypes
import numpy as np
from jax import lax
from jax.experimental import pallas as pl
from jax.experimental.pallas import tpu as pltpu
from jax.sharding import PartitionSpec as P

RADIUS = 8
C = 12
Z = 8
Y = 8
X = 256
EB = 64
TOUCH = 16
BLOCKS = 32
TILES = 32
SLABS = 4
ZY = Z * Y
HALF = X // 2
FEATURES = 4 * C
PARTS = 6
PART = C // PARTS
DIRECT = 3
CROSSED = 2
ACCS = 8
ROW = 4
SPARE = 8
ROWS = 2 * (TOUCH * EB + SPARE)
SENT = EB + EB // 4
PIECE = SENT // 2
GROUP = 8
CHUNK = 4
FAR = -1e30
STEP = ZY + 1
AHEAD = 4
TOGETHER = 4
VMEM_BYTES = 62 * 2**20
MESH = pl.DeviceIdType.MESH


def taps():
    sigma = np.float32(RADIUS / 3.0)
    offsets = np.arange(-RADIUS, RADIUS + 1).astype(np.float32)
    gauss = np.exp(-offsets * offsets / (2.0 * sigma * sigma)).astype(np.float32)
    gauss = gauss / gauss.sum()
    slope = -(offsets / sigma) * gauss
    curve = (offsets * offsets / (sigma * sigma) - 1.0) * gauss
    return [tap.astype(np.float64) for tap in (gauss, slope, curve)]


def two_terms(table):
    table = table.astype(np.float32)
    high = table.astype(ml_dtypes.bfloat16)
    low = (table - high.astype(np.float32)).astype(ml_dtypes.bfloat16)
    return high, low


def band(tap, size, start, stop):
    offset = np.arange(start, stop)[None, :] - np.arange(size)[:, None]
    return np.where(np.abs(offset) <= RADIUS, tap[np.clip(offset + RADIUS, 0, 2 * RADIUS)], 0.0)


def tables():
    gauss, slope, curve = taps()
    rows = []
    for kz, ky in ((gauss, gauss), (gauss, slope), (gauss, curve), (slope, gauss)):
        bz = band(kz, Z, -Z, 2 * Z).reshape(Z, 3, Z)
        by = band(ky, Y, -Y, 2 * Y).reshape(Y, 3, Y)
        rows.append(np.einsum("pdz,qey->pqdezy", bz, by).reshape(ZY, 9 * ZY))
    weights = np.concatenate(rows, axis=0).reshape(4 * ZY, 3, 3 * ZY)

    def both_terms(*blocks):
        return np.concatenate(two_terms(np.concatenate([weights[:, d + 1] for d in blocks], axis=1)), axis=0)

    near = np.stack([both_terms(0, 1), both_terms(0, -1)])
    far = np.stack([both_terms(-1), both_terms(1)])
    along = [two_terms(band(tap, X, 0, X).T) for tap in (gauss, slope, curve)]
    return near, far, np.concatenate([t[0] for t in along], 1), np.concatenate([t[1] for t in along], 1)


def split(values):
    high = values.astype(jnp.bfloat16)
    return high, (values - high.astype(jnp.float32)).astype(jnp.bfloat16)


def slot(dz, dt):
    return (dz + 1) * 3 + (dt + 1)


def filter_kernel(
    raw, faces_in, near_in, far_in, along_hi_in, along_lo_in, out, index,
    win, faces, partial, features, near, far, along_hi, along_lo, mixed_hi, mixed_lo, send, recv, local, stored,
):
    g, t = lax.axis_index("gz"), lax.axis_index("xy")
    odd = lax.rem(g, 2)
    mate = g + 1 - 2 * odd
    inner = (g == 1) | (g == 2)
    other = 3 - g
    has_left, has_right = t > 0, t < TILES - 1
    column = lax.rem(t, ROW)
    first_x, last_x = column == 0, column == ROW - 1
    second_x, third_x = column == 1, column == 2
    cross_left, cross_right = inner & first_x & has_left, inner & last_x & has_right

    loads = [
        pltpu.make_async_copy(source, target, local.at[k])
        for k, (source, target) in enumerate(
            (
                (raw, win.at[slot(0, 0)]),
                (faces_in.at[:, pl.ds(0, HALF)], faces.at[0]),
                (faces_in.at[:, pl.ds(HALF, HALF)], faces.at[1]),
                (near_in.at[odd], near),
                (far_in.at[odd], far),
                (along_hi_in, along_hi),
                (along_lo_in, along_lo),
            )
        )
    ]
    for load in loads:
        load.start()

    barrier = pltpu.get_barrier_semaphore()
    greeted = 0
    for condition, dg, dt in (
        (has_left, g, t - 1),
        (has_right, g, t + 1),
        (inner, other, t),
        (cross_left, other, t - 1),
        (cross_right, other, t + 1),
    ):
        @pl.when(condition)
        def _():
            pl.semaphore_signal(barrier, inc=1, device_id=(dg, dt), device_id_type=MESH)

        greeted += condition.astype(jnp.int32)
    pl.semaphore_signal(barrier, inc=1, device_id=(mate, t), device_id_type=MESH)
    pl.semaphore_wait(barrier, greeted + 1)

    def part(ref, q):
        return ref.at[pl.ds(q * PART, PART)]

    def copy(kind, q, source, target, dg, dt):
        return pltpu.make_async_remote_copy(
            src_ref=part(source, q),
            dst_ref=part(win.at[target], q),
            send_sem=send.at[kind, q],
            recv_sem=recv.at[kind, q],
            device_id=(dg, dt),
            device_id_type=MESH,
        )

    def copies(q):
        up = other - g

        def made(*args):
            return lambda: copy(*args)

        middle = inner & (second_x | third_x)
        direct, crossed = q < DIRECT, q < CROSSED
        from_left = inner & has_left & (second_x | (first_x & ~crossed))
        from_right = inner & has_right & (third_x | (last_x & ~crossed))
        left, right = win.at[slot(0, -1)], win.at[slot(0, 1)]
        third = win.at[slot(up, 0)]
        return (
            (made(0, q, raw, slot(0, -1), g, t + 1), has_right, has_left),
            (made(1, q, raw, slot(0, 1), g, t - 1), has_left, has_right),
            (made(2, q, raw, slot(g - mate, 0), mate, t), True, True),
            (made(3, q, raw, slot(g - other, 0), other, t), middle | (inner & direct), middle | (inner & direct)),
            (made(4, q, left, slot(g - mate, -1), mate, t), has_left, has_left),
            (made(5, q, right, slot(g - mate, 1), mate, t), has_right, has_right),
            (made(6, q, third, slot(up, -1), g, t + 1), middle, inner & (third_x | last_x)),
            (made(7, q, third, slot(up, 1), g, t - 1), middle, inner & (first_x | second_x)),
            (made(8, q, raw, slot(g - other, -1), other, t + 1), cross_right & crossed, cross_left & crossed),
            (made(9, q, raw, slot(g - other, 1), other, t - 1), cross_left & crossed, cross_right & crossed),
            (made(10, q, left, slot(g - other, -1), other, t), from_left, from_left),
            (made(11, q, right, slot(g - other, 1), other, t), from_right, from_right),
            (made(12, q, win.at[slot(up, -1)], slot(up, 0), g, t - 1), inner & second_x & ~direct, inner & first_x & ~direct),
            (made(13, q, win.at[slot(up, 1)], slot(up, 0), g, t + 1), inner & third_x & ~direct, inner & last_x & ~direct),
        )

    def start(q, kinds):
        for made, sent, _ in [copies(q)[k] for k in kinds]:
            pl.when(sent)(lambda made=made: made().start())

    def arrived(q, kinds, where=True):
        for made, _, received in [copies(q)[k] for k in kinds]:
            pl.when(received & where)(lambda made=made: made().wait_recv())

    def first(q, carry):
        start(q, (3, 0, 1, 8, 9, 2))
        return carry

    lax.fori_loop(0, PARTS, first, 0)

    def clear(target):
        def one(c, carry):
            win[target, c] = jnp.zeros((ZY, X), jnp.float32)
            return carry

        lax.fori_loop(0, C, one, 0)

    for d in (0, mate - g):
        pl.when(t == 0)(lambda d=d: clear(slot(d, -1)))
        pl.when(t == TILES - 1)(lambda d=d: clear(slot(d, 1)))
    pl.when(inner & (t == 0))(lambda: clear(slot(other - g, -1)))
    pl.when(inner & (t == TILES - 1))(lambda: clear(slot(other - g, 1)))
    for load in loads:
        load.wait()
    lane = lax.broadcasted_iota(jnp.int32, (ZY // 2, HALF), 1)
    spare = TOUCH * EB + lax.rem(lax.div(lane, ACCS), SPARE)
    for half in range(2):
        for k in range(2):
            found = faces[half, pl.ds(k, ZY // 2, stride=2), :]
            index[half, :, k * HALF : (k + 1) * HALF] = jnp.where(found < 0, spare, found) * 2

    def dot(a, b):
        return jnp.dot(a, b, preferred_element_type=jnp.float32)

    def across(weights, blocks, c):
        high, low = split(jnp.concatenate([win[block, c] for block in blocks], axis=0))
        both = dot(weights[...], high)
        return both[: 4 * ZY] + both[4 * ZY :] + dot(weights[: 4 * ZY], low)

    def forward(q):
        arrived(q, (0, 1))
        start(q, (4, 5, 10, 11))
        arrived(q, (3,), second_x | third_x)
        start(q, (6, 7))

    def begin(q):
        arrived(q, (2, 4, 5))
        for j in range(PART):
            c = q * PART + j
            partial[c] = across(near, [slot(d, dt) for d in (0, mate - g) for dt in (-1, 0, 1)], c)

    rows = PART * ZY

    def edge(k, q):
        row = (k * C + q * PART) * STEP
        return row // 8 * 8 if 0 < q < PARTS else (row + 7) // 8 * 8

    def stores(q):
        made = []
        for k in range(4):
            rows = pl.ds(edge(k, q), edge(k, q + 1) - edge(k, q))
            for half in range(2):
                made.append(
                    pltpu.make_async_copy(
                        features.at[half, rows], out.at[half, rows], stored.at[q, 2 * k + half]
                    )
                )
        return made

    def leave(q):
        for part_done in range(PARTS):
            @pl.when(q == part_done)
            def _():
                for made in stores(part_done):
                    made.start()

    def add_third(q):
        arrived(q, (3,), first_x | last_x)
        arrived(q, (6, 7, 8, 9, 12, 13))
        arrived(q, (10, 11), (q < DIRECT) | first_x | last_x)
        for j in range(PART):
            c = q * PART + j
            partial[c] += across(far, [slot(other - g, dt) for dt in (-1, 0, 1)], c)

    def end(q):
        for j in range(PART):
            high, low = split(partial[q * PART + j])
            for k in range(4):
                mixed_hi[k, j * ZY : (j + 1) * ZY, :] = high[k * ZY : (k + 1) * ZY]
                mixed_lo[k, j * ZY : (j + 1) * ZY, :] = low[k * ZY : (k + 1) * ZY]
        high, low = mixed_hi[...].reshape(4 * rows, X), mixed_lo[...].reshape(4 * rows, X)

        def along(n, k):
            columns = slice(k * X, (k + 1) * X)
            return (
                dot(high[:n], along_hi[:, columns])
                + dot(low[:n], along_hi[:, columns])
                + dot(high[:n], along_lo[:, columns])
            )

        by_gauss, by_slope, by_curve = along(4 * rows, 0), along(2 * rows, 1), along(rows, 2)
        smooth, grad_y, hess_yy, grad_z = (by_gauss[k * rows : (k + 1) * rows] for k in range(4))
        grad_x, hess_xy = by_slope[:rows], by_slope[rows:]
        half_trace = (hess_yy + by_curve) * 0.5
        spread = (hess_yy - by_curve) * 0.5
        deviation = jnp.sqrt(spread * spread + hess_xy * hess_xy)
        magnitude = jnp.sqrt(grad_z * grad_z + grad_y * grad_y + grad_x * grad_x)
        for k, value in enumerate((smooth, magnitude, half_trace + deviation, half_trace - deviation)):
            for j in range(PART):
                at = pl.ds((k * C + q * PART + j) * STEP, ZY)
                features[0, at, :] = value[j * ZY : (j + 1) * ZY, :HALF]
                features[1, at, :] = value[j * ZY : (j + 1) * ZY, HALF:]
        leave(q)

    forward(0)

    def near_work(q, carry):
        pl.when(q < PARTS)(lambda: forward(q))
        begin(q - 1)
        pl.when(~inner)(lambda: end(q - 1))
        return carry

    lax.fori_loop(1, PARTS + 1, near_work, 0)

    @pl.when(inner)
    def _():
        def pass_on(q, carry):
            arrived(q, (10, 11), second_x | third_x)
            start(q, (12, 13))
            return carry

        lax.fori_loop(DIRECT, PARTS, pass_on, 0)

        def far_work(q, carry):
            add_third(q)
            end(q)
            return carry

        lax.fori_loop(0, PARTS, far_work, 0)

    def finish(q, carry):
        for made, sent, _ in copies(q):
            pl.when(sent)(lambda made=made: made().wait_send())
        return carry

    lax.fori_loop(0, PARTS, finish, 0)
    for q in range(PARTS):
        for made in stores(q):
            made.wait()


def filtered(raw, faces):
    near, far, along_hi, along_lo = tables()
    hbm = pl.BlockSpec(memory_space=pltpu.HBM)
    return pl.pallas_call(
        filter_kernel,
        out_shape=(
            jax.ShapeDtypeStruct((2, FEATURES * STEP, HALF), jnp.float32),
            jax.ShapeDtypeStruct((2, ZY // 2, X), jnp.int32),
        ),
        in_specs=[hbm] * 6,
        out_specs=(hbm, pl.BlockSpec(memory_space=pltpu.VMEM)),
        scratch_shapes=[
            pltpu.VMEM((9, C, ZY, X), jnp.float32),
            pltpu.VMEM((2, ZY, HALF), jnp.int32),
            pltpu.VMEM((C, 4 * ZY, X), jnp.float32),
            pltpu.VMEM((2, FEATURES * STEP, HALF), jnp.float32),
            pltpu.VMEM(near.shape[1:], jnp.bfloat16),
            pltpu.VMEM(far.shape[1:], jnp.bfloat16),
            pltpu.VMEM(along_hi.shape, jnp.bfloat16),
            pltpu.VMEM(along_lo.shape, jnp.bfloat16),
            pltpu.VMEM((4, PART * ZY, X), jnp.bfloat16),
            pltpu.VMEM((4, PART * ZY, X), jnp.bfloat16),
            pltpu.SemaphoreType.DMA((14, PARTS)),
            pltpu.SemaphoreType.DMA((14, PARTS)),
            pltpu.SemaphoreType.DMA((7,)),
            pltpu.SemaphoreType.DMA((PARTS, 8)),
        ],
        compiler_params=pltpu.CompilerParams(
            collective_id=0, has_side_effects=True, vmem_limit_bytes=VMEM_BYTES
        ),
    )(raw, faces, *(jnp.asarray(table) for table in (near, far, along_hi, along_lo)))


def pool_kernel(
    features_in, index_in, touched_in, owner_in, upper, lower,
    empty_upper, empty_lower, full_upper, full_lower, cleared, placed,
    features, index, touched, owner, row_a, row_b, merged, local, ahead, *rest,
):
    accs, targets = rest[:ACCS], rest[ACCS:]
    for k in range(AHEAD):
        pltpu.make_async_copy(index_in.at[k], targets[k], ahead.at[k]).start()
    loads = [
        pltpu.make_async_copy(source, target, local.at[k])
        for k, (source, target) in enumerate(
            (
                (index_in, index),
                (features_in.at[0], features.at[pl.ds(0, FEATURES * STEP)]),
                (features_in.at[1], features.at[pl.ds(FEATURES * STEP, FEATURES * STEP)]),
                (touched_in, touched),
                (owner_in, owner),
            )
        )
    ]
    for load in loads:
        load.start()

    def summed(rows):
        sub = lax.broadcasted_iota(jnp.int32, (rows, HALF), 0)
        lane = lax.broadcasted_iota(jnp.int32, (rows, HALF), 1)
        return (lax.rem(sub, 2) == 1) | (lane >= 2 * FEATURES)

    pair, tile = summed(2), summed(16)
    start = jnp.where(tile, 0.0, FAR)

    def reset(i, carry):
        for acc in accs:
            acc[pl.ds(i * 16, 16), :] = start
        return carry

    def fetch(k, row):
        return pltpu.make_async_copy(index.at[row], targets[k], ahead.at[k])

    lax.fori_loop(0, ROWS // 16, reset, 0)
    lane = lax.broadcasted_iota(jnp.int32, (PIECE, HALF), 1)
    row = lax.broadcasted_iota(jnp.int32, (PIECE, HALF), 0)
    empty = jnp.where(lane >= 2 * FEATURES, 0.0, FAR)

    def fill(b, carry):
        empty_upper[b] = empty
        empty_lower[b] = jnp.where(row < EB - PIECE, empty, 0.0)
        return carry

    lax.fori_loop(0, BLOCKS, fill, 0)
    clearings = [
        pltpu.make_async_copy(empty_upper, upper, cleared.at[0]),
        pltpu.make_async_copy(empty_lower, lower, cleared.at[1]),
    ]
    for clearing in clearings:
        clearing.start()
    ones = jnp.ones((1, HALF), jnp.float32)

    def turn(n, row):
        at = n + lax.div(n, ZY) * (FEATURES * STEP - ZY)
        values = features[pl.ds(at, FEATURES, stride=STEP), :]
        row[...] = jnp.concatenate([values, -values, values[:31], ones], axis=0).T

    def collect(target, first, row):
        for v in range(HALF):
            acc = accs[v % ACCS]
            at = pl.ds(target[first + v], 2)
            value = jnp.broadcast_to(row[v : v + 1, :], (2, HALF))
            old = acc[at, :]
            acc[at, :] = jnp.where(pair, old + value, jnp.maximum(old, value))

    loads[0].wait()
    loads[1].wait()
    turn(0, row_a)

    def body(i, carry):
        pl.when(i == ZY // (2 * AHEAD) - 1)(lambda: loads[2].wait())
        for k in range(AHEAD):
            n = i * AHEAD + k
            fetch(k, n).wait()
            turn(2 * n + 1, row_b)
            collect(targets[k], 0, row_a)
            turn(jnp.minimum(2 * n + 2, 2 * ZY - 1), row_a)
            collect(targets[k], HALF, row_b)
            pl.when(n + AHEAD < ZY)(lambda: fetch(k, n + AHEAD).start())
        return carry

    lax.fori_loop(0, ZY // AHEAD, body, 0)
    loads[3].wait()
    loads[4].wait()

    for clearing in clearings:
        clearing.wait()
    lane = lax.broadcasted_iota(jnp.int32, (EB // 4, HALF), 1)

    def place(n, carry):
        for u in range(TOGETHER):
            for k in range(2 * EB // 16):
                rows = pl.ds(pl.multiple_of((n * TOGETHER + u) * 2 * EB + k * 16, 16), 16)
                total = accs[0][rows, :]
                for acc in accs[1:]:
                    more = acc[rows, :]
                    total = jnp.where(tile, total + more, jnp.maximum(total, more))
                merged[pl.ds(u * 2 * EB + k * 16, 16), :] = total
        for u in range(TOGETHER):
            i = n * TOGETHER + u
            extremes = merged[pl.ds(u * 2 * EB, EB, stride=2), :]
            full_upper[i] = extremes[:PIECE]
            full_lower[i, : EB - PIECE, :] = extremes[PIECE:]
            sums = merged[pl.ds(u * 2 * EB + 1, EB, stride=2), :]
            packed = jnp.zeros((EB // 4, HALF), jnp.float32)
            for j in range(4):
                group = pltpu.roll(sums[j * 16 : (j + 1) * 16], (32 * j - 16) % HALF, 1)
                packed = jnp.where((lane >= 32 * j) & (lane < 32 * j + 32), group, packed)
            full_lower[i, EB - PIECE :, :] = packed
        for u in range(TOGETHER):
            i = n * TOGETHER + u
            to = owner[touched[i]]
            tile_x, tile_yz = lax.rem(to, ROW), lax.div(to, ROW)
            pltpu.make_async_copy(full_upper.at[i], upper.at[tile_x * GROUP + tile_yz], placed.at[0, i]).start()
            pltpu.make_async_copy(full_lower.at[i], lower.at[to], placed.at[1, i]).start()
        return carry

    lax.fori_loop(0, TOUCH // TOGETHER, place, 0)

    def settle(i, carry):
        pltpu.make_async_copy(full_upper.at[i], upper.at[0], placed.at[0, i]).wait()
        pltpu.make_async_copy(full_lower.at[i], lower.at[0], placed.at[1, i]).wait()
        return carry

    lax.fori_loop(0, TOUCH, settle, 0)


def pooled(features, index, touched, owner):
    hbm = pl.BlockSpec(memory_space=pltpu.HBM)
    return pl.pallas_call(
        pool_kernel,
        out_shape=[jax.ShapeDtypeStruct((BLOCKS, PIECE, HALF), jnp.float32)] * 2,
        in_specs=[hbm] * 4,
        out_specs=[hbm] * 2,
        scratch_shapes=[pltpu.VMEM((BLOCKS, PIECE, HALF), jnp.float32)] * 2
        + [pltpu.VMEM((TOUCH, PIECE, HALF), jnp.float32)] * 2
        + [pltpu.SemaphoreType.DMA((2,)), pltpu.SemaphoreType.DMA((2, TOUCH))]
        + [
            pltpu.VMEM((2 * FEATURES * STEP, HALF), jnp.float32),
            pltpu.VMEM((ZY, X), jnp.int32),
            pltpu.SMEM((TOUCH,), jnp.int32),
            pltpu.SMEM((BLOCKS,), jnp.int32),
        ]
        + [pltpu.VMEM((HALF, HALF), jnp.float32)] * 2
        + [pltpu.VMEM((TOGETHER * HALF, HALF), jnp.float32)]
        + [pltpu.SemaphoreType.DMA((5,)), pltpu.SemaphoreType.DMA((AHEAD,))]
        + [pltpu.VMEM((ROWS, HALF), jnp.float32)] * ACCS
        + [pltpu.SMEM((X,), jnp.int32)] * AHEAD,
        compiler_params=pltpu.CompilerParams(vmem_limit_bytes=VMEM_BYTES),
    )(features, index, touched, owner)


def merge_kernel(
    upper, lower, out, upper_sum, lower_sum, upper_got, lower_got, upper_last, lower_last, send, recv, local
):
    g, t = lax.axis_index("gz"), lax.axis_index("xy")
    x, yz = lax.rem(t, ROW), lax.div(t, ROW)
    z, y = lax.rem(yz, 2), lax.div(yz, 2)
    zx = lax.rem(t, GROUP)
    loads = [
        pltpu.make_async_copy(upper.at[pl.ds(x * GROUP, GROUP)], upper_sum, local.at[0]),
        pltpu.make_async_copy(lower.at[pl.ds(y * GROUP, GROUP)], lower_sum, local.at[1]),
    ]
    for load in loads:
        load.start()

    def along_x(k):
        return lax.rem(x + k, ROW)

    def along_y(k):
        return lax.rem(y + k, ROW)

    def along_yz(k):
        return lax.rem(yz + k, GROUP)

    def along_zx(k):
        return lax.rem(zx + k, GROUP)

    barrier = pltpu.get_barrier_semaphore()

    def greet(peer):
        pl.semaphore_signal(barrier, inc=1, device_id=(g, peer), device_id_type=MESH)

    for k in range(1, ROW):
        greet(yz * ROW + along_x(k))
        greet(along_y(k) * GROUP + zx)
    for k in range(ROW):
        greet(along_y(k) * GROUP + (1 - z) * ROW + x)
    for k in range(1, ROW):
        greet(y * GROUP + (1 - z) * ROW + along_x(k))
    pl.semaphore_wait(barrier, 3 * (ROW - 1) + ROW)

    def copy(source, target, at, peer):
        return pltpu.make_async_remote_copy(
            src_ref=source,
            dst_ref=target,
            send_sem=send.at[at],
            recv_sem=recv.at[at],
            device_id=(g, peer),
            device_id_type=MESH,
        )

    def first_upper(k, c):
        source = upper.at[pl.ds(along_x(k) * GROUP + c * CHUNK, CHUNK)]
        target = upper_got.at[k - 1, pl.ds(c * CHUNK, CHUNK)]
        return copy(source, target, 2 * (k - 1) + c, yz * ROW + along_x(k))

    def first_lower(k, c):
        source = lower.at[pl.ds(along_y(k) * GROUP + c * CHUNK, CHUNK)]
        target = lower_got.at[k - 1, pl.ds(c * CHUNK, CHUNK)]
        return copy(source, target, 2 * (ROW + k - 2) + c, along_y(k) * GROUP + zx)

    def last_upper(k):
        source = upper_sum.at[along_yz(k)]
        return copy(source, upper_last.at[k - 1], 4 * (ROW - 1) + k - 1, along_yz(k) * ROW + x)

    def last_lower(k):
        source = lower_sum.at[along_zx(k)]
        return copy(source, lower_last.at[k - 1], 4 * (ROW - 1) + GROUP + k - 2, y * GROUP + along_zx(k))

    lane = lax.broadcasted_iota(jnp.int32, (PIECE, HALF), 1)
    row = lax.broadcasted_iota(jnp.int32, (PIECE, HALF), 0)
    upper_adds = lane >= 2 * FEATURES
    lower_adds = upper_adds | (row >= EB - PIECE)

    def join(adds, left, right):
        return jnp.where(adds, left + right, jnp.maximum(left, right))

    order = (2, 1, 3)
    for c in range(2):
        for k in order:
            first_upper(k, c).start()
            first_lower(k, c).start()
    for load in loads:
        load.wait()

    def stage(c, adds, first, got, summed, last, mine):
        for k in order:
            first(k, c).wait_recv()

        def one(b, carry):
            total = summed[b]
            for k in range(ROW - 1):
                total = join(adds, total, got[k, b])
            summed[b] = total
            away = lax.rem(b - mine + GROUP, GROUP)
            pl.when(away != 0)(lambda: last(away).start())
            return carry

        lax.fori_loop(c * CHUNK, (c + 1) * CHUNK, one, 0)

    for c in range(2):
        stage(c, upper_adds, first_upper, upper_got, upper_sum, last_upper, yz)
        stage(c, lower_adds, first_lower, lower_got, lower_sum, last_lower, zx)

    def gather(adds, total, got, last):
        for k in range(1, GROUP):
            last(k).wait_recv()
            total = join(adds, total, got[k - 1])
        return total

    total = jnp.concatenate(
        [
            gather(upper_adds, upper_sum[yz], upper_last, last_upper),
            gather(lower_adds, lower_sum[zx], lower_last, last_lower),
        ],
        axis=0,
    )
    extremes, packed = total[:EB], total[EB:]
    rest = jnp.concatenate([pltpu.roll(packed, (HALF + 16 - 32 * j) % HALF, 1) for j in range(4)], axis=0)
    count = extremes[:, HALF - 1 :]
    present = count > 0.0
    lane = lax.broadcasted_iota(jnp.int32, (EB, HALF), 1)
    means = jnp.where(lane < 31, pltpu.roll(extremes, HALF - 2 * FEATURES, 1), rest) / jnp.maximum(count, 1.0)
    signed = jnp.where(present, jnp.where(lane < FEATURES, extremes, -extremes), 0.0)
    shifted = pltpu.roll(signed, FEATURES, 1)
    out[:, :HALF] = jnp.where(lane < FEATURES, means, shifted)
    out[:, HALF:] = shifted[:, : 3 * FEATURES - HALF]

    for k in order:
        for c in range(2):
            first_upper(k, c).wait_send()
            first_lower(k, c).wait_send()
    for k in range(1, GROUP):
        last_upper(k).wait_send()
        last_lower(k).wait_send()


def merged_stats(upper, lower):
    hbm = pl.BlockSpec(memory_space=pltpu.HBM)
    copies = 4 * (ROW - 1) + 2 * (GROUP - 1)
    return pl.pallas_call(
        merge_kernel,
        out_shape=jax.ShapeDtypeStruct((EB, 3 * FEATURES), jnp.float32),
        in_specs=[hbm] * 2,
        out_specs=pl.BlockSpec(memory_space=pltpu.VMEM),
        scratch_shapes=[pltpu.VMEM((GROUP, PIECE, HALF), jnp.float32)] * 2
        + [pltpu.VMEM((ROW - 1, GROUP, PIECE, HALF), jnp.float32)] * 2
        + [pltpu.VMEM((GROUP - 1, PIECE, HALF), jnp.float32)] * 2
        + [
            pltpu.SemaphoreType.DMA((copies,)),
            pltpu.SemaphoreType.DMA((copies,)),
            pltpu.SemaphoreType.DMA((2,)),
        ],
        compiler_params=pltpu.CompilerParams(
            collective_id=1, has_side_effects=True, vmem_limit_bytes=VMEM_BYTES
        ),
    )(upper, lower)


def per_device(raw_volume, face_slot, touched, block_owner):
    features, index = filtered(raw_volume.reshape(C, ZY, X), face_slot.reshape(ZY, X))
    upper, lower = pooled(features, index.reshape(ZY, X), touched.reshape(-1), block_owner.reshape(-1))
    return merged_stats(upper, lower).T[None, None]


def solution(mesh):
    placed = (P(None, "gz", "xy", None), P("gz", "xy", None), P("gz", "xy", None), P("gz", None))
    return jax.shard_map(
        per_device, mesh=mesh, in_specs=placed, out_specs=P("gz", "xy", None, None), check_vma=False
    )
```

```python
import functools

import jax
import jax.numpy as jnp
import ml_dtypes
import numpy as np
from jax import lax
from jax.experimental import pallas as pl
from jax.experimental.pallas import tpu as pltpu
from jax.sharding import PartitionSpec as P

RADIUS = 8
C = 12
Z = 8
Y = 8
X = 256
EB = 64
TOUCH = 16
BLOCKS = 32
TILES = 32
SLABS = 4
ZY = Z * Y
HALF = X // 2
FEATURES = 4 * C
PARTS = 6
PART = C // PARTS
DIRECT = 3
CROSSED = 2
ACCS = 8
ROW = 4
SPARE = 8
ROWS = 2 * (TOUCH * EB + SPARE)
SENT = EB + EB // 4
PIECE = SENT // 2
GROUP = 8
CHUNK = 4
FAR = -1e30
STEP = ZY + 1
AHEAD = 4
TOGETHER = 4
VMEM_BYTES = 62 * 2**20
MERGE_BYTES = 107 * 2**19
MESH = pl.DeviceIdType.MESH


def taps():
    sigma = np.float32(RADIUS / 3.0)
    offsets = np.arange(-RADIUS, RADIUS + 1).astype(np.float32)
    gauss = np.exp(-offsets * offsets / (2.0 * sigma * sigma)).astype(np.float32)
    gauss = gauss / gauss.sum()
    slope = -(offsets / sigma) * gauss
    curve = (offsets * offsets / (sigma * sigma) - 1.0) * gauss
    return [tap.astype(np.float64) for tap in (gauss, slope, curve)]


def two_terms(table):
    table = table.astype(np.float32)
    high = table.astype(ml_dtypes.bfloat16)
    low = (table - high.astype(np.float32)).astype(ml_dtypes.bfloat16)
    return high, low


def band(tap, size, start, stop):
    offset = np.arange(start, stop)[None, :] - np.arange(size)[:, None]
    return np.where(np.abs(offset) <= RADIUS, tap[np.clip(offset + RADIUS, 0, 2 * RADIUS)], 0.0)


def tables():
    gauss, slope, curve = taps()
    rows = []
    for kz, ky in ((gauss, gauss), (gauss, slope), (gauss, curve), (slope, gauss)):
        bz = band(kz, Z, -Z, 2 * Z).reshape(Z, 3, Z)
        by = band(ky, Y, -Y, 2 * Y).reshape(Y, 3, Y)
        rows.append(np.einsum("pdz,qey->pqdezy", bz, by).reshape(ZY, 9 * ZY))
    weights = np.concatenate(rows, axis=0).reshape(4 * ZY, 3, 3 * ZY)

    def both_terms(*blocks):
        return np.concatenate(two_terms(np.concatenate([weights[:, d + 1] for d in blocks], axis=1)), axis=0)

    near = np.stack([both_terms(0, 1), both_terms(0, -1)])
    far = np.stack([both_terms(-1), both_terms(1)])
    along = [two_terms(band(tap, X, 0, X).T) for tap in (gauss, slope, curve)]
    return near, far, np.concatenate([t[0] for t in along], 1), np.concatenate([t[1] for t in along], 1)


def split(values):
    high = values.astype(jnp.bfloat16)
    return high, (values - high.astype(jnp.float32)).astype(jnp.bfloat16)


def slot(dz, dt):
    return (dz + 1) * 3 + (dt + 1)


def filter_kernel(
    raw, faces_in, near_in, far_in, along_hi_in, along_lo_in, out, index,
    win, faces, partial, features, near, far, along_hi, along_lo, mixed_hi, mixed_lo, send, recv, local, stored,
):
    g, t = lax.axis_index("gz"), lax.axis_index("xy")
    odd = lax.rem(g, 2)
    mate = g + 1 - 2 * odd
    inner = (g == 1) | (g == 2)
    other = 3 - g
    has_left, has_right = t > 0, t < TILES - 1
    column = lax.rem(t, ROW)
    first_x, last_x = column == 0, column == ROW - 1
    second_x, third_x = column == 1, column == 2
    cross_left, cross_right = inner & first_x & has_left, inner & last_x & has_right

    loads = [
        pltpu.make_async_copy(source, target, local.at[k])
        for k, (source, target) in enumerate(
            (
                (raw, win.at[slot(0, 0)]),
                (faces_in.at[:, pl.ds(0, HALF)], faces.at[0]),
                (faces_in.at[:, pl.ds(HALF, HALF)], faces.at[1]),
                (near_in.at[odd], near),
                (far_in.at[odd], far),
                (along_hi_in, along_hi),
                (along_lo_in, along_lo),
            )
        )
    ]
    for load in loads:
        load.start()

    barrier = pltpu.get_barrier_semaphore()
    greeted = 0
    for condition, dg, dt in (
        (has_left, g, t - 1),
        (has_right, g, t + 1),
        (inner, other, t),
        (cross_left, other, t - 1),
        (cross_right, other, t + 1),
    ):
        @pl.when(condition)
        def _():
            pl.semaphore_signal(barrier, inc=1, device_id=(dg, dt), device_id_type=MESH)

        greeted += condition.astype(jnp.int32)
    pl.semaphore_signal(barrier, inc=1, device_id=(mate, t), device_id_type=MESH)
    pl.semaphore_wait(barrier, greeted + 1)

    def part(ref, q):
        return ref.at[pl.ds(q * PART, PART)]

    def copy(kind, q, source, target, dg, dt):
        return pltpu.make_async_remote_copy(
            src_ref=part(source, q),
            dst_ref=part(win.at[target], q),
            send_sem=send.at[kind, q],
            recv_sem=recv.at[kind, q],
            device_id=(dg, dt),
            device_id_type=MESH,
        )

    def copies(q):
        up = other - g

        def made(*args):
            return lambda: copy(*args)

        middle = inner & (second_x | third_x)
        direct, crossed = q < DIRECT, q < CROSSED
        from_left = inner & has_left & (second_x | (first_x & ~crossed))
        from_right = inner & has_right & (third_x | (last_x & ~crossed))
        left, right = win.at[slot(0, -1)], win.at[slot(0, 1)]
        third = win.at[slot(up, 0)]
        return (
            (made(0, q, raw, slot(0, -1), g, t + 1), has_right, has_left),
            (made(1, q, raw, slot(0, 1), g, t - 1), has_left, has_right),
            (made(2, q, raw, slot(g - mate, 0), mate, t), True, True),
            (made(3, q, raw, slot(g - other, 0), other, t), middle | (inner & direct), middle | (inner & direct)),
            (made(4, q, left, slot(g - mate, -1), mate, t), has_left, has_left),
            (made(5, q, right, slot(g - mate, 1), mate, t), has_right, has_right),
            (made(6, q, third, slot(up, -1), g, t + 1), middle, inner & (third_x | last_x)),
            (made(7, q, third, slot(up, 1), g, t - 1), middle, inner & (first_x | second_x)),
            (made(8, q, raw, slot(g - other, -1), other, t + 1), cross_right & crossed, cross_left & crossed),
            (made(9, q, raw, slot(g - other, 1), other, t - 1), cross_left & crossed, cross_right & crossed),
            (made(10, q, left, slot(g - other, -1), other, t), from_left, from_left),
            (made(11, q, right, slot(g - other, 1), other, t), from_right, from_right),
            (made(12, q, win.at[slot(up, -1)], slot(up, 0), g, t - 1), inner & second_x & ~direct, inner & first_x & ~direct),
            (made(13, q, win.at[slot(up, 1)], slot(up, 0), g, t + 1), inner & third_x & ~direct, inner & last_x & ~direct),
        )

    def start(q, kinds):
        for made, sent, _ in [copies(q)[k] for k in kinds]:
            pl.when(sent)(lambda made=made: made().start())

    def arrived(q, kinds, where=True):
        for made, _, received in [copies(q)[k] for k in kinds]:
            pl.when(received & where)(lambda made=made: made().wait_recv())

    def first(q, carry):
        start(q, (3, 0, 1, 8, 9, 2))
        return carry

    lax.fori_loop(0, PARTS, first, 0)

    def clear(target):
        def one(c, carry):
            win[target, c] = jnp.zeros((ZY, X), jnp.float32)
            return carry

        lax.fori_loop(0, C, one, 0)

    for d in (0, mate - g):
        pl.when(t == 0)(lambda d=d: clear(slot(d, -1)))
        pl.when(t == TILES - 1)(lambda d=d: clear(slot(d, 1)))
    pl.when(inner & (t == 0))(lambda: clear(slot(other - g, -1)))
    pl.when(inner & (t == TILES - 1))(lambda: clear(slot(other - g, 1)))
    for load in loads:
        load.wait()
    lane = lax.broadcasted_iota(jnp.int32, (ZY // 2, HALF), 1)
    spare = TOUCH * EB + lax.rem(lax.div(lane, ACCS), SPARE)
    for half in range(2):
        for k in range(2):
            found = faces[half, pl.ds(k, ZY // 2, stride=2), :]
            index[half, :, k * HALF : (k + 1) * HALF] = jnp.where(found < 0, spare, found) * 2

    def dot(a, b):
        return jnp.dot(a, b, preferred_element_type=jnp.float32)

    def across(weights, blocks, c):
        high, low = split(jnp.concatenate([win[block, c] for block in blocks], axis=0))
        both = dot(weights[...], high)
        return both[: 4 * ZY] + both[4 * ZY :] + dot(weights[: 4 * ZY], low)

    def forward(q):
        arrived(q, (0, 1))
        start(q, (4, 5, 10, 11))
        arrived(q, (3,), second_x | third_x)
        start(q, (6, 7))

    def begin(q):
        arrived(q, (2, 4, 5))
        for j in range(PART):
            c = q * PART + j
            partial[c] = across(near, [slot(d, dt) for d in (0, mate - g) for dt in (-1, 0, 1)], c)

    rows = PART * ZY

    def edge(k, q):
        row = (k * C + q * PART) * STEP
        return row // 8 * 8 if 0 < q < PARTS else (row + 7) // 8 * 8

    def stores(q):
        made = []
        for k in range(4):
            rows = pl.ds(edge(k, q), edge(k, q + 1) - edge(k, q))
            for half in range(2):
                made.append(
                    pltpu.make_async_copy(
                        features.at[half, rows], out.at[half, rows], stored.at[q, 2 * k + half]
                    )
                )
        return made

    def leave(q):
        for part_done in range(PARTS):
            @pl.when(q == part_done)
            def _():
                for made in stores(part_done):
                    made.start()

    def add_third(q):
        arrived(q, (3,), first_x | last_x)
        arrived(q, (6, 7, 8, 9, 12, 13))
        arrived(q, (10, 11), (q < DIRECT) | first_x | last_x)
        for j in range(PART):
            c = q * PART + j
            partial[c] += across(far, [slot(other - g, dt) for dt in (-1, 0, 1)], c)

    def end(q):
        for j in range(PART):
            high, low = split(partial[q * PART + j])
            for k in range(4):
                mixed_hi[k, j * ZY : (j + 1) * ZY, :] = high[k * ZY : (k + 1) * ZY]
                mixed_lo[k, j * ZY : (j + 1) * ZY, :] = low[k * ZY : (k + 1) * ZY]
        high, low = mixed_hi[...].reshape(4 * rows, X), mixed_lo[...].reshape(4 * rows, X)

        def along(n, k):
            columns = slice(k * X, (k + 1) * X)
            return (
                dot(high[:n], along_hi[:, columns])
                + dot(low[:n], along_hi[:, columns])
                + dot(high[:n], along_lo[:, columns])
            )

        by_gauss, by_slope, by_curve = along(4 * rows, 0), along(2 * rows, 1), along(rows, 2)
        smooth, grad_y, hess_yy, grad_z = (by_gauss[k * rows : (k + 1) * rows] for k in range(4))
        grad_x, hess_xy = by_slope[:rows], by_slope[rows:]
        half_trace = (hess_yy + by_curve) * 0.5
        spread = (hess_yy - by_curve) * 0.5
        deviation = jnp.sqrt(spread * spread + hess_xy * hess_xy)
        magnitude = jnp.sqrt(grad_z * grad_z + grad_y * grad_y + grad_x * grad_x)
        for k, value in enumerate((smooth, magnitude, half_trace + deviation, half_trace - deviation)):
            for j in range(PART):
                at = pl.ds((k * C + q * PART + j) * STEP, ZY)
                features[0, at, :] = value[j * ZY : (j + 1) * ZY, :HALF]
                features[1, at, :] = value[j * ZY : (j + 1) * ZY, HALF:]
        leave(q)

    forward(0)

    def near_work(q, carry):
        pl.when(q < PARTS)(lambda: forward(q))
        begin(q - 1)
        pl.when(~inner)(lambda: end(q - 1))
        return carry

    lax.fori_loop(1, PARTS + 1, near_work, 0)

    @pl.when(inner)
    def _():
        def pass_on(q, carry):
            arrived(q, (10, 11), second_x | third_x)
            start(q, (12, 13))
            return carry

        lax.fori_loop(DIRECT, PARTS, pass_on, 0)

        def far_work(q, carry):
            add_third(q)
            end(q)
            return carry

        lax.fori_loop(0, PARTS, far_work, 0)

    def finish(q, carry):
        for made, sent, _ in copies(q):
            pl.when(sent)(lambda made=made: made().wait_send())
        return carry

    lax.fori_loop(0, PARTS, finish, 0)
    for q in range(PARTS):
        for made in stores(q):
            made.wait()


def filtered(raw, faces):
    near, far, along_hi, along_lo = tables()
    hbm = pl.BlockSpec(memory_space=pltpu.HBM)
    return pl.pallas_call(
        filter_kernel,
        out_shape=(
            jax.ShapeDtypeStruct((2, FEATURES * STEP, HALF), jnp.float32),
            jax.ShapeDtypeStruct((2, ZY // 2, X), jnp.int32),
        ),
        in_specs=[hbm] * 6,
        out_specs=(hbm, pl.BlockSpec(memory_space=pltpu.VMEM)),
        scratch_shapes=[
            pltpu.VMEM((9, C, ZY, X), jnp.float32),
            pltpu.VMEM((2, ZY, HALF), jnp.int32),
            pltpu.VMEM((C, 4 * ZY, X), jnp.float32),
            pltpu.VMEM((2, FEATURES * STEP, HALF), jnp.float32),
            pltpu.VMEM(near.shape[1:], jnp.bfloat16),
            pltpu.VMEM(far.shape[1:], jnp.bfloat16),
            pltpu.VMEM(along_hi.shape, jnp.bfloat16),
            pltpu.VMEM(along_lo.shape, jnp.bfloat16),
            pltpu.VMEM((4, PART * ZY, X), jnp.bfloat16),
            pltpu.VMEM((4, PART * ZY, X), jnp.bfloat16),
            pltpu.SemaphoreType.DMA((14, PARTS)),
            pltpu.SemaphoreType.DMA((14, PARTS)),
            pltpu.SemaphoreType.DMA((7,)),
            pltpu.SemaphoreType.DMA((PARTS, 8)),
        ],
        compiler_params=pltpu.CompilerParams(
            collective_id=0, has_side_effects=True, vmem_limit_bytes=VMEM_BYTES
        ),
    )(raw, faces, *(jnp.asarray(table) for table in (near, far, along_hi, along_lo)))


def pool_kernel(
    features_in, index_in, touched_in, owner_in, upper, lower,
    empty_upper, empty_lower, full_upper, full_lower, cleared, placed,
    features, index, touched, owner, row_a, row_b, merged, local, ahead, *rest,
):
    accs, targets = rest[:ACCS], rest[ACCS:]
    for k in range(AHEAD):
        pltpu.make_async_copy(index_in.at[k], targets[k], ahead.at[k]).start()
    loads = [
        pltpu.make_async_copy(source, target, local.at[k])
        for k, (source, target) in enumerate(
            (
                (index_in, index),
                (features_in.at[0], features.at[pl.ds(0, FEATURES * STEP)]),
                (features_in.at[1], features.at[pl.ds(FEATURES * STEP, FEATURES * STEP)]),
                (touched_in, touched),
                (owner_in, owner),
            )
        )
    ]
    for load in loads:
        load.start()

    def summed(rows):
        sub = lax.broadcasted_iota(jnp.int32, (rows, HALF), 0)
        lane = lax.broadcasted_iota(jnp.int32, (rows, HALF), 1)
        return (lax.rem(sub, 2) == 1) | (lane >= 2 * FEATURES)

    pair, tile = summed(2), summed(16)
    start = jnp.where(tile, 0.0, FAR)

    def reset(i, carry):
        for acc in accs:
            acc[pl.ds(i * 16, 16), :] = start
        return carry

    def fetch(k, row):
        return pltpu.make_async_copy(index.at[row], targets[k], ahead.at[k])

    lax.fori_loop(0, ROWS // 16, reset, 0)
    lane = lax.broadcasted_iota(jnp.int32, (PIECE, HALF), 1)
    row = lax.broadcasted_iota(jnp.int32, (PIECE, HALF), 0)
    empty = jnp.where(lane >= 2 * FEATURES, 0.0, FAR)

    def fill(b, carry):
        empty_upper[b] = empty
        empty_lower[b] = jnp.where(row < EB - PIECE, empty, 0.0)
        return carry

    lax.fori_loop(0, BLOCKS, fill, 0)
    clearings = [
        pltpu.make_async_copy(empty_upper, upper, cleared.at[0]),
        pltpu.make_async_copy(empty_lower, lower, cleared.at[1]),
    ]
    for clearing in clearings:
        clearing.start()
    ones = jnp.ones((1, HALF), jnp.float32)

    def turn(n, row):
        at = n + lax.div(n, ZY) * (FEATURES * STEP - ZY)
        values = features[pl.ds(at, FEATURES, stride=STEP), :]
        row[...] = jnp.concatenate([values, -values, values[:31], ones], axis=0).T

    def collect(target, first, row):
        for v in range(HALF):
            acc = accs[v % ACCS]
            at = pl.ds(target[first + v], 2)
            value = jnp.broadcast_to(row[v : v + 1, :], (2, HALF))
            old = acc[at, :]
            acc[at, :] = jnp.where(pair, old + value, jnp.maximum(old, value))

    loads[0].wait()
    loads[1].wait()
    turn(0, row_a)

    def body(i, carry):
        pl.when(i == ZY // (2 * AHEAD) - 1)(lambda: loads[2].wait())
        for k in range(AHEAD):
            n = i * AHEAD + k
            fetch(k, n).wait()
            turn(2 * n + 1, row_b)
            collect(targets[k], 0, row_a)
            turn(jnp.minimum(2 * n + 2, 2 * ZY - 1), row_a)
            collect(targets[k], HALF, row_b)
            pl.when(n + AHEAD < ZY)(lambda: fetch(k, n + AHEAD).start())
        return carry

    lax.fori_loop(0, ZY // AHEAD, body, 0)
    loads[3].wait()
    loads[4].wait()

    for clearing in clearings:
        clearing.wait()
    lane = lax.broadcasted_iota(jnp.int32, (EB // 4, HALF), 1)

    def place(n, carry):
        for u in range(TOGETHER):
            for k in range(2 * EB // 16):
                rows = pl.ds(pl.multiple_of((n * TOGETHER + u) * 2 * EB + k * 16, 16), 16)
                total = accs[0][rows, :]
                for acc in accs[1:]:
                    more = acc[rows, :]
                    total = jnp.where(tile, total + more, jnp.maximum(total, more))
                merged[pl.ds(u * 2 * EB + k * 16, 16), :] = total
        for u in range(TOGETHER):
            i = n * TOGETHER + u
            extremes = merged[pl.ds(u * 2 * EB, EB, stride=2), :]
            full_upper[i] = extremes[:PIECE]
            full_lower[i, : EB - PIECE, :] = extremes[PIECE:]
            sums = merged[pl.ds(u * 2 * EB + 1, EB, stride=2), :]
            packed = jnp.zeros((EB // 4, HALF), jnp.float32)
            for j in range(4):
                group = pltpu.roll(sums[j * 16 : (j + 1) * 16], (32 * j - 16) % HALF, 1)
                packed = jnp.where((lane >= 32 * j) & (lane < 32 * j + 32), group, packed)
            full_lower[i, EB - PIECE :, :] = packed
        for u in range(TOGETHER):
            i = n * TOGETHER + u
            to = owner[touched[i]]
            tile_x, tile_yz = lax.rem(to, ROW), lax.div(to, ROW)
            pltpu.make_async_copy(full_upper.at[i], upper.at[tile_x * GROUP + tile_yz], placed.at[0, i]).start()
            pltpu.make_async_copy(full_lower.at[i], lower.at[to], placed.at[1, i]).start()
        return carry

    lax.fori_loop(0, TOUCH // TOGETHER, place, 0)

    def settle(i, carry):
        pltpu.make_async_copy(full_upper.at[i], upper.at[0], placed.at[0, i]).wait()
        pltpu.make_async_copy(full_lower.at[i], lower.at[0], placed.at[1, i]).wait()
        return carry

    lax.fori_loop(0, TOUCH, settle, 0)


def pooled(features, index, touched, owner):
    hbm = pl.BlockSpec(memory_space=pltpu.HBM)
    return pl.pallas_call(
        pool_kernel,
        out_shape=[jax.ShapeDtypeStruct((BLOCKS, PIECE, HALF), jnp.float32)] * 2,
        in_specs=[hbm] * 4,
        out_specs=[hbm] * 2,
        scratch_shapes=[pltpu.VMEM((BLOCKS, PIECE, HALF), jnp.float32)] * 2
        + [pltpu.VMEM((TOUCH, PIECE, HALF), jnp.float32)] * 2
        + [pltpu.SemaphoreType.DMA((2,)), pltpu.SemaphoreType.DMA((2, TOUCH))]
        + [
            pltpu.VMEM((2 * FEATURES * STEP, HALF), jnp.float32),
            pltpu.VMEM((ZY, X), jnp.int32),
            pltpu.SMEM((TOUCH,), jnp.int32),
            pltpu.SMEM((BLOCKS,), jnp.int32),
        ]
        + [pltpu.VMEM((HALF, HALF), jnp.float32)] * 2
        + [pltpu.VMEM((TOGETHER * HALF, HALF), jnp.float32)]
        + [pltpu.SemaphoreType.DMA((5,)), pltpu.SemaphoreType.DMA((AHEAD,))]
        + [pltpu.VMEM((ROWS, HALF), jnp.float32)] * ACCS
        + [pltpu.SMEM((X,), jnp.int32)] * AHEAD,
        compiler_params=pltpu.CompilerParams(vmem_limit_bytes=VMEM_BYTES),
    )(features, index, touched, owner)


def merge_kernel(
    upper, lower, out, upper_sum, lower_sum, upper_got, lower_got, upper_last, lower_last, send, recv, local
):
    g, t = lax.axis_index("gz"), lax.axis_index("xy")
    x, yz = lax.rem(t, ROW), lax.div(t, ROW)
    z, y = lax.rem(yz, 2), lax.div(yz, 2)
    zx = lax.rem(t, GROUP)
    loads = [
        pltpu.make_async_copy(upper.at[pl.ds(x * GROUP, GROUP)], upper_sum, local.at[0]),
        pltpu.make_async_copy(lower.at[pl.ds(y * GROUP, GROUP)], lower_sum, local.at[1]),
    ]
    for load in loads:
        load.start()

    def along_x(k):
        return lax.rem(x + k, ROW)

    def along_y(k):
        return lax.rem(y + k, ROW)

    def along_yz(k):
        return lax.rem(yz + k, GROUP)

    def along_zx(k):
        return lax.rem(zx + k, GROUP)

    barrier = pltpu.get_barrier_semaphore()

    def greet(peer):
        pl.semaphore_signal(barrier, inc=1, device_id=(g, peer), device_id_type=MESH)

    for k in range(1, ROW):
        greet(yz * ROW + along_x(k))
        greet(along_y(k) * GROUP + zx)
    for k in range(ROW):
        greet(along_y(k) * GROUP + (1 - z) * ROW + x)
    for k in range(1, ROW):
        greet(y * GROUP + (1 - z) * ROW + along_x(k))
    pl.semaphore_wait(barrier, 3 * (ROW - 1) + ROW)

    def copy(source, target, at, peer):
        return pltpu.make_async_remote_copy(
            src_ref=source,
            dst_ref=target,
            send_sem=send.at[at],
            recv_sem=recv.at[at],
            device_id=(g, peer),
            device_id_type=MESH,
        )

    def first_upper(k, c):
        source = upper.at[pl.ds(along_x(k) * GROUP + c * CHUNK, CHUNK)]
        target = upper_got.at[k - 1, pl.ds(c * CHUNK, CHUNK)]
        return copy(source, target, 2 * (k - 1) + c, yz * ROW + along_x(k))

    def first_lower(k, c):
        source = lower.at[pl.ds(along_y(k) * GROUP + c * CHUNK, CHUNK)]
        target = lower_got.at[k - 1, pl.ds(c * CHUNK, CHUNK)]
        return copy(source, target, 2 * (ROW + k - 2) + c, along_y(k) * GROUP + zx)

    def last_upper(k):
        source = upper_sum.at[along_yz(k)]
        return copy(source, upper_last.at[k - 1], 4 * (ROW - 1) + k - 1, along_yz(k) * ROW + x)

    def last_lower(k):
        source = lower_sum.at[along_zx(k)]
        return copy(source, lower_last.at[k - 1], 4 * (ROW - 1) + GROUP + k - 2, y * GROUP + along_zx(k))

    lane = lax.broadcasted_iota(jnp.int32, (PIECE, HALF), 1)
    row = lax.broadcasted_iota(jnp.int32, (PIECE, HALF), 0)
    upper_adds = lane >= 2 * FEATURES
    lower_adds = upper_adds | (row >= EB - PIECE)

    def join(adds, left, right):
        return jnp.where(adds, left + right, jnp.maximum(left, right))

    order = (2, 1, 3)
    for c in range(2):
        for k in order:
            first_upper(k, c).start()
            first_lower(k, c).start()
    for load in loads:
        load.wait()

    def stage(c, adds, first, got, summed, last, mine):
        for k in order:
            first(k, c).wait_recv()

        def one(b, carry):
            total = summed[b]
            for k in range(ROW - 1):
                total = join(adds, total, got[k, b])
            summed[b] = total
            away = lax.rem(b - mine + GROUP, GROUP)
            pl.when(away != 0)(lambda: last(away).start())
            return carry

        lax.fori_loop(c * CHUNK, (c + 1) * CHUNK, one, 0)

    for c in range(2):
        stage(c, upper_adds, first_upper, upper_got, upper_sum, last_upper, yz)
        stage(c, lower_adds, first_lower, lower_got, lower_sum, last_lower, zx)

    def gather(adds, total, got, last):
        for k in range(1, GROUP):
            last(k).wait_recv()
            total = join(adds, total, got[k - 1])
        return total

    total = jnp.concatenate(
        [
            gather(upper_adds, upper_sum[yz], upper_last, last_upper),
            gather(lower_adds, lower_sum[zx], lower_last, last_lower),
        ],
        axis=0,
    )
    extremes, packed = total[:EB], total[EB:]
    rest = jnp.concatenate([pltpu.roll(packed, (HALF + 16 - 32 * j) % HALF, 1) for j in range(4)], axis=0)
    count = extremes[:, HALF - 1 :]
    present = count > 0.0
    lane = lax.broadcasted_iota(jnp.int32, (EB, HALF), 1)
    means = jnp.where(lane < 31, pltpu.roll(extremes, HALF - 2 * FEATURES, 1), rest) / jnp.maximum(count, 1.0)
    signed = jnp.where(present, jnp.where(lane < FEATURES, extremes, -extremes), 0.0)
    shifted = pltpu.roll(signed, FEATURES, 1)
    out[:, :HALF] = jnp.where(lane < FEATURES, means, shifted)
    out[:, HALF:] = shifted[:, : 3 * FEATURES - HALF]

    for k in order:
        for c in range(2):
            first_upper(k, c).wait_send()
            first_lower(k, c).wait_send()
    for k in range(1, GROUP):
        last_upper(k).wait_send()
        last_lower(k).wait_send()


def merged_stats(upper, lower):
    hbm = pl.BlockSpec(memory_space=pltpu.HBM)
    copies = 4 * (ROW - 1) + 2 * (GROUP - 1)
    return pl.pallas_call(
        merge_kernel,
        out_shape=jax.ShapeDtypeStruct((EB, 3 * FEATURES), jnp.float32),
        in_specs=[hbm] * 2,
        out_specs=pl.BlockSpec(memory_space=pltpu.VMEM),
        scratch_shapes=[pltpu.VMEM((GROUP, PIECE, HALF), jnp.float32)] * 2
        + [pltpu.VMEM((ROW - 1, GROUP, PIECE, HALF), jnp.float32)] * 2
        + [pltpu.VMEM((GROUP - 1, PIECE, HALF), jnp.float32)] * 2
        + [
            pltpu.SemaphoreType.DMA((copies,)),
            pltpu.SemaphoreType.DMA((copies,)),
            pltpu.SemaphoreType.DMA((2,)),
        ],
        compiler_params=pltpu.CompilerParams(
            collective_id=1, has_side_effects=True, vmem_limit_bytes=MERGE_BYTES
        ),
    )(upper, lower)


def per_device(raw_volume, face_slot, touched, block_owner):
    features, index = filtered(raw_volume.reshape(C, ZY, X), face_slot.reshape(ZY, X))
    upper, lower = pooled(features, index.reshape(ZY, X), touched.reshape(-1), block_owner.reshape(-1))
    return merged_stats(upper, lower).T[None, None]


def solution(mesh):
    placed = (P(None, "gz", "xy", None), P("gz", "xy", None), P("gz", "xy", None), P("gz", None))
    return jax.shard_map(
        per_device, mesh=mesh, in_specs=placed, out_specs=P("gz", "xy", None, None), check_vma=False
    )
```

```python
import functools

import jax
import jax.numpy as jnp
import ml_dtypes
import numpy as np
from jax import lax
from jax.experimental import pallas as pl
from jax.experimental.pallas import tpu as pltpu
from jax.sharding import PartitionSpec as P

RADIUS = 8
C = 12
Z = 8
Y = 8
X = 256
EB = 64
TOUCH = 16
BLOCKS = 32
TILES = 32
SLABS = 4
ZY = Z * Y
HALF = X // 2
FEATURES = 4 * C
PARTS = 6
PART = C // PARTS
DIRECT = 3
CROSSED = 2
ACCS = 8
ROW = 4
SPARE = 8
ROWS = 2 * (TOUCH * EB + SPARE)
SENT = EB + EB // 4
PIECE = SENT // 2
GROUP = 8
CHUNK = 4
FAR = -1e30
STEP = ZY + 1
AHEAD = 4
TOGETHER = 4
VMEM_BYTES = 62 * 2**20
MERGE_BYTES = 107 * 2**19
MESH = pl.DeviceIdType.MESH


def taps():
    sigma = np.float32(RADIUS / 3.0)
    offsets = np.arange(-RADIUS, RADIUS + 1).astype(np.float32)
    gauss = np.exp(-offsets * offsets / (2.0 * sigma * sigma)).astype(np.float32)
    gauss = gauss / gauss.sum()
    slope = -(offsets / sigma) * gauss
    curve = (offsets * offsets / (sigma * sigma) - 1.0) * gauss
    return [tap.astype(np.float64) for tap in (gauss, slope, curve)]


def two_terms(table):
    table = table.astype(np.float32)
    high = table.astype(ml_dtypes.bfloat16)
    low = (table - high.astype(np.float32)).astype(ml_dtypes.bfloat16)
    return high, low


def band(tap, size, start, stop):
    offset = np.arange(start, stop)[None, :] - np.arange(size)[:, None]
    return np.where(np.abs(offset) <= RADIUS, tap[np.clip(offset + RADIUS, 0, 2 * RADIUS)], 0.0)


def tables():
    gauss, slope, curve = taps()
    rows = []
    for kz, ky in ((gauss, gauss), (gauss, slope), (gauss, curve), (slope, gauss)):
        bz = band(kz, Z, -Z, 2 * Z).reshape(Z, 3, Z)
        by = band(ky, Y, -Y, 2 * Y).reshape(Y, 3, Y)
        rows.append(np.einsum("pdz,qey->pqdezy", bz, by).reshape(ZY, 9 * ZY))
    weights = np.concatenate(rows, axis=0).reshape(4 * ZY, 3, 3 * ZY)

    def both_terms(*blocks):
        return np.concatenate(two_terms(np.concatenate([weights[:, d + 1] for d in blocks], axis=1)), axis=0)

    near = np.stack([both_terms(0, 1), both_terms(0, -1)])
    far = np.stack([both_terms(-1), both_terms(1)])
    along = [two_terms(band(tap, X, 0, X).T) for tap in (gauss, slope, curve)]
    return near, far, np.concatenate([t[0] for t in along], 1), np.concatenate([t[1] for t in along], 1)


def split(values):
    high = values.astype(jnp.bfloat16)
    return high, (values - high.astype(jnp.float32)).astype(jnp.bfloat16)


def slot(dz, dt):
    return (dz + 1) * 3 + (dt + 1)


def filter_kernel(
    raw, faces_in, near_in, far_in, along_hi_in, along_lo_in, out, index,
    win, faces, partial, features, near, far, along_hi, along_lo, mixed_hi, mixed_lo, send, recv, local, stored,
):
    g, t = lax.axis_index("gz"), lax.axis_index("xy")
    odd = lax.rem(g, 2)
    mate = g + 1 - 2 * odd
    inner = (g == 1) | (g == 2)
    other = 3 - g
    has_left, has_right = t > 0, t < TILES - 1
    column = lax.rem(t, ROW)
    first_x, last_x = column == 0, column == ROW - 1
    second_x, third_x = column == 1, column == 2
    cross_left, cross_right = inner & first_x & has_left, inner & last_x & has_right

    loads = [
        pltpu.make_async_copy(source, target, local.at[k])
        for k, (source, target) in enumerate(
            (
                (raw, win.at[slot(0, 0)]),
                (faces_in.at[:, pl.ds(0, HALF)], faces.at[0, pl.ds(0, ZY)]),
                (faces_in.at[:, pl.ds(HALF, HALF)], faces.at[1, pl.ds(0, ZY)]),
                (near_in.at[odd], near),
                (far_in.at[odd], far),
                (along_hi_in, along_hi),
                (along_lo_in, along_lo),
            )
        )
    ]
    for load in loads:
        load.start()

    barrier = pltpu.get_barrier_semaphore()
    greeted = 0
    for condition, dg, dt in (
        (has_left, g, t - 1),
        (has_right, g, t + 1),
        (inner, other, t),
        (cross_left, other, t - 1),
        (cross_right, other, t + 1),
    ):
        @pl.when(condition)
        def _():
            pl.semaphore_signal(barrier, inc=1, device_id=(dg, dt), device_id_type=MESH)

        greeted += condition.astype(jnp.int32)
    pl.semaphore_signal(barrier, inc=1, device_id=(mate, t), device_id_type=MESH)
    pl.semaphore_wait(barrier, greeted + 1)

    def part(ref, q):
        return ref.at[pl.ds(q * PART, PART)]

    def copy(kind, q, source, target, dg, dt):
        return pltpu.make_async_remote_copy(
            src_ref=part(source, q),
            dst_ref=part(win.at[target], q),
            send_sem=send.at[kind, q],
            recv_sem=recv.at[kind, q],
            device_id=(dg, dt),
            device_id_type=MESH,
        )

    def copies(q):
        up = other - g

        def made(*args):
            return lambda: copy(*args)

        middle = inner & (second_x | third_x)
        direct, crossed = q < DIRECT, q < CROSSED
        from_left = inner & has_left & (second_x | (first_x & ~crossed))
        from_right = inner & has_right & (third_x | (last_x & ~crossed))
        left, right = win.at[slot(0, -1)], win.at[slot(0, 1)]
        third = win.at[slot(up, 0)]
        return (
            (made(0, q, raw, slot(0, -1), g, t + 1), has_right, has_left),
            (made(1, q, raw, slot(0, 1), g, t - 1), has_left, has_right),
            (made(2, q, raw, slot(g - mate, 0), mate, t), True, True),
            (made(3, q, raw, slot(g - other, 0), other, t), middle | (inner & direct), middle | (inner & direct)),
            (made(4, q, left, slot(g - mate, -1), mate, t), has_left, has_left),
            (made(5, q, right, slot(g - mate, 1), mate, t), has_right, has_right),
            (made(6, q, third, slot(up, -1), g, t + 1), middle, inner & (third_x | last_x)),
            (made(7, q, third, slot(up, 1), g, t - 1), middle, inner & (first_x | second_x)),
            (made(8, q, raw, slot(g - other, -1), other, t + 1), cross_right & crossed, cross_left & crossed),
            (made(9, q, raw, slot(g - other, 1), other, t - 1), cross_left & crossed, cross_right & crossed),
            (made(10, q, left, slot(g - other, -1), other, t), from_left, from_left),
            (made(11, q, right, slot(g - other, 1), other, t), from_right, from_right),
            (made(12, q, win.at[slot(up, -1)], slot(up, 0), g, t - 1), inner & second_x & ~direct, inner & first_x & ~direct),
            (made(13, q, win.at[slot(up, 1)], slot(up, 0), g, t + 1), inner & third_x & ~direct, inner & last_x & ~direct),
        )

    def start(q, kinds):
        for made, sent, _ in [copies(q)[k] for k in kinds]:
            pl.when(sent)(lambda made=made: made().start())

    def arrived(q, kinds, where=True):
        for made, _, received in [copies(q)[k] for k in kinds]:
            pl.when(received & where)(lambda made=made: made().wait_recv())

    def first(q, carry):
        start(q, (3, 0, 1, 8, 9, 2))
        return carry

    lax.fori_loop(0, PARTS, first, 0)

    def clear(target):
        def one(c, carry):
            win[target, c] = jnp.zeros((ZY, X), jnp.float32)
            return carry

        lax.fori_loop(0, C, one, 0)

    for d in (0, mate - g):
        pl.when(t == 0)(lambda d=d: clear(slot(d, -1)))
        pl.when(t == TILES - 1)(lambda d=d: clear(slot(d, 1)))
    pl.when(inner & (t == 0))(lambda: clear(slot(other - g, -1)))
    pl.when(inner & (t == TILES - 1))(lambda: clear(slot(other - g, 1)))
    for load in loads:
        load.wait()
    lane = lax.broadcasted_iota(jnp.int32, (ZY // 2, HALF), 1)
    spare = TOUCH * EB + lax.rem(lax.div(lane, ACCS), SPARE)
    for half in range(2):
        for k in range(2):
            found = faces[half, pl.ds(k, ZY // 2, stride=2), :]
            index[half, :, k * HALF : (k + 1) * HALF] = jnp.where(found < 0, spare, found) * 2

    def dot(a, b):
        return jnp.dot(a, b, preferred_element_type=jnp.float32)

    def across(weights, blocks, c):
        high, low = split(jnp.concatenate([win[block, c] for block in blocks], axis=0))
        both = dot(weights[...], high)
        return both[: 4 * ZY] + both[4 * ZY :] + dot(weights[: 4 * ZY], low)

    def forward(q):
        arrived(q, (0, 1))
        start(q, (4, 5, 10, 11))
        arrived(q, (3,), second_x | third_x)
        start(q, (6, 7))

    def begin(q):
        arrived(q, (2, 4, 5))
        for j in range(PART):
            c = q * PART + j
            partial[c] = across(near, [slot(d, dt) for d in (0, mate - g) for dt in (-1, 0, 1)], c)

    rows = PART * ZY

    def edge(k, q):
        row = (k * C + q * PART) * STEP
        return row // 8 * 8 if 0 < q < PARTS else (row + 7) // 8 * 8

    def stores(q):
        made = []
        for k in range(4):
            rows = pl.ds(edge(k, q), edge(k, q + 1) - edge(k, q))
            for half in range(2):
                made.append(
                    pltpu.make_async_copy(
                        features.at[half, rows], out.at[half, rows], stored.at[q, 2 * k + half]
                    )
                )
        return made

    def leave(q):
        for part_done in range(PARTS):
            @pl.when(q == part_done)
            def _():
                for made in stores(part_done):
                    made.start()

    def add_third(q):
        arrived(q, (3,), first_x | last_x)
        arrived(q, (6, 7, 8, 9, 12, 13))
        arrived(q, (10, 11), (q < DIRECT) | first_x | last_x)
        for j in range(PART):
            c = q * PART + j
            partial[c] += across(far, [slot(other - g, dt) for dt in (-1, 0, 1)], c)

    def end(q):
        for j in range(PART):
            high, low = split(partial[q * PART + j])
            for k in range(4):
                mixed_hi[k, j * ZY : (j + 1) * ZY, :] = high[k * ZY : (k + 1) * ZY]
                mixed_lo[k, j * ZY : (j + 1) * ZY, :] = low[k * ZY : (k + 1) * ZY]
        high, low = mixed_hi[...].reshape(4 * rows, X), mixed_lo[...].reshape(4 * rows, X)

        def along(n, k):
            columns = slice(k * X, (k + 1) * X)
            return (
                dot(high[:n], along_hi[:, columns])
                + dot(low[:n], along_hi[:, columns])
                + dot(high[:n], along_lo[:, columns])
            )

        by_gauss, by_slope, by_curve = along(4 * rows, 0), along(2 * rows, 1), along(rows, 2)
        smooth, grad_y, hess_yy, grad_z = (by_gauss[k * rows : (k + 1) * rows] for k in range(4))
        grad_x, hess_xy = by_slope[:rows], by_slope[rows:]
        half_trace = (hess_yy + by_curve) * 0.5
        spread = (hess_yy - by_curve) * 0.5
        deviation = jnp.sqrt(spread * spread + hess_xy * hess_xy)
        magnitude = jnp.sqrt(grad_z * grad_z + grad_y * grad_y + grad_x * grad_x)
        for k, value in enumerate((smooth, magnitude, half_trace + deviation, half_trace - deviation)):
            for j in range(PART):
                at = pl.ds((k * C + q * PART + j) * STEP, ZY)
                features[0, at, :] = value[j * ZY : (j + 1) * ZY, :HALF]
                features[1, at, :] = value[j * ZY : (j + 1) * ZY, HALF:]
        leave(q)

    forward(0)

    def near_work(q, carry):
        pl.when(q < PARTS)(lambda: forward(q))
        begin(q - 1)
        pl.when(~inner)(lambda: end(q - 1))
        return carry

    lax.fori_loop(1, PARTS + 1, near_work, 0)

    @pl.when(inner)
    def _():
        def pass_on(q, carry):
            arrived(q, (10, 11), second_x | third_x)
            start(q, (12, 13))
            return carry

        lax.fori_loop(DIRECT, PARTS, pass_on, 0)

        def far_work(q, carry):
            add_third(q)
            end(q)
            return carry

        lax.fori_loop(0, PARTS, far_work, 0)

    def finish(q, carry):
        for made, sent, _ in copies(q):
            pl.when(sent)(lambda made=made: made().wait_send())
        return carry

    lax.fori_loop(0, PARTS, finish, 0)
    for q in range(PARTS):
        for made in stores(q):
            made.wait()


def filtered(raw, faces):
    near, far, along_hi, along_lo = tables()
    hbm = pl.BlockSpec(memory_space=pltpu.HBM)
    return pl.pallas_call(
        filter_kernel,
        out_shape=(
            jax.ShapeDtypeStruct((2, FEATURES * STEP, HALF), jnp.float32),
            jax.ShapeDtypeStruct((2, ZY // 2, X), jnp.int32),
        ),
        in_specs=[hbm] * 6,
        out_specs=(hbm, pl.BlockSpec(memory_space=pltpu.VMEM)),
        scratch_shapes=[
            pltpu.VMEM((9, C, ZY, X), jnp.float32),
            pltpu.VMEM((2, ZY + 8, HALF), jnp.int32),
            pltpu.VMEM((C, 4 * ZY, X), jnp.float32),
            pltpu.VMEM((2, FEATURES * STEP, HALF), jnp.float32),
            pltpu.VMEM(near.shape[1:], jnp.bfloat16),
            pltpu.VMEM(far.shape[1:], jnp.bfloat16),
            pltpu.VMEM(along_hi.shape, jnp.bfloat16),
            pltpu.VMEM(along_lo.shape, jnp.bfloat16),
            pltpu.VMEM((4, PART * ZY, X), jnp.bfloat16),
            pltpu.VMEM((4, PART * ZY, X), jnp.bfloat16),
            pltpu.SemaphoreType.DMA((14, PARTS)),
            pltpu.SemaphoreType.DMA((14, PARTS)),
            pltpu.SemaphoreType.DMA((7,)),
            pltpu.SemaphoreType.DMA((PARTS, 8)),
        ],
        compiler_params=pltpu.CompilerParams(
            collective_id=0, has_side_effects=True, vmem_limit_bytes=VMEM_BYTES
        ),
    )(raw, faces, *(jnp.asarray(table) for table in (near, far, along_hi, along_lo)))


def pool_kernel(
    features_in, index_in, touched_in, owner_in, upper, lower,
    empty_upper, empty_lower, full_upper, full_lower, cleared, placed,
    features, index, touched, owner, row_a, row_b, merged, local, ahead, *rest,
):
    accs, targets = rest[:ACCS], rest[ACCS:]
    for k in range(AHEAD):
        pltpu.make_async_copy(index_in.at[k], targets[k], ahead.at[k]).start()
    loads = [
        pltpu.make_async_copy(source, target, local.at[k])
        for k, (source, target) in enumerate(
            (
                (index_in, index),
                (features_in.at[0], features.at[pl.ds(0, FEATURES * STEP)]),
                (features_in.at[1], features.at[pl.ds(FEATURES * STEP, FEATURES * STEP)]),
                (touched_in, touched),
                (owner_in, owner),
            )
        )
    ]
    for load in loads:
        load.start()

    def summed(rows):
        sub = lax.broadcasted_iota(jnp.int32, (rows, HALF), 0)
        lane = lax.broadcasted_iota(jnp.int32, (rows, HALF), 1)
        return (lax.rem(sub, 2) == 1) | (lane >= 2 * FEATURES)

    pair, tile = summed(2), summed(16)
    start = jnp.where(tile, 0.0, FAR)

    def reset(i, carry):
        for acc in accs:
            acc[pl.ds(i * 16, 16), :] = start
        return carry

    def fetch(k, row):
        return pltpu.make_async_copy(index.at[row], targets[k], ahead.at[k])

    lax.fori_loop(0, ROWS // 16, reset, 0)
    lane = lax.broadcasted_iota(jnp.int32, (PIECE, HALF), 1)
    row = lax.broadcasted_iota(jnp.int32, (PIECE, HALF), 0)
    empty = jnp.where(lane >= 2 * FEATURES, 0.0, FAR)

    def fill(b, carry):
        empty_upper[b] = empty
        empty_lower[b] = jnp.where(row < EB - PIECE, empty, 0.0)
        return carry

    lax.fori_loop(0, BLOCKS, fill, 0)
    clearings = [
        pltpu.make_async_copy(empty_upper, upper, cleared.at[0]),
        pltpu.make_async_copy(empty_lower, lower, cleared.at[1]),
    ]
    for clearing in clearings:
        clearing.start()
    ones = jnp.ones((1, HALF), jnp.float32)

    def turn(n, row):
        at = n + lax.div(n, ZY) * (FEATURES * STEP - ZY)
        values = features[pl.ds(at, FEATURES, stride=STEP), :]
        row[...] = jnp.concatenate([values, -values, values[:31], ones], axis=0).T

    def collect(target, first, row):
        for v in range(HALF):
            acc = accs[v % ACCS]
            at = pl.ds(target[first + v], 2)
            value = jnp.broadcast_to(row[v : v + 1, :], (2, HALF))
            old = acc[at, :]
            acc[at, :] = jnp.where(pair, old + value, jnp.maximum(old, value))

    loads[0].wait()
    loads[1].wait()
    turn(0, row_a)

    def body(i, carry):
        pl.when(i == ZY // (2 * AHEAD) - 1)(lambda: loads[2].wait())
        for k in range(AHEAD):
            n = i * AHEAD + k
            fetch(k, n).wait()
            turn(2 * n + 1, row_b)
            collect(targets[k], 0, row_a)
            turn(jnp.minimum(2 * n + 2, 2 * ZY - 1), row_a)
            collect(targets[k], HALF, row_b)
            pl.when(n + AHEAD < ZY)(lambda: fetch(k, n + AHEAD).start())
        return carry

    lax.fori_loop(0, ZY // AHEAD, body, 0)
    loads[3].wait()
    loads[4].wait()

    for clearing in clearings:
        clearing.wait()
    lane = lax.broadcasted_iota(jnp.int32, (EB // 4, HALF), 1)

    def place(n, carry):
        for u in range(TOGETHER):
            for k in range(2 * EB // 16):
                rows = pl.ds(pl.multiple_of((n * TOGETHER + u) * 2 * EB + k * 16, 16), 16)
                total = accs[0][rows, :]
                for acc in accs[1:]:
                    more = acc[rows, :]
                    total = jnp.where(tile, total + more, jnp.maximum(total, more))
                merged[pl.ds(u * 2 * EB + k * 16, 16), :] = total
        for u in range(TOGETHER):
            i = n * TOGETHER + u
            extremes = merged[pl.ds(u * 2 * EB, EB, stride=2), :]
            full_upper[i] = extremes[:PIECE]
            full_lower[i, : EB - PIECE, :] = extremes[PIECE:]
            sums = merged[pl.ds(u * 2 * EB + 1, EB, stride=2), :]
            packed = jnp.zeros((EB // 4, HALF), jnp.float32)
            for j in range(4):
                group = pltpu.roll(sums[j * 16 : (j + 1) * 16], (32 * j - 16) % HALF, 1)
                packed = jnp.where((lane >= 32 * j) & (lane < 32 * j + 32), group, packed)
            full_lower[i, EB - PIECE :, :] = packed
        for u in range(TOGETHER):
            i = n * TOGETHER + u
            to = owner[touched[i]]
            tile_x, tile_yz = lax.rem(to, ROW), lax.div(to, ROW)
            pltpu.make_async_copy(full_upper.at[i], upper.at[tile_x * GROUP + tile_yz], placed.at[0, i]).start()
            pltpu.make_async_copy(full_lower.at[i], lower.at[to], placed.at[1, i]).start()
        return carry

    lax.fori_loop(0, TOUCH // TOGETHER, place, 0)

    def settle(i, carry):
        pltpu.make_async_copy(full_upper.at[i], upper.at[0], placed.at[0, i]).wait()
        pltpu.make_async_copy(full_lower.at[i], lower.at[0], placed.at[1, i]).wait()
        return carry

    lax.fori_loop(0, TOUCH, settle, 0)


def pooled(features, index, touched, owner):
    hbm = pl.BlockSpec(memory_space=pltpu.HBM)
    return pl.pallas_call(
        pool_kernel,
        out_shape=[jax.ShapeDtypeStruct((BLOCKS, PIECE, HALF), jnp.float32)] * 2,
        in_specs=[hbm] * 4,
        out_specs=[hbm] * 2,
        scratch_shapes=[pltpu.VMEM((BLOCKS, PIECE, HALF), jnp.float32)] * 2
        + [pltpu.VMEM((TOUCH, PIECE, HALF), jnp.float32)] * 2
        + [pltpu.SemaphoreType.DMA((2,)), pltpu.SemaphoreType.DMA((2, TOUCH))]
        + [
            pltpu.VMEM((2 * FEATURES * STEP + ZY + 8, HALF), jnp.float32),
            pltpu.VMEM((ZY, X), jnp.int32),
            pltpu.SMEM((TOUCH,), jnp.int32),
            pltpu.SMEM((BLOCKS,), jnp.int32),
        ]
        + [pltpu.VMEM((HALF, HALF), jnp.float32)] * 2
        + [pltpu.VMEM((TOGETHER * HALF + 8, HALF), jnp.float32)]
        + [pltpu.SemaphoreType.DMA((5,)), pltpu.SemaphoreType.DMA((AHEAD,))]
        + [pltpu.VMEM((ROWS, HALF), jnp.float32)] * ACCS
        + [pltpu.SMEM((X,), jnp.int32)] * AHEAD,
        compiler_params=pltpu.CompilerParams(vmem_limit_bytes=VMEM_BYTES),
    )(features, index, touched, owner)


def merge_kernel(
    upper, lower, out, upper_sum, lower_sum, upper_got, lower_got, upper_last, lower_last, send, recv, local
):
    g, t = lax.axis_index("gz"), lax.axis_index("xy")
    x, yz = lax.rem(t, ROW), lax.div(t, ROW)
    z, y = lax.rem(yz, 2), lax.div(yz, 2)
    zx = lax.rem(t, GROUP)
    loads = [
        pltpu.make_async_copy(upper.at[pl.ds(x * GROUP, GROUP)], upper_sum, local.at[0]),
        pltpu.make_async_copy(lower.at[pl.ds(y * GROUP, GROUP)], lower_sum, local.at[1]),
    ]
    for load in loads:
        load.start()

    def along_x(k):
        return lax.rem(x + k, ROW)

    def along_y(k):
        return lax.rem(y + k, ROW)

    def along_yz(k):
        return lax.rem(yz + k, GROUP)

    def along_zx(k):
        return lax.rem(zx + k, GROUP)

    barrier = pltpu.get_barrier_semaphore()

    def greet(peer):
        pl.semaphore_signal(barrier, inc=1, device_id=(g, peer), device_id_type=MESH)

    for k in range(1, ROW):
        greet(yz * ROW + along_x(k))
        greet(along_y(k) * GROUP + zx)
    for k in range(ROW):
        greet(along_y(k) * GROUP + (1 - z) * ROW + x)
    for k in range(1, ROW):
        greet(y * GROUP + (1 - z) * ROW + along_x(k))
    pl.semaphore_wait(barrier, 3 * (ROW - 1) + ROW)

    def copy(source, target, at, peer):
        return pltpu.make_async_remote_copy(
            src_ref=source,
            dst_ref=target,
            send_sem=send.at[at],
            recv_sem=recv.at[at],
            device_id=(g, peer),
            device_id_type=MESH,
        )

    def first_upper(k, c):
        source = upper.at[pl.ds(along_x(k) * GROUP + c * CHUNK, CHUNK)]
        target = upper_got.at[k - 1, pl.ds(c * CHUNK, CHUNK)]
        return copy(source, target, 2 * (k - 1) + c, yz * ROW + along_x(k))

    def first_lower(k, c):
        source = lower.at[pl.ds(along_y(k) * GROUP + c * CHUNK, CHUNK)]
        target = lower_got.at[k - 1, pl.ds(c * CHUNK, CHUNK)]
        return copy(source, target, 2 * (ROW + k - 2) + c, along_y(k) * GROUP + zx)

    def last_upper(k):
        source = upper_sum.at[along_yz(k)]
        return copy(source, upper_last.at[k - 1], 4 * (ROW - 1) + k - 1, along_yz(k) * ROW + x)

    def last_lower(k):
        source = lower_sum.at[along_zx(k)]
        return copy(source, lower_last.at[k - 1], 4 * (ROW - 1) + GROUP + k - 2, y * GROUP + along_zx(k))

    lane = lax.broadcasted_iota(jnp.int32, (PIECE, HALF), 1)
    row = lax.broadcasted_iota(jnp.int32, (PIECE, HALF), 0)
    upper_adds = lane >= 2 * FEATURES
    lower_adds = upper_adds | (row >= EB - PIECE)

    def join(adds, left, right):
        return jnp.where(adds, left + right, jnp.maximum(left, right))

    order = (2, 1, 3)
    for c in range(2):
        for k in order:
            first_upper(k, c).start()
            first_lower(k, c).start()
    for load in loads:
        load.wait()

    def stage(c, adds, first, got, summed, last, mine):
        for k in order:
            first(k, c).wait_recv()

        def one(b, carry):
            total = summed[b]
            for k in range(ROW - 1):
                total = join(adds, total, got[k, b])
            summed[b] = total
            away = lax.rem(b - mine + GROUP, GROUP)
            pl.when(away != 0)(lambda: last(away).start())
            return carry

        lax.fori_loop(c * CHUNK, (c + 1) * CHUNK, one, 0)

    for c in range(2):
        stage(c, upper_adds, first_upper, upper_got, upper_sum, last_upper, yz)
        stage(c, lower_adds, first_lower, lower_got, lower_sum, last_lower, zx)

    def gather(adds, total, got, last):
        for k in range(1, GROUP):
            last(k).wait_recv()
            total = join(adds, total, got[k - 1])
        return total

    total = jnp.concatenate(
        [
            gather(upper_adds, upper_sum[yz], upper_last, last_upper),
            gather(lower_adds, lower_sum[zx], lower_last, last_lower),
        ],
        axis=0,
    )
    extremes, packed = total[:EB], total[EB:]
    rest = jnp.concatenate([pltpu.roll(packed, (HALF + 16 - 32 * j) % HALF, 1) for j in range(4)], axis=0)
    count = extremes[:, HALF - 1 :]
    present = count > 0.0
    lane = lax.broadcasted_iota(jnp.int32, (EB, HALF), 1)
    means = jnp.where(lane < 31, pltpu.roll(extremes, HALF - 2 * FEATURES, 1), rest) / jnp.maximum(count, 1.0)
    signed = jnp.where(present, jnp.where(lane < FEATURES, extremes, -extremes), 0.0)
    shifted = pltpu.roll(signed, FEATURES, 1)
    out[:, :HALF] = jnp.where(lane < FEATURES, means, shifted)
    out[:, HALF:] = shifted[:, : 3 * FEATURES - HALF]

    for k in order:
        for c in range(2):
            first_upper(k, c).wait_send()
            first_lower(k, c).wait_send()
    for k in range(1, GROUP):
        last_upper(k).wait_send()
        last_lower(k).wait_send()


def merged_stats(upper, lower):
    hbm = pl.BlockSpec(memory_space=pltpu.HBM)
    copies = 4 * (ROW - 1) + 2 * (GROUP - 1)
    return pl.pallas_call(
        merge_kernel,
        out_shape=jax.ShapeDtypeStruct((EB, 3 * FEATURES), jnp.float32),
        in_specs=[hbm] * 2,
        out_specs=pl.BlockSpec(memory_space=pltpu.VMEM),
        scratch_shapes=[pltpu.VMEM((GROUP, PIECE, HALF), jnp.float32)] * 2
        + [pltpu.VMEM((ROW - 1, GROUP, PIECE, HALF), jnp.float32)] * 2
        + [pltpu.VMEM((GROUP - 1, PIECE, HALF), jnp.float32)] * 2
        + [
            pltpu.SemaphoreType.DMA((copies,)),
            pltpu.SemaphoreType.DMA((copies,)),
            pltpu.SemaphoreType.DMA((2,)),
        ],
        compiler_params=pltpu.CompilerParams(
            collective_id=1, has_side_effects=True, vmem_limit_bytes=MERGE_BYTES
        ),
    )(upper, lower)


def per_device(raw_volume, face_slot, touched, block_owner):
    features, index = filtered(raw_volume.reshape(C, ZY, X), face_slot.reshape(ZY, X))
    upper, lower = pooled(features, index.reshape(ZY, X), touched.reshape(-1), block_owner.reshape(-1))
    return merged_stats(upper, lower).T[None, None]


def solution(mesh):
    placed = (P(None, "gz", "xy", None), P("gz", "xy", None), P("gz", "xy", None), P("gz", None))
    return jax.shard_map(
        per_device, mesh=mesh, in_specs=placed, out_specs=P("gz", "xy", None, None), check_vma=False
    )
```
